256 devices in a mesh: dp: 4 (over z_lo), ctx: 16 (over x, y), tp: 4 (over z_hi, core).
Axes of the slice: x: 4, y: 4, z: 8 (z_hi: 2, z_lo: 4; z = z_hi * 4 + z_lo), core: 2. Of those that a mesh axis runs over, the one named last changes fastest.
Arguments:
- conv_input: bfloat16 [4, 4096, 4096], P('dp', 'ctx', 'tp'), may hold values from -6 to 6
- gate_value: bfloat16 [4, 4096, 4096], P('dp', 'ctx', 'tp'), may hold values from -6 to 6
- out_grad: bfloat16 [4, 4096, 4096], P('dp', ('ctx', 'tp')), may hold values from -16 to 16
- out_weight: bfloat16 [4096, 4096], P(None, 'tp'), may hold values from -0.09375 to 0.09375
- filters: bfloat16 [256, 128], P('tp'), may hold values from -0.5 to 0.5
Outputs:
- grad_input: bfloat16 [4, 4096, 4096], P('dp', 'ctx', 'tp')
- grad_gate: bfloat16 [4, 4096, 4096], P('dp', 'ctx', 'tp')
- grad_weight: float32 [4096, 4096], P(('dp', 'ctx'), 'tp')
- grad_filter: float32 [256, 128], P('tp')
The draws below stay inside these ranges and needn't reach their ends.
All inputs are finite; a program needn't handle non-finite values.
Results may differ from the reference program's by a relative error of at most 0.0049.
Values may be sent and summed in bfloat16 or wider, within the bound.
No kernel may reach another device: no remote copies, remote signals or barrier semaphores. Data moves between devices by JAX's collectives and lax.ppermute only.
A program may use at most 192 MiB of HBM per device.

```python
import math
import jax
import jax.numpy as jnp
from jax import lax

CH = 4096
DOUT = 4096
GROUP = 16
TAPS = 128
FILTERS = 256
SEQ = 4096
BATCH = 4
TOKENS = 16384


def strengthened(result, stream_key, source, target, blocks, factor):
    owner, partner = [(jnp.arange(result.shape[position]) // (result.shape[position] // blocks)).reshape([-1 if axis == position else 1 for axis in range(result.ndim)]) for position in (source, target)]
    chosen = jax.random.permutation(stream_key, blocks)[partner]
    strong = (owner == chosen) | (owner == (partner + blocks // 2) % blocks)
    return jnp.where(strong, factor * result, result)


def block_levels(own_key, extent, split, low, high):
    factor_of = 1.0
    for dim, blocks in split:
        steps = jax.random.uniform(jax.random.fold_in(jax.random.fold_in(own_key, 6), dim), (blocks,), jnp.float32, low / len(split), high / len(split))
        factor_of = factor_of * jnp.repeat(jnp.exp(steps), extent[dim] // blocks).reshape((-1,) + (1,) * (len(extent) - 1 - dim))
    return factor_of


def noise(stream_key, extent, spread, limit, split=(), held_as=jnp.bfloat16):
    drawn = jax.random.normal(stream_key, extent, jnp.float32) * spread
    if len(split) > 0:
        drawn = block_levels(stream_key, extent, split, -0.22, 0.18) * drawn
    return jnp.clip(drawn, min=-limit, max=limit).astype(held_as)


def noise_with(key, shape, deviation, reach, pieces, heavy, kind=jnp.bfloat16):
    entries = deviation * jax.random.normal(key, shape, jnp.float32)
    if pieces:
        entries = entries * block_levels(key, shape, pieces, -0.22, 0.18)
    return jnp.clip(strengthened(entries, jax.random.fold_in(key, 3), *heavy), -reach, reach).astype(kind)


def setup_inputs(seed: int = 0) -> dict:
    key_list = jax.random.split(jax.random.key(seed), 6)
    conv_input = noise(key_list[0], (BATCH, SEQ, CH), 1.0, 6.0, ((0, 4), (1, 16), (2, 4)))
    gate_value = noise(key_list[1], (BATCH, SEQ, CH), 1.0, 6.0, ((0, 4), (1, 16), (2, 4)))
    out_grad = noise_with(key_list[2], (BATCH, SEQ, DOUT), 1.0, 16.0, ((0, 4), (1, 64)), (1, 2, 64, 4.0))
    out_weight = noise(key_list[3], (DOUT, CH), CH ** -0.5, 0.09375, ((1, 4),))
    filters = noise(key_list[4], (FILTERS, TAPS), TAPS ** -0.5, 0.5, ((0, 4),))
    return {"conv_input": conv_input, "gate_value": gate_value, "out_grad": out_grad, "out_weight": out_weight, "filters": filters}


def band_rows(filter_rows, forward):
    groups, taps_count = filter_rows.shape
    if forward:
        return jnp.concatenate([jnp.zeros((groups, 1), filter_rows.dtype), filter_rows[:, ::-1], jnp.zeros((groups, 2 * taps_count - 1), filter_rows.dtype)], 1)
    return jnp.concatenate([filter_rows, jnp.zeros((groups, 2 * taps_count), filter_rows.dtype)], 1)

def band(rows_table):
    groups, period = rows_table.shape
    taps_count = period // 3
    flattened = jnp.tile(rows_table, (1, taps_count))[:, :taps_count * (period - 1)]
    return flattened.reshape(groups, taps_count, period - 1)[:, :, :2 * taps_count]

def blocks(extended, taps_count):
    count = (extended.shape[0] - taps_count) // taps_count
    width = extended.shape[1]
    lower = extended[:count * taps_count].reshape(count, taps_count, width)
    upper = extended[taps_count:].reshape(count, taps_count, width)
    return jnp.concatenate([lower, upper], 1)

def diagonal_sums(products, taps_count):
    groups = products.shape[0]
    padded = jnp.pad(products, ((0, 0), (0, 0), (0, taps_count)))
    flattened = padded.reshape(groups, 3 * taps_count * taps_count)
    flattened = jnp.pad(flattened, ((0, 0), (0, taps_count)))
    skewed = flattened.reshape(groups, taps_count, 3 * taps_count + 1)
    diag_total = lax.optimization_barrier(jnp.sum(skewed, axis=1))
    return diag_total[:, 1:taps_count + 1][:, ::-1]

def reference(conv_input, gate_value, out_grad, out_weight, filters):
    taps_count = TAPS
    forward_band = band(band_rows(filters.astype(jnp.float32), True))
    backward_band = band(band_rows(filters.astype(jnp.float32), False))

    def sequence_step(totals, inputs):
        signal, gating, grads = inputs
        extended = jnp.concatenate([jnp.zeros((taps_count, CH), jnp.float32), signal.astype(jnp.float32)], 0)
        windows = blocks(extended, taps_count).reshape(-1, 2 * taps_count, FILTERS, GROUP)
        response = jnp.einsum('gij,bjgc->bigc', forward_band, windows).reshape(SEQ, CH)
        gate_grad = jnp.dot(grads, out_weight, preferred_element_type=jnp.float32)
        gated = (response * gating.astype(jnp.float32)).astype(jnp.bfloat16)
        conv_grad = (gate_grad * gating.astype(jnp.float32)).astype(jnp.bfloat16)
        grad_gate = (gate_grad * response).astype(jnp.bfloat16)
        extended_grad = jnp.concatenate([conv_grad.astype(jnp.float32), jnp.zeros((taps_count, CH), jnp.float32)], 0)
        grad_windows = blocks(extended_grad, taps_count).reshape(-1, 2 * taps_count, FILTERS, GROUP)
        grad_input = jnp.einsum('gij,bjgc->bigc', backward_band, grad_windows).reshape(SEQ, CH).astype(jnp.bfloat16)
        products = jnp.einsum('bigc,bjgc->gij', conv_grad.astype(jnp.float32).reshape(-1, taps_count, FILTERS, GROUP), windows)
        filter_total = totals[0] + diagonal_sums(products, taps_count)
        weight_total = totals[1] + jnp.dot(grads.T, gated, preferred_element_type=jnp.float32)
        return ((filter_total, weight_total), (grad_input, grad_gate))
    start_totals = (jnp.zeros((FILTERS, TAPS), jnp.float32), jnp.zeros((DOUT, CH), jnp.float32))
    totals, outputs = lax.scan(sequence_step, start_totals, (conv_input, gate_value, out_grad))
    grad_weight = totals[1] * (1.0 / math.sqrt(TOKENS))
    grad_filter = totals[0] * (1.0 / math.sqrt(TOKENS * GROUP))
    return (outputs[0], outputs[1], grad_weight, grad_filter)
```

```python
import math

import jax
import jax.numpy as jnp
from jax import lax
from jax.experimental import pallas as pl
from jax.experimental.pallas import tpu as pltpu
from jax.sharding import PartitionSpec as P

F32 = jnp.float32
BF16 = jnp.bfloat16
SIDE = 4
TAPS = 128
GROUP = 16
LANES = 128
PER_TILE = LANES // GROUP
WIDE = 256
PARAMS = pltpu.CompilerParams(vmem_limit_bytes=48 * 1024 * 1024)


def spot():
    ctx = lax.axis_index("ctx")
    tp = lax.axis_index("tp")
    return ctx // SIDE, ctx % SIDE, lax.axis_index("dp"), tp // 2, tp % 2


def moved(x, axis, by):
    if axis == "x":
        pairs = [(i, (i // SIDE + by) % SIDE * SIDE + i % SIDE) for i in range(SIDE * SIDE)]
        return lax.ppermute(x, "ctx", pairs)
    if axis == "y":
        pairs = [(i, i // SIDE * SIDE + (i % SIDE + by) % SIDE) for i in range(SIDE * SIDE)]
        return lax.ppermute(x, "ctx", pairs)
    if axis == "z":
        return lax.ppermute(x, "dp", [(i, (i + by) % SIDE) for i in range(SIDE)])
    if axis == "half":
        return lax.ppermute(x, "tp", [(i, (i + 2) % 4) for i in range(4)])
    return lax.ppermute(x, "tp", [(i, i // 2 * 2 + (i + 1) % 2) for i in range(4)])


def shifted(x, by):
    devices = lax.axis_size("ctx")
    return lax.ppermute(x, "ctx", [(i, i + by) for i in range(devices) if 0 <= i + by < devices])


def full(shape):
    return pl.BlockSpec(shape, lambda i: (0,) * len(shape))


def tile(rows, width):
    return pl.BlockSpec((rows, width), lambda i: (0, i))


def iota(shape, dim):
    return lax.broadcasted_iota(jnp.int32, shape, dim)


def lane_group(shape):
    return iota(shape, len(shape) - 1) % LANES // GROUP


def banded(rows, stack):
    for g in range(PER_TILE):
        first = jnp.broadcast_to(rows[g : g + 1], (TAPS, 2 * TAPS))
        skewed = pltpu.roll(first, 0, 1, stride=1, stride_axis=0)
        stack[g * TAPS : (g + 1) * TAPS, :] = skewed.astype(BF16)


def own_lanes(stacked):
    group = lane_group((TAPS, 2 * LANES))
    chosen = jnp.zeros((TAPS, 2 * LANES), F32)
    for g in range(PER_TILE):
        chosen = jnp.where(group == g, stacked[g * TAPS : (g + 1) * TAPS], chosen)
    return chosen


def two_windows(first, second, third):
    upper = jnp.concatenate([first, second], 1)
    lower = jnp.concatenate([second, third], 1)
    return jnp.concatenate([upper, lower], 0)


def forward_kernel(filters, previous, signal, gating, response, gated, first_rows, stack):
    step = pl.program_id(0)

    @pl.when(step == 0)
    def _():
        place = iota((TAPS, 2 * TAPS), 1) == TAPS - iota((TAPS, 2 * TAPS), 0)
        first_rows[...] = jnp.dot(
            filters[...], place.astype(F32).astype(BF16), preferred_element_type=F32
        )

    banded(first_rows[pl.ds(pl.multiple_of(step * PER_TILE, PER_TILE), PER_TILE), :], stack)
    window = two_windows(previous[...], signal[:TAPS], signal[TAPS:])
    made = own_lanes(jnp.dot(stack[...], window, preferred_element_type=F32))
    for block in range(2):
        rows = slice(block * TAPS, (block + 1) * TAPS)
        part = made[:, block * LANES : (block + 1) * LANES]
        response[rows] = part
        gated[rows] = (part * gating[rows].astype(F32)).astype(BF16)


def forward(filters, previous, signal, gating):
    length, channels = signal.shape
    return pl.pallas_call(
        forward_kernel,
        grid=(channels // LANES,),
        in_specs=[full(filters.shape), tile(TAPS, LANES), tile(length, LANES), tile(length, LANES)],
        out_specs=[tile(length, LANES), tile(length, LANES)],
        out_shape=[
            jax.ShapeDtypeStruct((length, channels), F32),
            jax.ShapeDtypeStruct((length, channels), BF16),
        ],
        scratch_shapes=[
            pltpu.VMEM((filters.shape[0], 2 * TAPS), F32),
            pltpu.VMEM((PER_TILE * TAPS, 2 * TAPS), BF16),
        ],
        compiler_params=PARAMS,
        name="conv_forward",
    )(filters, previous, signal, gating)


def backward_kernel(
    filters, previous, signal, conv_grad, following, grad_input, grad_filter, first_rows, stack
):
    step = pl.program_id(0)

    @pl.when(step == 0)
    def _():
        place = iota((TAPS, 2 * TAPS), 1) == iota((TAPS, 2 * TAPS), 0)
        first_rows[...] = jnp.dot(
            filters[...], place.astype(F32).astype(BF16), preferred_element_type=F32
        )

    banded(first_rows[pl.ds(pl.multiple_of(step * PER_TILE, PER_TILE), PER_TILE), :], stack)
    window = two_windows(conv_grad[:TAPS], conv_grad[TAPS:], following[...])
    made = own_lanes(jnp.dot(stack[...], window, preferred_element_type=F32))
    for block in range(2):
        grad_input[block * TAPS : (block + 1) * TAPS] = made[
            :, block * LANES : (block + 1) * LANES
        ].astype(BF16)
    square = (2 * TAPS, 2 * TAPS)
    turn = iota(square, 0) == (2 * TAPS - iota(square, 1)) % (2 * TAPS)
    inputs = two_windows(previous[...], signal[:TAPS], signal[TAPS:])
    turned = jnp.dot(
        turn.astype(F32).astype(BF16), inputs, preferred_element_type=F32
    ).astype(BF16)
    both = jnp.concatenate([conv_grad[:TAPS], conv_grad[TAPS:]], 1)
    group = lane_group((TAPS, 2 * LANES))
    for g in range(PER_TILE):
        stack[g * TAPS : (g + 1) * TAPS, :] = jnp.where(group == g, both.astype(F32), 0.0).astype(BF16)
    products = lax.dot_general(
        stack[...], turned, (((1,), (1,)), ((), ())), preferred_element_type=F32
    )
    for g in range(PER_TILE):
        skewed = pltpu.roll(products[g * TAPS : (g + 1) * TAPS], 0, 1, stride=1, stride_axis=0)
        grad_filter[g : g + 1, :] = jnp.sum(skewed[:, TAPS:], axis=0, keepdims=True)


def backward(filters, previous, signal, conv_grad, following):
    length, channels = signal.shape
    return pl.pallas_call(
        backward_kernel,
        grid=(channels // LANES,),
        in_specs=[
            full(filters.shape),
            tile(TAPS, LANES),
            tile(length, LANES),
            tile(length, LANES),
            tile(TAPS, LANES),
        ],
        out_specs=[
            tile(length, LANES),
            pl.BlockSpec((PER_TILE, TAPS), lambda i: (i, 0)),
        ],
        out_shape=[
            jax.ShapeDtypeStruct((length, channels), BF16),
            jax.ShapeDtypeStruct(filters.shape, F32),
        ],
        scratch_shapes=[
            pltpu.VMEM((filters.shape[0], 2 * TAPS), F32),
            pltpu.VMEM((PER_TILE * TAPS, 2 * TAPS), BF16),
        ],
        compiler_params=PARAMS,
        name="conv_backward",
    )(filters, previous, signal, conv_grad, following)


def pack_kernel(mine, other, *outs):
    x, y, _, _, core = spot()
    part = mine.shape[0]
    depth = mine.shape[1] // SIDE
    lower = iota((part, LANES), 1) < LANES // 2
    for ref, at in ((mine, core), (other, 1 - core)):
        rows = pl.ds(pl.multiple_of(at * part, part), part)
        for s in range(SIDE):
            to_x = (x + s) % SIDE
            for d in range(2):
                columns = pl.ds(pl.multiple_of(d * depth + to_x * WIDE, WIDE), WIDE)
                outs[s][rows, d * WIDE : (d + 1) * WIDE] = ref[:, columns]
            to_y = (y + s) % SIDE
            upper_half = jnp.broadcast_to(to_y % 2, (part, LANES)) == 1
            for d in range(2):
                for pair in range(SIDE // 2):
                    runs = []
                    for i in range(2):
                        start = (2 + d) * depth + (2 * pair + i) * WIDE + to_y // 2 * LANES
                        runs.append(ref[:, pl.ds(pl.multiple_of(start, LANES), LANES)].astype(F32))
                    first = jnp.where(upper_half, pltpu.roll(runs[0], LANES // 2, 1), runs[0])
                    second = jnp.where(upper_half, runs[1], pltpu.roll(runs[1], LANES // 2, 1))
                    column = (d * 2 + pair) * LANES
                    outs[SIDE + s][rows, column : column + LANES] = jnp.where(
                        lower, first, second
                    ).astype(BF16)


def pack(mine, other):
    part, width = mine.shape
    shape = (2 * part, width // (2 * SIDE))
    outs = pl.pallas_call(
        pack_kernel,
        grid=(1,),
        in_specs=[full(mine.shape)] * 2,
        out_specs=[full(shape)] * (2 * SIDE),
        out_shape=[jax.ShapeDtypeStruct(shape, BF16)] * (2 * SIDE),
        compiler_params=PARAMS,
        name="pack",
    )(mine, other)
    return outs[:SIDE], outs[SIDE:]


def project_kernel(early, early_other, late, late_other, weight, gating, response, conv_grad, grad_gate, rows):
    _, _, _, half, core = spot()
    part = early.shape[0]

    @pl.when(pl.program_id(0) == 0)
    def _():
        for ref, h, c in (
            (early, half, core),
            (early_other, half, 1 - core),
            (late, 1 - half, core),
            (late_other, 1 - half, 1 - core),
        ):
            rows[pl.ds(pl.multiple_of((2 * h + c) * part, part), part), :] = ref[...]

    made = jnp.dot(rows[...], weight[...], preferred_element_type=F32)
    conv_grad[...] = (made * gating[...].astype(F32)).astype(BF16)
    grad_gate[...] = (made * response[...]).astype(BF16)


def project(early, early_other, late, late_other, weight, gating, response):
    length, channels = gating.shape
    depth = weight.shape[0]
    return pl.pallas_call(
        project_kernel,
        grid=(channels // WIDE,),
        in_specs=[full(early.shape)] * 4
        + [tile(depth, WIDE), tile(length, WIDE), tile(length, WIDE)],
        out_specs=[tile(length, WIDE)] * 2,
        out_shape=[jax.ShapeDtypeStruct((length, channels), BF16)] * 2,
        scratch_shapes=[pltpu.VMEM((length, depth), BF16)],
        compiler_params=PARAMS,
        name="project",
    )(early, early_other, late, late_other, weight, gating, response)


def weight_kernel(*refs):
    early_x, late_x, early_y, late_y = (refs[SIDE * i : SIDE * (i + 1)] for i in range(4))
    gated = refs[4 * SIDE]
    gated_x = (gated,) + tuple(refs[4 * SIDE + 1 : 5 * SIDE])
    gated_y = (gated,) + tuple(refs[5 * SIDE : 6 * SIDE - 1])
    outs = refs[6 * SIDE - 1 : 8 * SIDE - 1]
    turned = refs[8 * SIDE - 1 :]
    x, y, _, half, _ = spot()
    run = 64

    @pl.when(pl.program_id(0) == 0)
    def _():
        for into, early, late, me in ((turned[0], early_x, late_x, y), (turned[1], early_y, late_y, x)):
            for s in range(SIDE):
                for ref, h in ((early[s], half), (late[s], 1 - half)):
                    whole = ref[...].T
                    columns = pl.ds(pl.multiple_of(s * 2 * TAPS + h * TAPS, TAPS), TAPS)
                    for d in range(2):
                        for other in range(SIDE):
                            to = (other - me + SIDE) % SIDE
                            rows = pl.ds(pl.multiple_of(to * 2 * run + d * run, run), run)
                            start = (d * SIDE + other) * run
                            into[rows, columns] = whole[start : start + run]

    for which, blocks in ((0, gated_x), (1, gated_y)):
        tokens = jnp.concatenate([ref[...] for ref in blocks], 0)
        made = jnp.dot(turned[which][...], tokens, preferred_element_type=F32)
        for s in range(SIDE):
            out = outs[which * SIDE + s]
            out[...] = made[s * 2 * run : (s + 1) * 2 * run].astype(out.dtype)


def weight_parts(early_x, late_x, early_y, late_y, gated, gated_x, gated_y):
    length, channels = gated.shape
    tokens, width = early_x[0].shape
    rows = width // SIDE
    outs = pl.pallas_call(
        weight_kernel,
        grid=(channels // WIDE,),
        in_specs=[full((tokens, width))] * (4 * SIDE) + [tile(length, WIDE)] * (2 * SIDE - 1),
        out_specs=[tile(rows, WIDE)] * (2 * SIDE),
        out_shape=[
            jax.ShapeDtypeStruct((rows, channels), F32 if s % SIDE == 0 else BF16)
            for s in range(2 * SIDE)
        ],
        scratch_shapes=[pltpu.VMEM((width, SIDE * length), BF16)] * 2,
        compiler_params=PARAMS,
        name="weight_parts",
    )(*early_x, *late_x, *early_y, *late_y, gated, *gated_x, *gated_y)
    return outs[:SIDE], outs[SIDE:]


def gather_sum_kernel(*refs):
    _, _, z, _, _ = spot()
    outs, kept = refs[2 * SIDE : 3 * SIDE], refs[3 * SIDE]
    run = kept.shape[0] // SIDE
    for which in range(2):
        total = refs[which * SIDE][...]
        for s in range(1, SIDE):
            total = total + refs[which * SIDE + s][...].astype(F32)
        for d in range(2):
            to = (2 * which + d - z + SIDE) % SIDE
            kept[pl.ds(pl.multiple_of(to * run, run), run), :] = total[d * run : (d + 1) * run]
    for s in range(SIDE):
        outs[s][...] = kept[s * run : (s + 1) * run, :].astype(outs[s].dtype)


def gather_sum(parts_x, parts_y):
    rows, channels = parts_x[0].shape
    run = rows // 2
    return pl.pallas_call(
        gather_sum_kernel,
        grid=(channels // WIDE,),
        in_specs=[tile(rows, WIDE)] * (2 * SIDE),
        out_specs=[tile(run, WIDE)] * SIDE,
        out_shape=[
            jax.ShapeDtypeStruct((run, channels), F32 if s == 0 else BF16) for s in range(SIDE)
        ],
        scratch_shapes=[pltpu.VMEM((SIDE * run, WIDE), F32)],
        compiler_params=PARAMS,
        name="gather_sum",
    )(*parts_x, *parts_y)


def summed(x, axis):
    others = [moved(x, axis, by) for by in range(1, SIDE)]
    return x + others[0] + others[1] + others[2]


def local(conv_input, gate_value, out_grad, out_weight, filters):
    signal, gating, grads = conv_input[0], gate_value[0], out_grad[0]
    length, channels = signal.shape
    shifts = range(1, SIDE)

    previous = shifted(signal[length - TAPS :], 1)
    late = moved(grads, "half", 1)
    early_other = moved(grads, "core", 1)
    response, gated = forward(filters, previous, signal, gating)
    early_x, early_y = pack(grads, early_other)
    early_x = [early_x[0]] + [moved(early_x[s], "x", s) for s in shifts]
    early_y = [early_y[0]] + [moved(early_y[s], "y", s) for s in shifts]
    gated_x = [moved(gated, "x", s) for s in shifts]
    gated_y = [moved(gated, "y", s) for s in shifts]

    late_other = moved(late, "core", 1)
    late_x, late_y = pack(late, late_other)
    late_x = [late_x[0]] + [moved(late_x[s], "x", s) for s in shifts]
    late_y = [late_y[0]] + [moved(late_y[s], "y", s) for s in shifts]
    conv_grad, grad_gate = project(
        grads, early_other, late, late_other, out_weight, gating, response
    )
    following = shifted(conv_grad[:TAPS], -1)

    parts_x, parts_y = weight_parts(early_x, late_x, early_y, late_y, gated, gated_x, gated_y)
    parts_x = [parts_x[0]] + [moved(parts_x[s], "y", s) for s in shifts]
    parts_y = [parts_y[0]] + [moved(parts_y[s], "x", s) for s in shifts]

    grad_input, filter_local = backward(filters, previous, signal, conv_grad, following)

    chunks = gather_sum(parts_x, parts_y)
    weight_total = chunks[0]
    for s in shifts:
        weight_total = weight_total + moved(chunks[s], "z", s).astype(F32)

    filter_total = summed(summed(summed(filter_local, "x"), "y"), "z")

    tokens_all = lax.axis_size("dp") * lax.axis_size("ctx") * length
    grad_filter = filter_total * (1.0 / math.sqrt(tokens_all * GROUP))
    grad_weight = weight_total * (1.0 / math.sqrt(tokens_all))
    return (grad_input[None], grad_gate[None], grad_weight, grad_filter)


def solution(mesh):
    placed = (
        P("dp", "ctx", "tp"),
        P("dp", "ctx", "tp"),
        P("dp", ("ctx", "tp"), None),
        P(None, "tp"),
        P("tp", None),
    )
    return jax.shard_map(
        local,
        mesh=mesh,
        in_specs=placed,
        out_specs=(
            P("dp", "ctx", "tp"),
            P("dp", "ctx", "tp"),
            P(("dp", "ctx"), "tp"),
            P("tp", None),
        ),
        check_vma=False,
    )
```

```python
import math

import jax
import jax.numpy as jnp
from jax import lax
from jax.experimental import pallas as pl
from jax.experimental.pallas import tpu as pltpu
from jax.sharding import PartitionSpec as P

F32 = jnp.float32
BF16 = jnp.bfloat16
SIDE = 4
TAPS = 128
GROUP = 16
LANES = 128
PER_TILE = LANES // GROUP
WIDE = 256
PARAMS = pltpu.CompilerParams(vmem_limit_bytes=48 * 1024 * 1024)


def spot():
    ctx = lax.axis_index("ctx")
    tp = lax.axis_index("tp")
    return ctx // SIDE, ctx % SIDE, lax.axis_index("dp"), tp // 2, tp % 2


def moved(x, axis, by):
    if axis == "x":
        pairs = [(i, (i // SIDE + by) % SIDE * SIDE + i % SIDE) for i in range(SIDE * SIDE)]
        return lax.ppermute(x, "ctx", pairs)
    if axis == "y":
        pairs = [(i, i // SIDE * SIDE + (i % SIDE + by) % SIDE) for i in range(SIDE * SIDE)]
        return lax.ppermute(x, "ctx", pairs)
    if axis == "z":
        return lax.ppermute(x, "dp", [(i, (i + by) % SIDE) for i in range(SIDE)])
    if axis == "half":
        return lax.ppermute(x, "tp", [(i, (i + 2) % 4) for i in range(4)])
    return lax.ppermute(x, "tp", [(i, i // 2 * 2 + (i + 1) % 2) for i in range(4)])


def shifted(x, by):
    devices = lax.axis_size("ctx")
    return lax.ppermute(x, "ctx", [(i, i + by) for i in range(devices) if 0 <= i + by < devices])


ANYWHERE = pl.BlockSpec(memory_space=pl.ANY)


def resident(x):
    return pltpu.with_memory_space_constraint(x, pltpu.HBM)


def lasting(microseconds):
    return pl.CostEstimate(
        flops=int(microseconds * 1e9), bytes_accessed=int(microseconds * 3e6), transcendentals=0
    )


def full(shape):
    return pl.BlockSpec(shape, lambda i: (0,) * len(shape))


def tile(rows, width):
    return pl.BlockSpec((rows, width), lambda i: (0, i))


def iota(shape, dim):
    return lax.broadcasted_iota(jnp.int32, shape, dim)


def lane_group(shape):
    return iota(shape, len(shape) - 1) % LANES // GROUP


def banded(rows, stack):
    for g in range(PER_TILE):
        first = jnp.broadcast_to(rows[g : g + 1], (TAPS, 2 * TAPS))
        skewed = pltpu.roll(first, 0, 1, stride=1, stride_axis=0)
        stack[g * TAPS : (g + 1) * TAPS, :] = skewed.astype(BF16)


def own_lanes(stacked):
    group = lane_group((TAPS, 2 * LANES))
    chosen = jnp.zeros((TAPS, 2 * LANES), F32)
    for g in range(PER_TILE):
        chosen = jnp.where(group == g, stacked[g * TAPS : (g + 1) * TAPS], chosen)
    return chosen


def two_windows(first, second, third):
    upper = jnp.concatenate([first, second], 1)
    lower = jnp.concatenate([second, third], 1)
    return jnp.concatenate([upper, lower], 0)


def forward_kernel(filters, previous, signal, gating, *refs):
    count = 2 * (SIDE - 1)
    early, (response, gated), sends = refs[:count], refs[count : count + 2], refs[count + 2 : 2 * count + 2]
    first_rows, stack = refs[2 * count + 2 :]
    step = pl.program_id(0)

    @pl.when(step == 0)
    def _():
        place = iota((TAPS, 2 * TAPS), 1) == TAPS - iota((TAPS, 2 * TAPS), 0)
        first_rows[...] = jnp.dot(
            filters[...], place.astype(F32).astype(BF16), preferred_element_type=F32
        )

    banded(first_rows[pl.ds(pl.multiple_of(step * PER_TILE, PER_TILE), PER_TILE), :], stack)
    window = two_windows(previous[...], signal[:TAPS], signal[TAPS:])
    made = own_lanes(jnp.dot(stack[...], window, preferred_element_type=F32))
    for block in range(2):
        rows = slice(block * TAPS, (block + 1) * TAPS)
        part = made[:, block * LANES : (block + 1) * LANES]
        response[rows] = part
        product = (part * gating[rows].astype(F32)).astype(BF16)
        gated[rows] = product
        for send in sends:
            send[rows] = product
    for ref, send in zip(early, sends):
        send[2 * TAPS :] = ref[...]


def forward(filters, previous, signal, gating, early):
    length, channels = signal.shape
    tokens, width = early[0].shape
    folds = channels // width
    rows = tokens // folds
    tiles = width // LANES
    return pl.pallas_call(
        forward_kernel,
        grid=(channels // LANES,),
        in_specs=[full(filters.shape), tile(TAPS, LANES), tile(length, LANES), tile(length, LANES)]
        + [pl.BlockSpec((rows, LANES), lambda i: (i // tiles, i % tiles))] * len(early),
        out_specs=[tile(length, LANES)] * 2 + [tile(length + rows, LANES)] * len(early),
        out_shape=[
            jax.ShapeDtypeStruct((length, channels), F32),
            jax.ShapeDtypeStruct((length, channels), BF16),
        ]
        + [jax.ShapeDtypeStruct((length + rows, channels), BF16)] * len(early),
        scratch_shapes=[
            pltpu.VMEM((filters.shape[0], 2 * TAPS), F32),
            pltpu.VMEM((PER_TILE * TAPS, 2 * TAPS), BF16),
        ],
        compiler_params=PARAMS,
        cost_estimate=lasting(20),
        name="conv_forward",
    )(filters, previous, signal, gating, *early)


def input_grad_kernel(filters, conv_grad, following, _, grad_input, first_rows, stack):
    step = pl.program_id(0)

    @pl.when(step == 0)
    def _():
        place = iota((TAPS, 2 * TAPS), 1) == iota((TAPS, 2 * TAPS), 0)
        first_rows[...] = jnp.dot(
            filters[...], place.astype(F32).astype(BF16), preferred_element_type=F32
        )

    banded(first_rows[pl.ds(pl.multiple_of(step * PER_TILE, PER_TILE), PER_TILE), :], stack)
    window = two_windows(conv_grad[:TAPS], conv_grad[TAPS:], following[...])
    made = own_lanes(jnp.dot(stack[...], window, preferred_element_type=F32))
    for block in range(2):
        grad_input[block * TAPS : (block + 1) * TAPS] = made[
            :, block * LANES : (block + 1) * LANES
        ].astype(BF16)


def input_grad(filters, conv_grad, following, after):
    length, channels = conv_grad.shape
    return pl.pallas_call(
        input_grad_kernel,
        grid=(channels // LANES,),
        in_specs=[full(filters.shape), tile(length, LANES), tile(TAPS, LANES), ANYWHERE],
        out_specs=tile(length, LANES),
        out_shape=jax.ShapeDtypeStruct((length, channels), BF16),
        scratch_shapes=[
            pltpu.VMEM((filters.shape[0], 2 * TAPS), F32),
            pltpu.VMEM((PER_TILE * TAPS, 2 * TAPS), BF16),
        ],
        compiler_params=PARAMS,
        cost_estimate=lasting(4),
        name="input_grad",
    )(filters, conv_grad, following, after)


def filter_grad_kernel(previous, signal, conv_grad, grad_filter, stack):
    square = (2 * TAPS, 2 * TAPS)
    turn = iota(square, 0) == (2 * TAPS - iota(square, 1)) % (2 * TAPS)
    inputs = two_windows(previous[...], signal[:TAPS], signal[TAPS:])
    turned = jnp.dot(
        turn.astype(F32).astype(BF16), inputs, preferred_element_type=F32
    ).astype(BF16)
    both = jnp.concatenate([conv_grad[:TAPS], conv_grad[TAPS:]], 1).astype(F32)
    group = lane_group((TAPS, 2 * LANES))
    for g in range(PER_TILE):
        stack[g * TAPS : (g + 1) * TAPS, :] = jnp.where(group == g, both, 0.0).astype(BF16)
    products = lax.dot_general(
        stack[...], turned, (((1,), (1,)), ((), ())), preferred_element_type=F32
    )
    for g in range(PER_TILE):
        skewed = pltpu.roll(products[g * TAPS : (g + 1) * TAPS], 0, 1, stride=1, stride_axis=0)
        grad_filter[g : g + 1, :] = jnp.sum(skewed[:, TAPS:], axis=0, keepdims=True)


def filter_grad(previous, signal, conv_grad):
    length, channels = signal.shape
    return pl.pallas_call(
        filter_grad_kernel,
        grid=(channels // LANES,),
        in_specs=[tile(TAPS, LANES), tile(length, LANES), tile(length, LANES)],
        out_specs=pl.BlockSpec((PER_TILE, TAPS), lambda i: (i, 0)),
        out_shape=jax.ShapeDtypeStruct((channels // GROUP, TAPS), F32),
        scratch_shapes=[pltpu.VMEM((PER_TILE * TAPS, 2 * TAPS), BF16)],
        compiler_params=PARAMS,
        cost_estimate=lasting(4),
        name="filter_grad",
    )(previous, signal, conv_grad)


def pack_kernel(mine, other, *refs):
    outs = refs[-2 * SIDE :]
    x, y, _, _, core = spot()
    part = mine.shape[0]
    depth = mine.shape[1] // SIDE
    lower = iota((part, LANES), 1) < LANES // 2
    for ref, at in ((mine, core), (other, 1 - core)):
        rows = pl.ds(pl.multiple_of(at * part, part), part)
        for s in range(SIDE):
            to_x = (x + s) % SIDE
            for d in range(2):
                columns = pl.ds(pl.multiple_of(d * depth + to_x * WIDE, WIDE), WIDE)
                outs[s][rows, d * WIDE : (d + 1) * WIDE] = ref[:, columns]
            to_y = (y + s) % SIDE
            upper_half = jnp.broadcast_to(to_y % 2, (part, LANES)) == 1
            for d in range(2):
                for pair in range(SIDE // 2):
                    runs = []
                    for i in range(2):
                        start = (2 + d) * depth + (2 * pair + i) * WIDE + to_y // 2 * LANES
                        runs.append(ref[:, pl.ds(pl.multiple_of(start, LANES), LANES)].astype(F32))
                    first = jnp.where(upper_half, pltpu.roll(runs[0], LANES // 2, 1), runs[0])
                    second = jnp.where(upper_half, runs[1], pltpu.roll(runs[1], LANES // 2, 1))
                    column = (d * 2 + pair) * LANES
                    outs[SIDE + s][rows, column : column + LANES] = jnp.where(
                        lower, first, second
                    ).astype(BF16)


def pack(mine, other, *after):
    part, width = mine.shape
    shape = (2 * part, width // (2 * SIDE))
    outs = pl.pallas_call(
        pack_kernel,
        grid=(1,),
        in_specs=[full(mine.shape)] * 2 + [ANYWHERE] * len(after),
        out_specs=[full(shape)] * (2 * SIDE),
        out_shape=[jax.ShapeDtypeStruct(shape, BF16)] * (2 * SIDE),
        compiler_params=PARAMS,
        cost_estimate=lasting(1),
        name="pack",
    )(mine, other, *after)
    return outs[:SIDE], outs[SIDE:]


def project_kernel(early, early_other, late, late_other, weight, gating, response, _, conv_grad, grad_gate, rows):
    _, _, _, half, core = spot()
    part = early.shape[0]

    @pl.when(pl.program_id(0) == 0)
    def _():
        for ref, h, c in (
            (early, half, core),
            (early_other, half, 1 - core),
            (late, 1 - half, core),
            (late_other, 1 - half, 1 - core),
        ):
            rows[pl.ds(pl.multiple_of((2 * h + c) * part, part), part), :] = ref[...]

    made = jnp.dot(rows[...], weight[...], preferred_element_type=F32)
    conv_grad[...] = (made * gating[...].astype(F32)).astype(BF16)
    grad_gate[...] = (made * response[...]).astype(BF16)


def project(early, early_other, late, late_other, weight, gating, response, after):
    length, channels = gating.shape
    depth = weight.shape[0]
    return pl.pallas_call(
        project_kernel,
        grid=(channels // WIDE,),
        in_specs=[full(early.shape)] * 4
        + [tile(depth, WIDE), tile(length, WIDE), tile(length, WIDE), ANYWHERE],
        out_specs=[tile(length, WIDE)] * 2,
        out_shape=[jax.ShapeDtypeStruct((length, channels), BF16)] * 2,
        scratch_shapes=[pltpu.VMEM((length, depth), BF16)],
        compiler_params=PARAMS,
        cost_estimate=lasting(7),
        name="project",
    )(early, early_other, late, late_other, weight, gating, response, after)


def weight_kernel(*refs):
    shifts = SIDE - 1
    counts = (1, 1, SIDE, SIDE, 1, shifts, shifts, shifts, shifts, 1, 2 * SIDE, 2)
    taken, groups = 0, []
    for count in counts:
        groups.append(refs[taken : taken + count])
        taken += count
    own_x, own_y, late_x, late_y, gated, gated_x, gated_y, early_x, early_y, _, outs, turned = groups
    x, y, _, half, _ = spot()
    run = 64

    def unfolded(ref):
        width = late_x[0].shape[1]
        return jnp.concatenate([ref[:, :width], ref[:, width:]], 0)

    @pl.when(pl.program_id(0) == 0)
    def _():
        for into, own, early, late, me in (
            (turned[0], own_x[0], early_x, late_x, y),
            (turned[1], own_y[0], early_y, late_y, x),
        ):
            for s in range(SIDE):
                for block, h in (
                    (own[...] if s == 0 else unfolded(early[s - 1]), half),
                    (late[s][...], 1 - half),
                ):
                    whole = block.T
                    columns = pl.ds(pl.multiple_of(s * 2 * TAPS + h * TAPS, TAPS), TAPS)
                    for d in range(2):
                        for other in range(SIDE):
                            to = (other - me + SIDE) % SIDE
                            rows = pl.ds(pl.multiple_of(to * 2 * run + d * run, run), run)
                            start = (d * SIDE + other) * run
                            into[rows, columns] = whole[start : start + run]

    for which, blocks in ((0, gated + gated_x), (1, gated + gated_y)):
        tokens = jnp.concatenate([ref[...] for ref in blocks], 0)
        made = jnp.dot(turned[which][...], tokens, preferred_element_type=F32)
        for s in range(SIDE):
            out = outs[which * SIDE + s]
            out[...] = made[s * 2 * run : (s + 1) * 2 * run].astype(out.dtype)


def weight_parts(own_x, own_y, late_x, late_y, gated, got_x, got_y, after):
    length, channels = gated.shape
    tokens, width = own_x.shape
    rows = width // SIDE
    folded = got_x[0].shape[0] - length
    tail = pl.BlockSpec((folded, channels), lambda i: (length // folded, 0))
    outs = pl.pallas_call(
        weight_kernel,
        grid=(channels // WIDE,),
        in_specs=[full((tokens, width))] * (2 + 2 * SIDE)
        + [tile(length, WIDE)] * (2 * SIDE - 1)
        + [tail] * (2 * SIDE - 2)
        + [ANYWHERE],
        out_specs=[tile(rows, WIDE)] * (2 * SIDE),
        out_shape=[
            jax.ShapeDtypeStruct((rows, channels), F32 if s % SIDE == 0 else BF16)
            for s in range(2 * SIDE)
        ],
        scratch_shapes=[pltpu.VMEM((width, SIDE * length), BF16)] * 2,
        compiler_params=PARAMS,
        cost_estimate=lasting(6),
        name="weight_parts",
    )(own_x, own_y, *late_x, *late_y, gated, *got_x, *got_y, *got_x, *got_y, after)
    return outs[:SIDE], outs[SIDE:]


def gather_sum_kernel(*refs):
    _, _, z, _, _ = spot()
    outs, kept = refs[2 * SIDE : 3 * SIDE], refs[3 * SIDE]
    run = kept.shape[0] // SIDE
    for which in range(2):
        total = refs[which * SIDE][...]
        for s in range(1, SIDE):
            total = total + refs[which * SIDE + s][...].astype(F32)
        for d in range(2):
            to = (2 * which + d - z + SIDE) % SIDE
            kept[pl.ds(pl.multiple_of(to * run, run), run), :] = total[d * run : (d + 1) * run]
    for s in range(SIDE):
        outs[s][...] = kept[s * run : (s + 1) * run, :].astype(outs[s].dtype)


def gather_sum(parts_x, parts_y):
    rows, channels = parts_x[0].shape
    run = rows // 2
    return pl.pallas_call(
        gather_sum_kernel,
        grid=(channels // WIDE,),
        in_specs=[tile(rows, WIDE)] * (2 * SIDE),
        out_specs=[tile(run, WIDE)] * SIDE,
        out_shape=[
            jax.ShapeDtypeStruct((run, channels), F32 if s == 0 else BF16) for s in range(SIDE)
        ],
        scratch_shapes=[pltpu.VMEM((SIDE * run, WIDE), F32)],
        compiler_params=PARAMS,
        cost_estimate=lasting(1),
        name="gather_sum",
    )(*parts_x, *parts_y)


def tied(x, *after):
    return lax.optimization_barrier((x, *after))[0]


def partnered(x, axis, by):
    if axis == "z":
        return lax.ppermute(x, "dp", [(i, i ^ by) for i in range(SIDE)])
    step = by * (SIDE if axis == "x" else 1)
    return lax.ppermute(x, "ctx", [(i, i ^ step) for i in range(SIDE * SIDE)])


def summed(x):
    for axis in ("x", "y", "z"):
        for by in (1, 2):
            x = x + partnered(x, axis, by)
    return x


def exchanged(sends, axis):
    return [moved(sends[s - 1], axis, s) for s in range(1, SIDE)]


def local(conv_input, gate_value, out_grad, out_weight, filters):
    signal, gating, grads = conv_input[0], gate_value[0], out_grad[0]
    length, channels = signal.shape
    shifts = range(1, SIDE)

    previous = shifted(signal[length - TAPS :], 1)
    early_other = moved(grads, "core", 1)
    late = moved(grads, "half", 1)
    signal, gating, filters, grads = (resident(x) for x in (signal, gating, filters, grads))
    early_x, early_y = pack(grads, early_other)
    response, gated, *sends = forward(
        filters, previous, signal, gating, [*early_x[1:], *early_y[1:]]
    )
    got_x, got_y = [], []
    for got, axis, parts in ((got_x, "x", sends[: SIDE - 1]), (got_y, "y", sends[SIDE - 1 :])):
        first = moved(parts[0], axis, 1)
        got += [first, moved(tied(parts[1], first), axis, 2), moved(parts[2], axis, 3)]

    late_other = moved(late, "core", 1)
    late_x, late_y = pack(late, late_other, got_x[0], got_y[0], got_x[2], got_y[2])
    conv_grad, grad_gate = project(
        grads, early_other, late, late_other, resident(out_weight), gating, response, late_x[0]
    )
    late_x = [late_x[0]] + exchanged(late_x[1:], "x")
    late_y = [late_y[0]] + exchanged(late_y[1:], "y")
    following = shifted(conv_grad[:TAPS], -1)
    filter_local = filter_grad(previous, signal, conv_grad)

    parts_x, parts_y = weight_parts(
        early_x[0], early_y[0], late_x, late_y, gated, got_x, got_y, filter_local
    )
    grad_input = input_grad(filters, conv_grad, following, parts_x[0])
    parts_x = [parts_x[0]] + exchanged(parts_x[1:], "y")
    parts_y = [parts_y[0]] + exchanged(parts_y[1:], "x")
    filter_total = summed(tied(filter_local, parts_x[1]))
    chunks = gather_sum(parts_x, parts_y)
    weight_total = chunks[0]
    for s in shifts:
        weight_total = weight_total + moved(chunks[s], "z", s).astype(F32)

    tokens_all = lax.axis_size("dp") * lax.axis_size("ctx") * length
    grad_filter = filter_total * (1.0 / math.sqrt(tokens_all * GROUP))
    grad_weight = weight_total * (1.0 / math.sqrt(tokens_all))
    return (grad_input[None], grad_gate[None], grad_weight, grad_filter)


def solution(mesh):
    placed = (
        P("dp", "ctx", "tp"),
        P("dp", "ctx", "tp"),
        P("dp", ("ctx", "tp"), None),
        P(None, "tp"),
        P("tp", None),
    )
    return jax.shard_map(
        local,
        mesh=mesh,
        in_specs=placed,
        out_specs=(
            P("dp", "ctx", "tp"),
            P("dp", "ctx", "tp"),
            P(("dp", "ctx"), "tp"),
            P("tp", None),
        ),
        check_vma=False,
    )
```

```python
import math

import jax
import jax.numpy as jnp
from jax import lax
from jax.experimental import pallas as pl
from jax.experimental.pallas import tpu as pltpu
from jax.sharding import PartitionSpec as P

F32 = jnp.float32
BF16 = jnp.bfloat16
SIDE = 4
TAPS = 128
GROUP = 16
LANES = 128
PER_TILE = LANES // GROUP
WIDE = 256


def room(mebibytes):
    return pltpu.CompilerParams(vmem_limit_bytes=mebibytes * 1024 * 1024)


def spot():
    ctx = lax.axis_index("ctx")
    tp = lax.axis_index("tp")
    return ctx // SIDE, ctx % SIDE, lax.axis_index("dp"), tp // 2, tp % 2


def moved(x, axis, by):
    if axis == "x":
        pairs = [(i, (i // SIDE + by) % SIDE * SIDE + i % SIDE) for i in range(SIDE * SIDE)]
        return lax.ppermute(x, "ctx", pairs)
    if axis == "y":
        pairs = [(i, i // SIDE * SIDE + (i % SIDE + by) % SIDE) for i in range(SIDE * SIDE)]
        return lax.ppermute(x, "ctx", pairs)
    if axis == "z":
        return lax.ppermute(x, "dp", [(i, (i + by) % SIDE) for i in range(SIDE)])
    if axis == "half":
        return lax.ppermute(x, "tp", [(i, (i + 2) % 4) for i in range(4)])
    return lax.ppermute(x, "tp", [(i, i // 2 * 2 + (i + 1) % 2) for i in range(4)])


def shifted(x, by):
    devices = lax.axis_size("ctx")
    return lax.ppermute(x, "ctx", [(i, i + by) for i in range(devices) if 0 <= i + by < devices])


ANYWHERE = pl.BlockSpec(memory_space=pl.ANY)
HALF = LANES // 2


def resident(x):
    return pltpu.with_memory_space_constraint(x, pltpu.HBM)


def whole(shape, place=None):
    place = place or (0,) * len(shape)
    return pl.BlockSpec(tuple(shape), lambda i: place, pipeline_mode=pl.Buffered(1))


def full(shape):
    return pl.BlockSpec(tuple(shape), lambda i: (0,) * len(shape))


def tile(rows, width):
    return pl.BlockSpec((rows, width), lambda i: (0, i))


def iota(shape, dim):
    return lax.broadcasted_iota(jnp.int32, shape, dim)


def aligned(index, size):
    return pl.ds(pl.multiple_of(index * size, size), size)


def lasting(microseconds):
    return pl.CostEstimate(flops=int(microseconds * 1e9), bytes_accessed=0, transcendentals=0)


def once(kernel, name, ins, outs, scratch=(), after=(), lasts=0):
    def body(*refs):
        kernel(*refs[: len(ins)], *refs[len(ins) + len(after) :])

    specs = [i[1] if isinstance(i, tuple) else whole(i.shape) for i in ins]
    arrays = [i[0] if isinstance(i, tuple) else i for i in ins]
    return pl.pallas_call(
        body,
        grid=(1,),
        in_specs=specs + [ANYWHERE] * len(after),
        out_specs=[whole(shape) for shape, _ in outs],
        out_shape=[jax.ShapeDtypeStruct(shape, dtype) for shape, dtype in outs],
        scratch_shapes=list(scratch),
        compiler_params=room(12),
        cost_estimate=lasting(lasts),
        name=name,
    )(*arrays, *after)


def first_rows(filters, shifted_by):
    lane, tap = iota((TAPS, 2 * TAPS), 1), iota((TAPS, 2 * TAPS), 0)
    place = lane == (TAPS - tap if shifted_by else tap)
    return jnp.dot(filters, place.astype(F32).astype(BF16), preferred_element_type=F32)


def banded(rows, stack):
    for g in range(PER_TILE):
        first = jnp.broadcast_to(rows[g : g + 1], (TAPS, 2 * TAPS))
        skewed = pltpu.roll(first, 0, 1, stride=1, stride_axis=0)
        stack[g * TAPS : (g + 1) * TAPS, :] = skewed.astype(BF16)


def lane_group(shape):
    return iota(shape, len(shape) - 1) % LANES // GROUP


def own_lanes(stacked):
    group = lane_group((TAPS, 2 * LANES))
    chosen = jnp.zeros((TAPS, 2 * LANES), F32)
    for g in range(PER_TILE):
        chosen = jnp.where(group == g, stacked[g * TAPS : (g + 1) * TAPS], chosen)
    return chosen


def two_windows(first, second, third):
    upper = jnp.concatenate([first, second], 1)
    lower = jnp.concatenate([second, third], 1)
    return jnp.concatenate([upper, lower], 0)


def forward_kernel(filters, previous, signal, gating, *refs):
    shifts = SIDE - 1
    early, (response, gated), sends = refs[: 2 * shifts], refs[2 * shifts : 2 * shifts + 2], refs[2 * shifts + 2 : -1]
    stack = refs[-1]
    rows = first_rows(filters[...], True)
    count = signal.shape[1] // LANES
    for i in range(count):
        columns = slice(i * LANES, (i + 1) * LANES)
        which, place = divmod(i, count // 2)
        to = slice(place * LANES, (place + 1) * LANES)
        band = stack.at[i % 2]
        banded(rows[i * PER_TILE : (i + 1) * PER_TILE], band)
        window = two_windows(previous[:, columns], signal[:TAPS, columns], signal[TAPS:, columns])
        made = own_lanes(jnp.dot(band[...], window, preferred_element_type=F32))
        for block in range(2):
            tokens = slice(block * TAPS, (block + 1) * TAPS)
            part = made[:, block * LANES : (block + 1) * LANES]
            response[tokens, columns] = part
            product = (part * gating[tokens, columns].astype(F32)).astype(BF16)
            gated[tokens, columns] = product
            for send in sends[which * shifts : (which + 1) * shifts]:
                send[tokens, to] = product
    for ref, send in zip(early, sends):
        send[2 * TAPS :] = ref[...]


def forward(filters, previous, signal, gating, early):
    length, channels = signal.shape
    rows, width = early[0].shape
    response, gated, *sends = once(
        forward_kernel,
        "conv_forward",
        [filters, previous, signal, gating, *early],
        [((length, channels), F32), ((length, channels), BF16)]
        + [((length + rows, width), BF16)] * len(early),
        [pltpu.VMEM((2, PER_TILE * TAPS, 2 * TAPS), BF16)],
    )
    return response, gated, sends[: SIDE - 1], sends[SIDE - 1 :]


def input_grad_kernel(filters, conv_grad, following, grad_input, stack):
    rows = first_rows(filters[...], False)
    for i in range(conv_grad.shape[1] // LANES):
        columns = slice(i * LANES, (i + 1) * LANES)
        band = stack.at[i % 2]
        banded(rows[i * PER_TILE : (i + 1) * PER_TILE], band)
        window = two_windows(
            conv_grad[:TAPS, columns], conv_grad[TAPS:, columns], following[:, columns]
        )
        made = own_lanes(jnp.dot(band[...], window, preferred_element_type=F32))
        for block in range(2):
            grad_input[block * TAPS : (block + 1) * TAPS, columns] = made[
                :, block * LANES : (block + 1) * LANES
            ].astype(BF16)


def input_grad(filters, conv_grad, following, after):
    return once(
        input_grad_kernel,
        "input_grad",
        [filters, conv_grad, following],
        [(conv_grad.shape, BF16)],
        [pltpu.VMEM((2, PER_TILE * TAPS, 2 * TAPS), BF16)],
        after,
        4,
    )[0]


def filter_grad_kernel(previous, signal, conv_grad, grad_filter, stack):
    square = (2 * TAPS, 2 * TAPS)
    turn = iota(square, 0) == (2 * TAPS - iota(square, 1)) % (2 * TAPS)
    turn = turn.astype(F32).astype(BF16)
    group = lane_group((TAPS, 2 * LANES))
    for i in range(signal.shape[1] // LANES):
        columns = slice(i * LANES, (i + 1) * LANES)
        masked = stack.at[i % 2]
        inputs = two_windows(previous[:, columns], signal[:TAPS, columns], signal[TAPS:, columns])
        turned = jnp.dot(turn, inputs, preferred_element_type=F32).astype(BF16)
        both = jnp.concatenate([conv_grad[:TAPS, columns], conv_grad[TAPS:, columns]], 1)
        both = both.astype(F32)
        for g in range(PER_TILE):
            masked[g * TAPS : (g + 1) * TAPS, :] = jnp.where(group == g, both, 0.0).astype(BF16)
        products = lax.dot_general(
            masked[...], turned, (((1,), (1,)), ((), ())), preferred_element_type=F32
        )
        for g in range(PER_TILE):
            skewed = pltpu.roll(products[g * TAPS : (g + 1) * TAPS], 0, 1, stride=1, stride_axis=0)
            row = i * PER_TILE + g
            grad_filter[row : row + 1, :] = jnp.sum(skewed[:, TAPS:], axis=0, keepdims=True)


def filter_grad(previous, signal, conv_grad, after):
    return once(
        filter_grad_kernel,
        "filter_grad",
        [previous, signal, conv_grad],
        [((signal.shape[1] // GROUP, TAPS), F32)],
        [pltpu.VMEM((2, PER_TILE * TAPS, 2 * TAPS), BF16)],
        after,
        4,
    )[0]


def pack_kernel(mine, *outs):
    x, y, _, _, _ = spot()
    part = mine.shape[0]
    depth = mine.shape[1] // SIDE
    lower = iota((part, LANES), 1) < HALF
    for s in range(SIDE):
        to_x, to_y = (x + s) % SIDE, (y + s) % SIDE
        upper_half = jnp.broadcast_to(to_y % 2, (part, LANES)) == 1
        for d in range(SIDE):
            rows = slice(d // 2 * part, (d // 2 + 1) * part)
            column = d % 2 * WIDE
            start = pl.multiple_of(d * depth + to_x * WIDE, WIDE)
            outs[s][rows, column : column + WIDE] = mine[:, pl.ds(start, WIDE)]
            for pair in range(SIDE // 2):
                runs = []
                for i in range(2):
                    start = d * depth + (2 * pair + i) * WIDE + to_y // 2 * LANES
                    runs.append(mine[:, pl.ds(pl.multiple_of(start, LANES), LANES)].astype(F32))
                first = jnp.where(upper_half, pltpu.roll(runs[0], HALF, 1), runs[0])
                second = jnp.where(upper_half, runs[1], pltpu.roll(runs[1], HALF, 1))
                both = jnp.where(lower, first, second).astype(BF16)
                at = column + pair * LANES
                outs[SIDE + s][rows, at : at + LANES] = both


def pack(mine, after=()):
    part, width = mine.shape
    outs = once(
        pack_kernel, "pack", [mine], [((2 * part, width // (2 * SIDE)), BF16)] * (2 * SIDE), (), after
    )
    return outs[:SIDE], outs[SIDE:]


def turn_into(parts, out, base, me):
    part = parts[0].shape[0] // 2
    for fold in range(2):
        for pair in range(SIDE // 2):
            block = jnp.concatenate(
                [ref[fold * part : (fold + 1) * part] for ref in parts[2 * pair : 2 * pair + 2]], 0
            )
            whole = block.T
            for d in range(2):
                for q in range(SIDE):
                    to = (q - me + SIDE) % SIDE
                    rows = pl.ds(pl.multiple_of(base + to * WIDE + (2 * fold + d) * HALF, HALF), HALF)
                    start = d * WIDE + q * HALF
                    out[rows, pair * LANES : (pair + 1) * LANES] = whole[start : start + HALF]


def turn_early_kernel(*refs):
    x, y, _, _, _ = spot()
    out = refs[-1]
    turn_into(refs[:SIDE], out, 0, y)
    turn_into(refs[SIDE : 2 * SIDE], out, out.shape[0] // 2, x)


def turn_early(own_x, got_x, own_y, got_y, after):
    rows, width = own_x.shape
    count = got_x[0].shape[0] // rows
    tail = whole((rows, width), (count - 1, 0))
    parts = [own_x, *[(got, tail) for got in got_x], own_y, *[(got, tail) for got in got_y]]
    return once(turn_early_kernel, "turn_early", parts, [((4 * width, WIDE), BF16)], (), after)[0]


def turn_late(parts, axis, after=()):
    def kernel(*refs):
        x, y, _, _, _ = spot()
        turn_into(refs[:SIDE], refs[-1], 0, y if axis == "x" else x)

    return once(kernel, "turn_late", parts, [((2 * parts[0].shape[1], WIDE), BF16)], (), after)[0]


def project_kernel(mine, other, weight, gating, response, *refs):
    _, _, _, half, core = spot()
    part = mine.shape[0]
    rows = refs[-1]
    conv_grad, grad_gate = refs[-3:-1]

    @pl.when(pl.program_id(0) == 0)
    def _():
        rows[aligned(core, part), :] = mine[...]
        rows[aligned(1 - core, part), :] = other[...]

    late = len(refs) > 3
    tokens = aligned(1 - half if late else half, TAPS)
    made = jnp.dot(rows[...], weight[...], preferred_element_type=F32)
    made_conv = (made * gating[tokens, :].astype(F32)).astype(BF16)
    made_gate = (made * response[tokens, :]).astype(BF16)
    if late:
        conv_grad[tokens, :] = made_conv
        grad_gate[tokens, :] = made_gate
        conv_grad[aligned(half, TAPS), :] = refs[0][...]
        grad_gate[aligned(half, TAPS), :] = refs[1][...]
    else:
        conv_grad[...] = made_conv
        grad_gate[...] = made_gate


def project(mine, other, weight, gating, response, done=(), after=()):
    length, channels = gating.shape
    depth = weight.shape[0]
    made = length if done else 2 * mine.shape[0]

    def body(*refs):
        kept = 5 + len(done)
        project_kernel(*refs[:kept], *refs[kept + len(after) :])

    return pl.pallas_call(
        body,
        grid=(channels // WIDE,),
        in_specs=[full(mine.shape)] * 2
        + [tile(depth, WIDE), tile(length, WIDE), tile(length, WIDE)]
        + [tile(TAPS, WIDE)] * len(done)
        + [ANYWHERE] * len(after),
        out_specs=[tile(made, WIDE)] * 2,
        out_shape=[jax.ShapeDtypeStruct((made, channels), BF16)] * 2,
        scratch_shapes=[pltpu.VMEM((2 * mine.shape[0], depth), BF16)],
        compiler_params=room(16),
        cost_estimate=lasting(5 if done else 0),
        name="project_late" if done else "project_early",
    )(mine, other, weight, gating, response, *done, *after)


def weight_kernel(early, early_other, late, late_other, gated, *refs):
    _, _, _, half, core = spot()
    got, outs = refs[: SIDE - 1], refs[SIDE - 1 :]
    part = WIDE // SIDE
    tokens = []
    for h, c in ((half, core), (half, 1 - core), (1 - half, core), (1 - half, 1 - core)):
        rows = aligned(2 * h + c, part)
        tokens += [gated[rows, :]] + [ref[rows, :] for ref in got]
    tokens = jnp.concatenate(tokens, 0)
    for s, out in enumerate(outs):
        rows = slice(s * WIDE, (s + 1) * WIDE)
        features = jnp.concatenate([ref[rows] for ref in (early, early_other, late, late_other)], 1)
        out[...] = jnp.dot(features, tokens, preferred_element_type=F32).astype(out.dtype)


def weight_part(which, early, early_other, late, late_other, gated, got, after=()):
    length = gated.shape[0]
    features = late.shape[0]
    width = got[0].shape[1]
    spec = whole((features, WIDE), (which, 0))
    return once(
        weight_kernel,
        "weight_part",
        [
            (early, spec),
            (early_other, spec),
            late,
            late_other,
            (gated, whole((length, width), (0, which))),
            *[(one, whole((length, width))) for one in got],
        ],
        [((features // SIDE, width), F32 if s == 0 else BF16) for s in range(SIDE)],
        (),
        after,
        3,
    )


def first_sum_kernel(*refs):
    _, _, z, _, _ = spot()
    outs, kept = refs[SIDE : 2 * SIDE], refs[2 * SIDE]
    total = refs[0][...]
    for ref in refs[1:SIDE]:
        total = total + ref[...].astype(F32)
    run = kept.shape[0] // SIDE
    for d in range(SIDE):
        kept[aligned((d - z + SIDE) % SIDE, run), :] = total[d * run : (d + 1) * run]
    for s, out in enumerate(outs):
        out[...] = kept[s * run : (s + 1) * run, :].astype(out.dtype)


def first_sum(parts, after=()):
    rows, width = parts[0].shape
    return once(
        first_sum_kernel,
        "first_sum",
        parts,
        [((rows // SIDE, width), F32 if s == 0 else BF16) for s in range(SIDE)],
        [pltpu.VMEM((rows, width), F32)],
        after,
        1,
    )


def last_sum(parts_x, parts_y, scale):
    def kernel(*refs):
        out = refs[-1]
        width = refs[0].shape[1]
        for which in range(2):
            total = refs[which * SIDE][...]
            for ref in refs[which * SIDE + 1 : (which + 1) * SIDE]:
                total = total + ref[...].astype(F32)
            out[:, which * width : (which + 1) * width] = total * scale

    rows, width = parts_x[0].shape
    return once(kernel, "last_sum", [*parts_x, *parts_y], [((rows, 2 * width), F32)])[0]


def tied(x, *after):
    return lax.optimization_barrier((x, *after))[0]


def partnered(x, axis, by):
    if axis == "z":
        return lax.ppermute(x, "dp", [(i, i ^ by) for i in range(SIDE)])
    step = by * (SIDE if axis == "x" else 1)
    return lax.ppermute(x, "ctx", [(i, i ^ step) for i in range(SIDE * SIDE)])


def paired(x, axis, by, after=()):
    return x + partnered(tied(x, *after), axis, by)


def exchanged(parts, axis):
    return [parts[0]] + [moved(parts[s], axis, s) for s in range(1, SIDE)]


def local(conv_input, gate_value, out_grad, out_weight, filters):
    signal, gating, grads = conv_input[0], gate_value[0], out_grad[0]
    length, channels = signal.shape
    halo_sent = signal[length - TAPS :]
    signal, gating, filters, weight = (
        resident(x) for x in (signal, gating, filters, out_weight)
    )
    tokens_all = lax.axis_size("dp") * lax.axis_size("ctx") * length

    late = moved(grads, "half", 1)
    previous = shifted(halo_sent, 1)
    early_other = moved(grads, "core", 1)
    early_x, early_y = pack(resident(grads), (early_other,))
    response, gated, sends_x, sends_y = forward(
        filters, previous, signal, gating, [*early_x[1:], *early_y[1:]]
    )
    got_x, got_y = [], []
    for got, axis, parts in ((got_x, "x", sends_x), (got_y, "y", sends_y)):
        first = moved(parts[0], axis, 1)
        got += [first, moved(tied(parts[1], first), axis, 2), moved(parts[2], axis, 3)]
    conv_early, gate_early = project(resident(grads), early_other, weight, gating, response)

    late_other = moved(tied(late, conv_early, got_x[0], got_y[0], got_x[2], got_y[2]), "core", 1)
    late_x, late_y = pack(late, (late_other,))
    late_x = exchanged(late_x, "x")
    late_y = exchanged(late_y, "y")
    conv_grad, grad_gate = project(
        late,
        late_other,
        weight,
        gating,
        response,
        (conv_early, gate_early),
        (late_x[0],),
    )
    early = turn_early(early_x[0], got_x, early_y[0], got_y, (conv_grad, *late_x[1:], *late_y[1:]))
    early_swap = moved(early, "core", 1)
    turned_x = turn_late(late_x, "x", (early,))
    swap_x = moved(turned_x, "core", 1)
    turned_y = turn_late(late_y, "y", (turned_x,))
    swap_y = moved(turned_y, "core", 1)
    following = shifted(conv_grad[:TAPS], -1)
    filter_local = filter_grad(previous, signal, conv_grad, (turned_y,))
    parts_x = weight_part(
        0, early, early_swap, turned_x, swap_x, gated, got_x, (filter_local,)
    )
    parts_y = weight_part(
        1, early, early_swap, turned_y, swap_y, gated, got_y, (parts_x[0],)
    )
    filter_sum = paired(filter_local, "x", 1)
    filter_sum = paired(filter_sum, "x", 2, (parts_x[0],))
    filter_sum = paired(filter_sum, "y", 1, (parts_y[0],))
    parts_x, parts_y = exchanged(parts_x, "y"), exchanged(parts_y, "x")
    filter_sum = paired(filter_sum, "y", 2, (parts_x[1], parts_x[3]))
    sums_x = first_sum(parts_x)
    filter_sum = paired(filter_sum, "z", 1, (sums_x[0],))
    sums_y = first_sum(parts_y, (sums_x[0],))
    filter_total = paired(filter_sum, "z", 2, (sums_y[0],))
    grad_input = input_grad(filters, conv_grad, following, (sums_y[0],))
    grad_weight = last_sum(
        exchanged(sums_x, "z"), exchanged(sums_y, "z"), 1.0 / math.sqrt(tokens_all)
    )
    grad_filter = filter_total * (1.0 / math.sqrt(tokens_all * GROUP))
    return (grad_input[None], grad_gate[None], grad_weight, grad_filter)


def solution(mesh):
    placed = (
        P("dp", "ctx", "tp"),
        P("dp", "ctx", "tp"),
        P("dp", ("ctx", "tp"), None),
        P(None, "tp"),
        P("tp", None),
    )
    return jax.shard_map(
        local,
        mesh=mesh,
        in_specs=placed,
        out_specs=(
            P("dp", "ctx", "tp"),
            P("dp", "ctx", "tp"),
            P(("dp", "ctx"), "tp"),
            P("tp", None),
        ),
        check_vma=False,
    )
```

```python
import math

import jax
import jax.numpy as jnp
from jax import lax
from jax.experimental import pallas as pl
from jax.experimental.pallas import tpu as pltpu
from jax.sharding import PartitionSpec as P

F32 = jnp.float32
BF16 = jnp.bfloat16
SIDE = 4
TAPS = 128
GROUP = 16
LANES = 128
PER_TILE = LANES // GROUP
WIDE = 256


def room(mebibytes):
    return pltpu.CompilerParams(vmem_limit_bytes=mebibytes * 1024 * 1024)


def spot():
    ctx = lax.axis_index("ctx")
    tp = lax.axis_index("tp")
    return ctx // SIDE, ctx % SIDE, lax.axis_index("dp"), tp // 2, tp % 2


def moved(x, axis, by):
    if axis == "x":
        pairs = [(i, (i // SIDE + by) % SIDE * SIDE + i % SIDE) for i in range(SIDE * SIDE)]
        return lax.ppermute(x, "ctx", pairs)
    if axis == "y":
        pairs = [(i, i // SIDE * SIDE + (i % SIDE + by) % SIDE) for i in range(SIDE * SIDE)]
        return lax.ppermute(x, "ctx", pairs)
    if axis == "z":
        return lax.ppermute(x, "dp", [(i, (i + by) % SIDE) for i in range(SIDE)])
    if axis == "half":
        return lax.ppermute(x, "tp", [(i, (i + 2) % 4) for i in range(4)])
    return lax.ppermute(x, "tp", [(i, i // 2 * 2 + (i + 1) % 2) for i in range(4)])


def shifted(x, by):
    devices = lax.axis_size("ctx")
    return lax.ppermute(x, "ctx", [(i, i + by) for i in range(devices) if 0 <= i + by < devices])


ANYWHERE = pl.BlockSpec(memory_space=pl.ANY)
HALF = LANES // 2


def resident(x):
    return pltpu.with_memory_space_constraint(x, pltpu.HBM)


def whole(shape, place=None):
    place = place or (0,) * len(shape)
    return pl.BlockSpec(tuple(shape), lambda i: place, pipeline_mode=pl.Buffered(1))


def full(shape):
    return pl.BlockSpec(tuple(shape), lambda i: (0,) * len(shape))


def tile(rows, width):
    return pl.BlockSpec((rows, width), lambda i: (0, i))


def iota(shape, dim):
    return lax.broadcasted_iota(jnp.int32, shape, dim)


def aligned(index, size):
    return pl.ds(pl.multiple_of(index * size, size), size)


def lasting(microseconds):
    return pl.CostEstimate(flops=int(microseconds * 1e9), bytes_accessed=0, transcendentals=0)


def once(kernel, name, ins, outs, scratch=(), after=(), lasts=0):
    def body(*refs):
        kernel(*refs[: len(ins)], *refs[len(ins) + len(after) :])

    specs = [i[1] if isinstance(i, tuple) else whole(i.shape) for i in ins]
    arrays = [i[0] if isinstance(i, tuple) else i for i in ins]
    return pl.pallas_call(
        body,
        grid=(1,),
        in_specs=specs + [ANYWHERE] * len(after),
        out_specs=[whole(shape) for shape, _ in outs],
        out_shape=[jax.ShapeDtypeStruct(shape, dtype) for shape, dtype in outs],
        scratch_shapes=list(scratch),
        compiler_params=room(12),
        cost_estimate=lasting(lasts),
        name=name,
    )(*arrays, *after)


def first_rows(filters, shifted_by):
    lane, tap = iota((TAPS, 2 * TAPS), 1), iota((TAPS, 2 * TAPS), 0)
    place = lane == (TAPS - tap if shifted_by else tap)
    return jnp.dot(filters, place.astype(F32).astype(BF16), preferred_element_type=F32)


def banded(rows, stack):
    for g in range(PER_TILE):
        first = jnp.broadcast_to(rows[g : g + 1], (TAPS, 2 * TAPS))
        skewed = pltpu.roll(first, 0, 1, stride=1, stride_axis=0)
        stack[g * TAPS : (g + 1) * TAPS, :] = skewed.astype(BF16)


def lane_group(shape):
    return iota(shape, len(shape) - 1) % LANES // GROUP


def own_lanes(stacked):
    group = lane_group((TAPS, 2 * LANES))
    chosen = jnp.zeros((TAPS, 2 * LANES), F32)
    for g in range(PER_TILE):
        chosen = jnp.where(group == g, stacked[g * TAPS : (g + 1) * TAPS], chosen)
    return chosen


def two_windows(first, second, third):
    upper = jnp.concatenate([first, second], 1)
    lower = jnp.concatenate([second, third], 1)
    return jnp.concatenate([upper, lower], 0)


def forward_kernel(filters, previous, signal, gating, *refs):
    shifts = 2
    early, (response, gated), sends = refs[: 2 * shifts], refs[2 * shifts : 2 * shifts + 2], refs[2 * shifts + 2 : -1]
    stack = refs[-1]
    rows = first_rows(filters[...], True)
    count = signal.shape[1] // LANES
    for i in range(count):
        columns = slice(i * LANES, (i + 1) * LANES)
        which, place = divmod(i, count // 2)
        to = slice(place * LANES, (place + 1) * LANES)
        band = stack.at[i % 2]
        banded(rows[i * PER_TILE : (i + 1) * PER_TILE], band)
        window = two_windows(previous[:, columns], signal[:TAPS, columns], signal[TAPS:, columns])
        made = own_lanes(jnp.dot(band[...], window, preferred_element_type=F32))
        for block in range(2):
            tokens = slice(block * TAPS, (block + 1) * TAPS)
            part = made[:, block * LANES : (block + 1) * LANES]
            response[tokens, columns] = part
            product = (part * gating[tokens, columns].astype(F32)).astype(BF16)
            gated[tokens, columns] = product
            for send in sends[which * shifts : (which + 1) * shifts]:
                send[tokens, to] = product
    for ref, send in zip(early, sends):
        send[2 * TAPS :] = ref[...]


def forward(filters, previous, signal, gating, early):
    length, channels = signal.shape
    rows, width = early[0].shape
    response, gated, *sends = once(
        forward_kernel,
        "conv_forward",
        [filters, previous, signal, gating, *early],
        [((length, channels), F32), ((length, channels), BF16)]
        + [((length + rows, width), BF16)] * len(early),
        [pltpu.VMEM((2, PER_TILE * TAPS, 2 * TAPS), BF16)],
    )
    return response, gated, sends[:2], sends[2:]


def input_grad_kernel(filters, conv_grad, following, grad_input, stack):
    rows = first_rows(filters[...], False)
    for i in range(conv_grad.shape[1] // LANES):
        columns = slice(i * LANES, (i + 1) * LANES)
        band = stack.at[i % 2]
        banded(rows[i * PER_TILE : (i + 1) * PER_TILE], band)
        window = two_windows(
            conv_grad[:TAPS, columns], conv_grad[TAPS:, columns], following[:, columns]
        )
        made = own_lanes(jnp.dot(band[...], window, preferred_element_type=F32))
        for block in range(2):
            grad_input[block * TAPS : (block + 1) * TAPS, columns] = made[
                :, block * LANES : (block + 1) * LANES
            ].astype(BF16)


def input_grad(filters, conv_grad, following, after):
    return once(
        input_grad_kernel,
        "input_grad",
        [filters, conv_grad, following],
        [(conv_grad.shape, BF16)],
        [pltpu.VMEM((2, PER_TILE * TAPS, 2 * TAPS), BF16)],
        after,
    )[0]


def filter_grad_kernel(previous, signal, conv_grad, grad_filter, stack):
    square = (2 * TAPS, 2 * TAPS)
    turn = iota(square, 0) == (2 * TAPS - iota(square, 1)) % (2 * TAPS)
    turn = turn.astype(F32).astype(BF16)
    group = lane_group((TAPS, 2 * LANES))
    for i in range(signal.shape[1] // LANES):
        columns = slice(i * LANES, (i + 1) * LANES)
        masked = stack.at[i % 2]
        inputs = two_windows(previous[:, columns], signal[:TAPS, columns], signal[TAPS:, columns])
        turned = jnp.dot(turn, inputs, preferred_element_type=F32).astype(BF16)
        both = jnp.concatenate([conv_grad[:TAPS, columns], conv_grad[TAPS:, columns]], 1)
        both = both.astype(F32)
        for g in range(PER_TILE):
            masked[g * TAPS : (g + 1) * TAPS, :] = jnp.where(group == g, both, 0.0).astype(BF16)
        products = lax.dot_general(
            masked[...], turned, (((1,), (1,)), ((), ())), preferred_element_type=F32
        )
        for g in range(PER_TILE):
            skewed = pltpu.roll(products[g * TAPS : (g + 1) * TAPS], 0, 1, stride=1, stride_axis=0)
            row = i * PER_TILE + g
            grad_filter[row : row + 1, :] = jnp.sum(skewed[:, TAPS:], axis=0, keepdims=True)


def filter_grad(previous, signal, conv_grad, after):
    return once(
        filter_grad_kernel,
        "filter_grad",
        [previous, signal, conv_grad],
        [((signal.shape[1] // GROUP, TAPS), F32)],
        [pltpu.VMEM((2, PER_TILE * TAPS, 2 * TAPS), BF16)],
        after,
        4,
    )[0]


def pack_kernel(mine, *outs):
    x, y, _, _, _ = spot()
    part = mine.shape[0]
    depth = mine.shape[1] // SIDE
    lower = iota((part, LANES), 1) < HALF
    for s in range(SIDE):
        to_x, to_y = (x + s) % SIDE, (y + s) % SIDE
        upper_half = jnp.broadcast_to(to_y % 2, (part, LANES)) == 1
        for d in range(SIDE):
            rows = slice(d // 2 * part, (d // 2 + 1) * part)
            column = d % 2 * WIDE
            start = pl.multiple_of(d * depth + to_x * WIDE, WIDE)
            outs[s][rows, column : column + WIDE] = mine[:, pl.ds(start, WIDE)]
            for pair in range(SIDE // 2):
                runs = []
                for i in range(2):
                    start = d * depth + (2 * pair + i) * WIDE + to_y // 2 * LANES
                    runs.append(mine[:, pl.ds(pl.multiple_of(start, LANES), LANES)].astype(F32))
                first = jnp.where(upper_half, pltpu.roll(runs[0], HALF, 1), runs[0])
                second = jnp.where(upper_half, runs[1], pltpu.roll(runs[1], HALF, 1))
                both = jnp.where(lower, first, second).astype(BF16)
                at = column + pair * LANES
                outs[SIDE + s][rows, at : at + LANES] = both


def pack(mine, after=()):
    part, width = mine.shape
    outs = once(
        pack_kernel, "pack", [mine], [((2 * part, width // (2 * SIDE)), BF16)] * (2 * SIDE), (), after
    )
    return outs[:SIDE], outs[SIDE:]


def relay_kernel(count, mine, *refs):
    before_x, after_x, before_y, after_y, opposite_x, opposite_y = refs[:6]
    outs = refs[6 + count :]
    part = opposite_x.shape[0]
    pack_kernel(mine, *(out.at[:part] for out in outs))
    for first, before, opposite, after in (
        (0, before_x, opposite_x, after_x),
        (SIDE, before_y, opposite_y, after_y),
    ):
        outs[first + 1][part:] = before[:TAPS]
        outs[first + 2][part:] = opposite[...]
        outs[first + 3][part:] = after[TAPS : 2 * TAPS]


def relay(mine, got_x, got_y, opposite_x, opposite_y, after):
    rows, width = opposite_x.shape
    got = [
        (part, whole((2 * TAPS, width))) for part in (got_x[0], got_x[1], got_y[0], got_y[1])
    ]
    shapes = ([(rows, width)] + [(rows + TAPS, width)] * (SIDE - 1)) * 2

    def kernel(*refs):
        relay_kernel(0, *refs)

    outs = once(
        kernel, "relay", [mine, *got, opposite_x, opposite_y], [(shape, BF16) for shape in shapes], (), after
    )
    return outs[:SIDE], outs[SIDE:]


def turn_into(parts, out, base, me):
    part = parts[0].shape[0] // 2
    for fold in range(2):
        for pair in range(SIDE // 2):
            block = jnp.concatenate(
                [ref[fold * part : (fold + 1) * part] for ref in parts[2 * pair : 2 * pair + 2]], 0
            )
            transposed = block.T
            for d in range(2):
                for q in range(SIDE):
                    to = (q - me + SIDE) % SIDE
                    rows = pl.ds(pl.multiple_of(base + to * WIDE + (2 * fold + d) * HALF, HALF), HALF)
                    start = d * WIDE + q * HALF
                    out[rows, pair * LANES : (pair + 1) * LANES] = transposed[start : start + HALF]


def turn_early_kernel(*refs):
    x, y, _, _, _ = spot()
    out = refs[-1]
    turn_into(refs[:SIDE], out, 0, y)
    turn_into(refs[SIDE : 2 * SIDE], out, out.shape[0] // 2, x)


def turn_early(own_x, got_x, late_x, own_y, got_y, late_y, after):
    rows, width = own_x.shape
    parts = []
    for own, got, late in ((own_x, got_x, late_x), (own_y, got_y, late_y)):
        for part in (own, got[0], late[2], got[1]):
            parts.append((part, whole((rows, width), (part.shape[0] // rows - 1, 0))))
    return once(turn_early_kernel, "turn_early", parts, [((4 * width, WIDE), BF16)], (), after)[0]


def turn_late(parts, axis, after=()):
    rows, width = parts[0].shape

    def kernel(*refs):
        x, y, _, _, _ = spot()
        turn_into(refs[:SIDE], refs[-1], 0, y if axis == "x" else x)

    ins = [(part, whole((rows, width))) for part in parts]
    return once(kernel, "turn_late", ins, [((2 * width, WIDE), BF16)], (), after)[0]


def project_kernel(mine, other, weight, gating, response, *refs):
    _, _, _, half, core = spot()
    part = mine.shape[0]
    rows = refs[-1]
    conv_grad, grad_gate = refs[-3:-1]

    @pl.when(pl.program_id(0) == 0)
    def _():
        rows[aligned(core, part), :] = mine[...]
        rows[aligned(1 - core, part), :] = other[...]

    late = len(refs) > 3
    tokens = aligned(1 - half if late else half, TAPS)
    made = jnp.dot(rows[...], weight[...], preferred_element_type=F32)
    made_conv = (made * gating[tokens, :].astype(F32)).astype(BF16)
    made_gate = (made * response[tokens, :]).astype(BF16)
    if late:
        conv_grad[tokens, :] = made_conv
        grad_gate[tokens, :] = made_gate
        conv_grad[aligned(half, TAPS), :] = refs[0][...]
        grad_gate[aligned(half, TAPS), :] = refs[1][...]
    else:
        conv_grad[...] = made_conv
        grad_gate[...] = made_gate


def project(mine, other, weight, gating, response, done=(), after=()):
    length, channels = gating.shape
    depth = weight.shape[0]
    made = length if done else 2 * mine.shape[0]

    def body(*refs):
        kept = 5 + len(done)
        project_kernel(*refs[:kept], *refs[kept + len(after) :])

    return pl.pallas_call(
        body,
        grid=(channels // WIDE,),
        in_specs=[full(mine.shape)] * 2
        + [tile(depth, WIDE), tile(length, WIDE), tile(length, WIDE)]
        + [tile(TAPS, WIDE)] * len(done)
        + [ANYWHERE] * len(after),
        out_specs=[tile(made, WIDE)] * 2,
        out_shape=[jax.ShapeDtypeStruct((made, channels), BF16)] * 2,
        scratch_shapes=[pltpu.VMEM((2 * mine.shape[0], depth), BF16)],
        compiler_params=room(16),
        cost_estimate=lasting(5 if done else 0),
        name="project_late" if done else "project_early",
    )(mine, other, weight, gating, response, *done, *after)


def weight_kernel(early, early_other, late, late_other, gated, first, third, before, after, *outs):
    _, _, _, half, core = spot()
    part = WIDE // SIDE
    tokens = []
    for h, c in ((half, core), (half, 1 - core), (1 - half, core), (1 - half, 1 - core)):
        rows, own_rows = aligned(2 * h + c, part), aligned(c, part)
        upper = jnp.broadcast_to(h, (part, gated.shape[1])) == 0
        opposite = jnp.where(
            upper, before[own_rows, :].astype(F32), after[own_rows, :].astype(F32)
        ).astype(BF16)
        tokens += [gated[rows, :], first[rows, :], opposite, third[rows, :]]
    tokens = jnp.concatenate(tokens, 0)
    for s, out in enumerate(outs):
        rows = slice(s * WIDE, (s + 1) * WIDE)
        features = jnp.concatenate([ref[rows] for ref in (early, early_other, late, late_other)], 1)
        out[...] = jnp.dot(features, tokens, preferred_element_type=F32).astype(out.dtype)


def weight_part(which, early, early_other, turned, turned_other, gated, got, late, after=()):
    length = gated.shape[0]
    features = turned.shape[0]
    width = got[0].shape[1]
    spec = whole((features, WIDE), (which, 0))
    below = whole((TAPS, width), (1, 0))
    return once(
        weight_kernel,
        "weight_part",
        [
            (early, spec),
            (early_other, spec),
            turned,
            turned_other,
            (gated, whole((length, width), (0, which))),
            *[(one, whole((length, width))) for one in got],
            (late[1], below),
            (late[3], below),
        ],
        [((features // SIDE, width), F32 if s == 0 else BF16) for s in range(SIDE)],
        (),
        after,
        3,
    )


def first_sum_kernel(*refs):
    _, _, z, _, _ = spot()
    outs, kept = refs[2 * SIDE : 3 * SIDE], refs[3 * SIDE]
    width = refs[0].shape[1]
    run = kept.shape[0] // SIDE
    for which in range(2):
        parts = refs[which * SIDE : (which + 1) * SIDE]
        total = parts[0][...]
        for ref in parts[1:]:
            total = total + ref[...].astype(F32)
        for d in range(SIDE):
            rows = aligned((d - z + SIDE) % SIDE, run)
            kept[rows, which * width : (which + 1) * width] = total[d * run : (d + 1) * run]
    for s, out in enumerate(outs):
        out[...] = kept[s * run : (s + 1) * run, :].astype(out.dtype)


def first_sum(parts_x, parts_y, after=()):
    rows, width = parts_x[0].shape
    return once(
        first_sum_kernel,
        "first_sum",
        [*parts_x, *parts_y],
        [((rows // SIDE, 2 * width), F32 if s == 0 else BF16) for s in range(SIDE)],
        [pltpu.VMEM((rows, 2 * width), F32)],
        after,
        1,
    )


def last_sum(parts, scale):
    def kernel(*refs):
        out = refs[-1]
        total = refs[0][...]
        for ref in refs[1:SIDE]:
            total = total + ref[...].astype(F32)
        out[...] = total * scale

    return once(kernel, "last_sum", parts, [(parts[0].shape, F32)])[0]


def tied(x, *after):
    return lax.optimization_barrier((x, *after))[0]


def partnered(x, axis, by):
    if axis == "z":
        return lax.ppermute(x, "dp", [(i, i ^ by) for i in range(SIDE)])
    step = by * (SIDE if axis == "x" else 1)
    return lax.ppermute(x, "ctx", [(i, i ^ step) for i in range(SIDE * SIDE)])


def paired(x, axis, by, before=()):
    return x + partnered(tied(x, *before), axis, by)


def exchanged(parts, axis):
    return [parts[0]] + [moved(parts[s], axis, s) for s in range(1, SIDE)]


def local(conv_input, gate_value, out_grad, out_weight, filters):
    signal, gating, grads = conv_input[0], gate_value[0], out_grad[0]
    length, channels = signal.shape
    halo_sent = signal[length - TAPS :]
    signal, gating, filters, weight = (
        resident(x) for x in (signal, gating, filters, out_weight)
    )
    tokens_all = lax.axis_size("dp") * lax.axis_size("ctx") * length

    late = moved(grads, "half", 1)
    previous = shifted(halo_sent, 1)
    early_other = moved(grads, "core", 1)
    grads = resident(grads)
    early_x, early_y = pack(grads, (early_other,))
    response, gated, sends_x, sends_y = forward(
        filters, previous, signal, gating, [early_x[1], early_x[3], early_y[1], early_y[3]]
    )
    got_x = [moved(sends_x[0], "x", 1), moved(sends_x[1], "x", 3)]
    got_y = [moved(sends_y[0], "y", 1), moved(sends_y[1], "y", 3)]
    conv_early, gate_early = project(grads, early_other, weight, gating, response)

    late_other = moved(tied(late, conv_early, *got_x, *got_y), "core", 1)
    late_x, late_y = relay(late, got_x, got_y, early_x[2], early_y[2], (late_other,))
    conv_grad, grad_gate = project(
        late,
        late_other,
        weight,
        gating,
        response,
        (conv_early, gate_early),
        (late_x[0],),
    )
    late_x, late_y = exchanged(late_x, "x"), exchanged(late_y, "y")
    early = turn_early(
        early_x[0], got_x, late_x, early_y[0], got_y, late_y, (conv_grad, *late_x[1:], *late_y[1:])
    )
    early_swap = moved(early, "core", 1)
    turned_x = turn_late(late_x, "x", (early,))
    swap_x = moved(turned_x, "core", 1)
    turned_y = turn_late(late_y, "y", (turned_x,))
    swap_y = moved(turned_y, "core", 1)
    following = shifted(conv_grad[:TAPS], -1)
    filter_local = filter_grad(previous, signal, conv_grad, (turned_y,))
    parts_x = weight_part(
        0, early, early_swap, turned_x, swap_x, gated, got_x, late_x, (filter_local,)
    )
    filter_sum = paired(filter_local, "x", 1, (parts_x[0],))
    parts_y = weight_part(
        1, early, early_swap, turned_y, swap_y, gated, got_y, late_y, (parts_x[0], filter_sum)
    )
    filter_sum = paired(filter_sum, "x", 2, (parts_y[0],))
    parts_x, parts_y = exchanged(parts_x, "y"), exchanged(parts_y, "x")
    filter_sum = paired(paired(filter_sum, "y", 1, parts_x[1:]), "y", 2)
    sums = first_sum(parts_x, parts_y, (filter_sum,))
    grad_input = input_grad(filters, conv_grad, following, (sums[0],))
    sums = exchanged(sums, "z")
    filter_parts = exchanged([tied(filter_sum, sums[1])] * SIDE, "z")
    filter_total = (filter_parts[0] + filter_parts[2]) + (filter_parts[1] + filter_parts[3])
    grad_weight = last_sum(sums, 1.0 / math.sqrt(tokens_all))
    grad_filter = filter_total * (1.0 / math.sqrt(tokens_all * GROUP))
    return (grad_input[None], grad_gate[None], grad_weight, grad_filter)


def solution(mesh):
    placed = (
        P("dp", "ctx", "tp"),
        P("dp", "ctx", "tp"),
        P("dp", ("ctx", "tp"), None),
        P(None, "tp"),
        P("tp", None),
    )
    return jax.shard_map(
        local,
        mesh=mesh,
        in_specs=placed,
        out_specs=(
            P("dp", "ctx", "tp"),
            P("dp", "ctx", "tp"),
            P(("dp", "ctx"), "tp"),
            P("tp", None),
        ),
        check_vma=False,
    )
```

```python
import math

import jax
import jax.numpy as jnp
from jax import lax
from jax.experimental import pallas as pl
from jax.experimental.pallas import tpu as pltpu
from jax.sharding import PartitionSpec as P

F32 = jnp.float32
BF16 = jnp.bfloat16
SIDE = 4
TAPS = 128
GROUP = 16
LANES = 128
PER_TILE = LANES // GROUP
WIDE = 256


def room(mebibytes):
    return pltpu.CompilerParams(vmem_limit_bytes=mebibytes * 1024 * 1024)


def spot():
    ctx = lax.axis_index("ctx")
    tp = lax.axis_index("tp")
    return ctx // SIDE, ctx % SIDE, lax.axis_index("dp"), tp // 2, tp % 2


def moved(x, axis, by):
    if axis == "x":
        pairs = [(i, (i // SIDE + by) % SIDE * SIDE + i % SIDE) for i in range(SIDE * SIDE)]
        return lax.ppermute(x, "ctx", pairs)
    if axis == "y":
        pairs = [(i, i // SIDE * SIDE + (i % SIDE + by) % SIDE) for i in range(SIDE * SIDE)]
        return lax.ppermute(x, "ctx", pairs)
    if axis == "z":
        return lax.ppermute(x, "dp", [(i, (i + by) % SIDE) for i in range(SIDE)])
    if axis == "half":
        return lax.ppermute(x, "tp", [(i, (i + 2) % 4) for i in range(4)])
    return lax.ppermute(x, "tp", [(i, i // 2 * 2 + (i + 1) % 2) for i in range(4)])


def shifted(x, by):
    devices = lax.axis_size("ctx")
    return lax.ppermute(x, "ctx", [(i, i + by) for i in range(devices) if 0 <= i + by < devices])


ANYWHERE = pl.BlockSpec(memory_space=pl.ANY)
HALF = LANES // 2


def resident(x):
    return pltpu.with_memory_space_constraint(x, pltpu.HBM)


def whole(shape, place=None):
    place = place or (0,) * len(shape)
    return pl.BlockSpec(tuple(shape), lambda i: place, pipeline_mode=pl.Buffered(1))


def full(shape):
    return pl.BlockSpec(tuple(shape), lambda i: (0,) * len(shape))


def tile(rows, width):
    return pl.BlockSpec((rows, width), lambda i: (0, i))


def iota(shape, dim):
    return lax.broadcasted_iota(jnp.int32, shape, dim)


def aligned(index, size):
    return pl.ds(pl.multiple_of(index * size, size), size)


def lasting(microseconds):
    return pl.CostEstimate(flops=int(microseconds * 1e9), bytes_accessed=0, transcendentals=0)


def once(kernel, name, ins, outs, scratch=(), after=(), lasts=0):
    def body(*refs):
        kernel(*refs[: len(ins)], *refs[len(ins) + len(after) :])

    specs = [i[1] if isinstance(i, tuple) else whole(i.shape) for i in ins]
    arrays = [i[0] if isinstance(i, tuple) else i for i in ins]
    return pl.pallas_call(
        body,
        grid=(1,),
        in_specs=specs + [ANYWHERE] * len(after),
        out_specs=[whole(shape) for shape, _ in outs],
        out_shape=[jax.ShapeDtypeStruct(shape, dtype) for shape, dtype in outs],
        scratch_shapes=list(scratch),
        compiler_params=room(12),
        cost_estimate=lasting(lasts),
        name=name,
    )(*arrays, *after)


def first_rows(filters, shifted_by):
    lane, tap = iota((TAPS, 2 * TAPS), 1), iota((TAPS, 2 * TAPS), 0)
    place = lane == (TAPS - tap if shifted_by else tap)
    return jnp.dot(filters, place.astype(F32).astype(BF16), preferred_element_type=F32)


def banded(rows, stack):
    for g in range(PER_TILE):
        first = jnp.broadcast_to(rows[g : g + 1], (TAPS, 2 * TAPS))
        skewed = pltpu.roll(first, 0, 1, stride=1, stride_axis=0)
        stack[g * TAPS : (g + 1) * TAPS, :] = skewed.astype(BF16)


def lane_group(shape):
    return iota(shape, len(shape) - 1) % LANES // GROUP


def own_lanes(stacked):
    group = lane_group((TAPS, 2 * LANES))
    chosen = jnp.zeros((TAPS, 2 * LANES), F32)
    for g in range(PER_TILE):
        chosen = jnp.where(group == g, stacked[g * TAPS : (g + 1) * TAPS], chosen)
    return chosen


def two_windows(first, second, third):
    upper = jnp.concatenate([first, second], 1)
    lower = jnp.concatenate([second, third], 1)
    return jnp.concatenate([upper, lower], 0)


def forward_kernel(filters, previous, signal, gating, *refs):
    shifts = 2
    early, (response, gated), sends = refs[: 2 * shifts], refs[2 * shifts : 2 * shifts + 2], refs[2 * shifts + 2 : -1]
    stack = refs[-1]
    rows = first_rows(filters[...], True)
    count = signal.shape[1] // LANES
    for i in range(count):
        columns = slice(i * LANES, (i + 1) * LANES)
        which, place = divmod(i, count // 2)
        to = slice(place * LANES, (place + 1) * LANES)
        band = stack.at[i % 2]
        banded(rows[i * PER_TILE : (i + 1) * PER_TILE], band)
        window = two_windows(previous[:, columns], signal[:TAPS, columns], signal[TAPS:, columns])
        made = own_lanes(jnp.dot(band[...], window, preferred_element_type=F32))
        for block in range(2):
            tokens = slice(block * TAPS, (block + 1) * TAPS)
            part = made[:, block * LANES : (block + 1) * LANES]
            response[tokens, columns] = part
            product = (part * gating[tokens, columns].astype(F32)).astype(BF16)
            gated[tokens, columns] = product
            for send in sends[which * shifts : (which + 1) * shifts]:
                send[tokens, to] = product
    for ref, send in zip(early, sends):
        send[2 * TAPS :] = ref[...]


def forward(filters, previous, signal, gating, early):
    length, channels = signal.shape
    rows, width = early[0].shape
    response, gated, *sends = once(
        forward_kernel,
        "conv_forward",
        [filters, previous, signal, gating, *early],
        [((length, channels), F32), ((length, channels), BF16)]
        + [((length + rows, width), BF16)] * len(early),
        [pltpu.VMEM((2, PER_TILE * TAPS, 2 * TAPS), BF16)],
    )
    return response, gated, sends[:2], sends[2:]


def input_grad_kernel(filters, conv_grad, following, grad_input, stack):
    rows = first_rows(filters[...], False)
    for i in range(conv_grad.shape[1] // LANES):
        columns = slice(i * LANES, (i + 1) * LANES)
        band = stack.at[i % 2]
        banded(rows[i * PER_TILE : (i + 1) * PER_TILE], band)
        window = two_windows(
            conv_grad[:TAPS, columns], conv_grad[TAPS:, columns], following[:, columns]
        )
        made = own_lanes(jnp.dot(band[...], window, preferred_element_type=F32))
        for block in range(2):
            grad_input[block * TAPS : (block + 1) * TAPS, columns] = made[
                :, block * LANES : (block + 1) * LANES
            ].astype(BF16)


def input_grad(filters, conv_grad, following, after):
    return once(
        input_grad_kernel,
        "input_grad",
        [filters, conv_grad, following],
        [(conv_grad.shape, BF16)],
        [pltpu.VMEM((2, PER_TILE * TAPS, 2 * TAPS), BF16)],
        after,
    )[0]


def filter_grad_kernel(previous, signal, conv_grad, grad_filter, stack):
    square = (2 * TAPS, 2 * TAPS)
    turn = iota(square, 0) == (2 * TAPS - iota(square, 1)) % (2 * TAPS)
    turn = turn.astype(F32).astype(BF16)
    group = lane_group((TAPS, 2 * LANES))
    for i in range(signal.shape[1] // LANES):
        columns = slice(i * LANES, (i + 1) * LANES)
        masked = stack.at[i % 2]
        inputs = two_windows(previous[:, columns], signal[:TAPS, columns], signal[TAPS:, columns])
        turned = jnp.dot(turn, inputs, preferred_element_type=F32).astype(BF16)
        both = jnp.concatenate([conv_grad[:TAPS, columns], conv_grad[TAPS:, columns]], 1)
        both = both.astype(F32)
        for g in range(PER_TILE):
            masked[g * TAPS : (g + 1) * TAPS, :] = jnp.where(group == g, both, 0.0).astype(BF16)
        products = lax.dot_general(
            masked[...], turned, (((1,), (1,)), ((), ())), preferred_element_type=F32
        )
        for g in range(PER_TILE):
            skewed = pltpu.roll(products[g * TAPS : (g + 1) * TAPS], 0, 1, stride=1, stride_axis=0)
            row = i * PER_TILE + g
            grad_filter[row : row + 1, :] = jnp.sum(skewed[:, TAPS:], axis=0, keepdims=True)


def filter_grad(previous, signal, conv_grad, after):
    return once(
        filter_grad_kernel,
        "filter_grad",
        [previous, signal, conv_grad],
        [((signal.shape[1] // GROUP, TAPS), F32)],
        [pltpu.VMEM((2, PER_TILE * TAPS, 2 * TAPS), BF16)],
        after,
        4,
    )[0]


def pack_kernel(mine, *outs):
    x, y, _, _, _ = spot()
    part = mine.shape[0]
    depth = mine.shape[1] // SIDE
    lower = iota((part, LANES), 1) < HALF
    for s in range(SIDE):
        to_x, to_y = (x + s) % SIDE, (y + s) % SIDE
        upper_half = jnp.broadcast_to(to_y % 2, (part, LANES)) == 1
        for d in range(SIDE):
            rows = slice(d // 2 * part, (d // 2 + 1) * part)
            column = d % 2 * WIDE
            start = pl.multiple_of(d * depth + to_x * WIDE, WIDE)
            outs[s][rows, column : column + WIDE] = mine[:, pl.ds(start, WIDE)]
            for pair in range(SIDE // 2):
                runs = []
                for i in range(2):
                    start = d * depth + (2 * pair + i) * WIDE + to_y // 2 * LANES
                    runs.append(mine[:, pl.ds(pl.multiple_of(start, LANES), LANES)].astype(F32))
                first = jnp.where(upper_half, pltpu.roll(runs[0], HALF, 1), runs[0])
                second = jnp.where(upper_half, runs[1], pltpu.roll(runs[1], HALF, 1))
                both = jnp.where(lower, first, second).astype(BF16)
                at = column + pair * LANES
                outs[SIDE + s][rows, at : at + LANES] = both


def pack(mine, after=()):
    part, width = mine.shape
    outs = once(
        pack_kernel, "pack", [mine], [((2 * part, width // (2 * SIDE)), BF16)] * (2 * SIDE), (), after
    )
    return outs[:SIDE], outs[SIDE:]


def relay_kernel(count, mine, *refs):
    before_x, after_x, before_y, after_y, opposite_x, opposite_y = refs[:6]
    outs = refs[6 + count :]
    part = opposite_x.shape[0]
    pack_kernel(mine, *(out.at[:part] for out in outs))
    for first, before, opposite, after in (
        (0, before_x, opposite_x, after_x),
        (SIDE, before_y, opposite_y, after_y),
    ):
        outs[first + 1][part:] = before[:TAPS]
        outs[first + 2][part:] = opposite[...]
        outs[first + 3][part:] = after[TAPS : 2 * TAPS]


def relay(mine, got_x, got_y, opposite_x, opposite_y, after):
    rows, width = opposite_x.shape
    got = [
        (part, whole((2 * TAPS, width))) for part in (got_x[0], got_x[1], got_y[0], got_y[1])
    ]
    shapes = ([(rows, width)] + [(rows + TAPS, width)] * (SIDE - 1)) * 2

    def kernel(*refs):
        relay_kernel(0, *refs)

    outs = once(
        kernel, "relay", [mine, *got, opposite_x, opposite_y], [(shape, BF16) for shape in shapes], (), after
    )
    return outs[:SIDE], outs[SIDE:]


def turn_into(parts, out, base, me):
    part = parts[0].shape[0] // 2
    for fold in range(2):
        for pair in range(SIDE // 2):
            block = jnp.concatenate(
                [ref[fold * part : (fold + 1) * part] for ref in parts[2 * pair : 2 * pair + 2]], 0
            )
            transposed = block.T
            for d in range(2):
                for q in range(SIDE):
                    to = (q - me + SIDE) % SIDE
                    rows = pl.ds(pl.multiple_of(base + to * WIDE + (2 * fold + d) * HALF, HALF), HALF)
                    start = d * WIDE + q * HALF
                    out[rows, pair * LANES : (pair + 1) * LANES] = transposed[start : start + HALF]


def turn_early_kernel(*refs):
    x, y, _, _, _ = spot()
    out = refs[-1]
    turn_into(refs[:SIDE], out, 0, y)
    turn_into(refs[SIDE : 2 * SIDE], out, out.shape[0] // 2, x)


def turn_early(own_x, got_x, late_x, own_y, got_y, late_y, after):
    rows, width = own_x.shape
    parts = []
    for own, got, late in ((own_x, got_x, late_x), (own_y, got_y, late_y)):
        for part in (own, got[0], late[2], got[1]):
            parts.append((part, whole((rows, width), (part.shape[0] // rows - 1, 0))))
    return once(turn_early_kernel, "turn_early", parts, [((4 * width, WIDE), BF16)], (), after)[0]


def turn_late(parts, axis, after=()):
    rows, width = parts[0].shape

    def kernel(*refs):
        x, y, _, _, _ = spot()
        turn_into(refs[:SIDE], refs[-1], 0, y if axis == "x" else x)

    ins = [(part, whole((rows, width))) for part in parts]
    return once(kernel, "turn_late", ins, [((2 * width, WIDE), BF16)], (), after)[0]


def project_kernel(mine, other, weight, gating, response, *refs):
    _, _, _, half, core = spot()
    part = mine.shape[0]
    rows = refs[-1]
    conv_grad, grad_gate = refs[-3:-1]

    @pl.when(pl.program_id(0) == 0)
    def _():
        rows[aligned(core, part), :] = mine[...]
        rows[aligned(1 - core, part), :] = other[...]

    late = len(refs) > 3
    tokens = aligned(1 - half if late else half, TAPS)
    made = jnp.dot(rows[...], weight[...], preferred_element_type=F32)
    made_conv = (made * gating[tokens, :].astype(F32)).astype(BF16)
    made_gate = (made * response[tokens, :]).astype(BF16)
    if late:
        conv_grad[tokens, :] = made_conv
        grad_gate[tokens, :] = made_gate
        conv_grad[aligned(half, TAPS), :] = refs[0][...]
        grad_gate[aligned(half, TAPS), :] = refs[1][...]
    else:
        conv_grad[...] = made_conv
        grad_gate[...] = made_gate


def project(mine, other, weight, gating, response, done=(), after=()):
    length, channels = gating.shape
    depth = weight.shape[0]
    made = length if done else 2 * mine.shape[0]

    def body(*refs):
        kept = 5 + len(done)
        project_kernel(*refs[:kept], *refs[kept + len(after) :])

    return pl.pallas_call(
        body,
        grid=(channels // WIDE,),
        in_specs=[full(mine.shape)] * 2
        + [tile(depth, WIDE), tile(length, WIDE), tile(length, WIDE)]
        + [tile(TAPS, WIDE)] * len(done)
        + [ANYWHERE] * len(after),
        out_specs=[tile(made, WIDE)] * 2,
        out_shape=[jax.ShapeDtypeStruct((made, channels), BF16)] * 2,
        scratch_shapes=[pltpu.VMEM((2 * mine.shape[0], depth), BF16)],
        compiler_params=room(16),
        cost_estimate=lasting(5 if done else 0),
        name="project_late" if done else "project_early",
    )(mine, other, weight, gating, response, *done, *after)


def high_and_low(x):
    high = x.astype(BF16).astype(F32)
    return high, (x - high).astype(BF16).astype(F32)


def folded(x, rows):
    return jnp.concatenate([x[i : i + rows] for i in range(0, x.shape[0], rows)], 1)


def unfolded(x):
    return jnp.concatenate([x[:, i : i + LANES] for i in range(0, x.shape[1], LANES)], 0)


def riding(ref, start, rows):
    pair = ref[start : start + 2 * rows].astype(F32)
    return unfolded(pair[:rows] + pair[rows:])


def four_sum(parts):
    return (parts[0] + parts[2]) + (parts[1] + parts[3])


def weight_kernel(early, early_other, late, late_other, gated, first, third, before, after, *refs):
    extra, outs = refs[:-SIDE], refs[-SIDE:]
    _, _, _, half, core = spot()
    part = WIDE // SIDE
    tokens = []
    for h, c in ((half, core), (half, 1 - core), (1 - half, core), (1 - half, 1 - core)):
        rows, own_rows = aligned(2 * h + c, part), aligned(c, part)
        upper = jnp.broadcast_to(h, (part, gated.shape[1])) == 0
        opposite = jnp.where(
            upper, before[own_rows, :].astype(F32), after[own_rows, :].astype(F32)
        ).astype(BF16)
        tokens += [gated[rows, :], first[rows, :], opposite, third[rows, :]]
    tokens = jnp.concatenate(tokens, 0)
    for s, out in enumerate(outs):
        rows = slice(s * WIDE, (s + 1) * WIDE)
        features = jnp.concatenate([ref[rows] for ref in (early, early_other, late, late_other)], 1)
        out[:WIDE] = jnp.dot(features, tokens, preferred_element_type=F32).astype(out.dtype)
    if extra:
        rows = LANES * extra[0].shape[0] // gated.shape[1]
        pair = jnp.concatenate([folded(part, rows) for part in high_and_low(extra[0][...])], 0)
        for out in outs[1:]:
            out[WIDE:] = pair.astype(BF16)


def weight_part(
    which, early, early_other, turned, turned_other, gated, got, late, extra=(), after=()
):
    length = gated.shape[0]
    features = turned.shape[0]
    width = got[0].shape[1]
    spec = whole((features, WIDE), (which, 0))
    below = whole((TAPS, width), (1, 0))
    return once(
        weight_kernel,
        "weight_part",
        [
            (early, spec),
            (early_other, spec),
            turned,
            turned_other,
            (gated, whole((length, width), (0, which))),
            *[(one, whole((length, width))) for one in got],
            (late[1], below),
            (late[3], below),
            *extra,
        ],
        [((features // SIDE, width), F32)]
        + [((features // SIDE + sum(2 * x.size // width for x in extra), width), BF16)] * (SIDE - 1),
        (),
        after,
        3,
    )


def filter_sum_y(own, parts):
    below = parts[0].shape[0] - WIDE
    rows = below // 2

    def kernel(*refs):
        values = [sum(high_and_low(refs[0][...]))]
        values += [riding(ref, 0, rows) for ref in refs[1:-1]]
        refs[-1][...] = four_sum(values)

    tails = [(part, whole((below, part.shape[1]), (WIDE // below, 0))) for part in parts]
    return once(kernel, "filter_sum_y", [own, *tails], [(own.shape, F32)])[0]


def first_sum_kernel(*refs):
    _, _, z, _, _ = spot()
    extra, outs, own_extra, kept = refs[2 * SIDE], refs[2 * SIDE + 1 : -2], refs[-2], refs[-1]
    width = refs[0].shape[1]
    run = kept.shape[0] // SIDE
    for which in range(2):
        parts = refs[which * SIDE : (which + 1) * SIDE]
        total = parts[0][...]
        for ref in parts[1:]:
            total = total + ref[...].astype(F32)
        for d in range(SIDE):
            rows = aligned((d - z + SIDE) % SIDE, run)
            kept[rows, which * width : (which + 1) * width] = total[d * run : (d + 1) * run]
    high, low = (folded(part, own_extra.shape[0]) for part in high_and_low(extra[...]))
    own_extra[...] = high + low
    for s, out in enumerate(outs):
        out[:run] = kept[s * run : (s + 1) * run, :].astype(out.dtype)
        if s:
            out[run:] = jnp.concatenate([high, low], 0).astype(BF16)


def first_sum(parts_x, parts_y, extra):
    rows, width = parts_x[0].shape
    below = LANES * extra.shape[0] // (2 * width)
    run = rows // SIDE
    *sums, own_extra = once(
        first_sum_kernel,
        "first_sum",
        [*[(part, whole((rows, width))) for part in (*parts_x, *parts_y)], extra],
        [((run, 2 * width), F32)]
        + [((run + 2 * below, 2 * width), BF16)] * (SIDE - 1)
        + [((below, 2 * width), F32)],
        [pltpu.VMEM((rows, 2 * width), F32)],
        (),
        1,
    )
    return sums, own_extra


def last_sum(parts, own_extra, filters, scale, filter_scale):
    rows = parts[0].shape[0]
    below = own_extra.shape[0]

    def kernel(*refs):
        own, others, extra, out, filter_out = refs[0], refs[1:SIDE], refs[SIDE], refs[-2], refs[-1]
        total = own[...]
        for ref in others:
            total = total + ref[:rows].astype(F32)
        out[...] = total * scale
        values = [unfolded(extra[...])] + [riding(ref, rows, below) for ref in others]
        filter_out[...] = four_sum(values) * filter_scale

    return once(
        kernel, "last_sum", [*parts, own_extra], [(parts[0].shape, F32), (filters.shape, F32)]
    )


def tied(x, *after):
    return lax.optimization_barrier((x, *after))[0]


def partnered(x, axis, by):
    if axis == "z":
        return lax.ppermute(x, "dp", [(i, i ^ by) for i in range(SIDE)])
    step = by * (SIDE if axis == "x" else 1)
    return lax.ppermute(x, "ctx", [(i, i ^ step) for i in range(SIDE * SIDE)])


def paired(x, axis, by, before=()):
    return x + partnered(tied(x, *before), axis, by)


def exchanged(parts, axis):
    return [parts[0]] + [moved(parts[s], axis, s) for s in range(1, SIDE)]


def local(conv_input, gate_value, out_grad, out_weight, filters):
    signal, gating, grads = conv_input[0], gate_value[0], out_grad[0]
    length, channels = signal.shape
    halo_sent = signal[length - TAPS :]
    signal, gating, filters, weight = (
        resident(x) for x in (signal, gating, filters, out_weight)
    )
    tokens_all = lax.axis_size("dp") * lax.axis_size("ctx") * length

    late = moved(grads, "half", 1)
    previous = shifted(halo_sent, 1)
    early_other = moved(grads, "core", 1)
    grads = resident(grads)
    early_x, early_y = pack(grads, (early_other,))
    response, gated, sends_x, sends_y = forward(
        filters, previous, signal, gating, [early_x[1], early_x[3], early_y[1], early_y[3]]
    )
    got_x = [moved(sends_x[0], "x", 1), moved(sends_x[1], "x", 3)]
    got_y = [moved(sends_y[0], "y", 1), moved(sends_y[1], "y", 3)]
    conv_early, gate_early = project(grads, early_other, weight, gating, response)

    late_other = moved(tied(late, conv_early, *got_x, *got_y), "core", 1)
    late_x, late_y = relay(late, got_x, got_y, early_x[2], early_y[2], (late_other,))
    conv_grad, grad_gate = project(
        late,
        late_other,
        weight,
        gating,
        response,
        (conv_early, gate_early),
        (late_x[0],),
    )
    late_x, late_y = exchanged(late_x, "x"), exchanged(late_y, "y")
    early = turn_early(
        early_x[0], got_x, late_x, early_y[0], got_y, late_y, (conv_grad, *late_x[1:], *late_y[1:])
    )
    early_swap = moved(early, "core", 1)
    turned_x = turn_late(late_x, "x", (early,))
    swap_x = moved(turned_x, "core", 1)
    turned_y = turn_late(late_y, "y", (turned_x,))
    swap_y = moved(turned_y, "core", 1)
    following = shifted(conv_grad[:TAPS], -1)
    filter_local = filter_grad(previous, signal, conv_grad, (turned_y,))
    parts_x = weight_part(
        0, early, early_swap, turned_x, swap_x, gated, got_x, late_x, (filter_local,)
    )
    parts_y = weight_part(
        1, early, early_swap, turned_y, swap_y, gated, got_y, late_y, (), (parts_x[0],)
    )
    parts_x, parts_y = exchanged(parts_x, "y"), exchanged(parts_y, "x")
    filter_sum = filter_sum_y(filter_local, parts_x[1:])
    filter_sum = paired(paired(filter_sum, "x", 1), "x", 2)
    sums, own_filter = first_sum(parts_x, parts_y, filter_sum)
    grad_input = input_grad(filters, conv_grad, following, (sums[0],))
    grad_weight, grad_filter = last_sum(
        exchanged(sums, "z"),
        own_filter,
        filters,
        1.0 / math.sqrt(tokens_all),
        1.0 / math.sqrt(tokens_all * GROUP),
    )
    return (grad_input[None], grad_gate[None], grad_weight, grad_filter)


def solution(mesh):
    placed = (
        P("dp", "ctx", "tp"),
        P("dp", "ctx", "tp"),
        P("dp", ("ctx", "tp"), None),
        P(None, "tp"),
        P("tp", None),
    )
    return jax.shard_map(
        local,
        mesh=mesh,
        in_specs=placed,
        out_specs=(
            P("dp", "ctx", "tp"),
            P("dp", "ctx", "tp"),
            P(("dp", "ctx"), "tp"),
            P("tp", None),
        ),
        check_vma=False,
    )
```

```python
import math

import jax
import jax.numpy as jnp
from jax import lax
from jax.experimental import pallas as pl
from jax.experimental.pallas import tpu as pltpu
from jax.sharding import PartitionSpec as P

F32 = jnp.float32
BF16 = jnp.bfloat16
SIDE = 4
TAPS = 128
GROUP = 16
LANES = 128
PER_TILE = LANES // GROUP
WIDE = 256


def room(mebibytes):
    return pltpu.CompilerParams(vmem_limit_bytes=mebibytes * 1024 * 1024)


def spot():
    ctx = lax.axis_index("ctx")
    tp = lax.axis_index("tp")
    return ctx // SIDE, ctx % SIDE, lax.axis_index("dp"), tp // 2, tp % 2


def moved(x, axis):
    step = 2 if axis == "half" else 1
    return lax.ppermute(x, "tp", [(i, i ^ step) for i in range(4)])


def in_plane(x, gather, target):
    pairs = []
    for i in range(SIDE * SIDE):
        for j in range(4):
            place_x, place_y = divmod(i, SIDE)
            if (j % 2 == 0) == gather:
                place_x = target(place_x)
            else:
                place_y = target(place_y)
            pairs.append((i * 4 + j, (place_x * SIDE + place_y) * 4 + j))
    return lax.ppermute(x, ("ctx", "tp"), pairs)


def stepped(x, gather, by):
    return in_plane(x, gather, lambda place: (place + by) % SIDE)


def shifted(x, by):
    devices = lax.axis_size("ctx")
    return lax.ppermute(x, "ctx", [(i, i + by) for i in range(devices) if 0 <= i + by < devices])


ANYWHERE = pl.BlockSpec(memory_space=pl.ANY)
HALF = LANES // 2


def resident(x):
    return pltpu.with_memory_space_constraint(x, pltpu.HBM)


def whole(shape, place=None):
    place = place or (0,) * len(shape)
    return pl.BlockSpec(tuple(shape), lambda i: place, pipeline_mode=pl.Buffered(1))


def full(shape):
    return pl.BlockSpec(tuple(shape), lambda i: (0,) * len(shape))


def tile(rows, width):
    return pl.BlockSpec((rows, width), lambda i: (0, i))


def iota(shape, dim):
    return lax.broadcasted_iota(jnp.int32, shape, dim)


def aligned(index, size):
    return pl.ds(pl.multiple_of(index * size, size), size)


def lasting(microseconds):
    return pl.CostEstimate(flops=int(microseconds * 1e9), bytes_accessed=0, transcendentals=0)


def once(kernel, name, ins, outs, scratch=(), after=(), lasts=0):
    def body(*refs):
        kernel(*refs[: len(ins)], *refs[len(ins) + len(after) :])

    specs = [i[1] if isinstance(i, tuple) else whole(i.shape) for i in ins]
    arrays = [i[0] if isinstance(i, tuple) else i for i in ins]
    return pl.pallas_call(
        body,
        grid=(1,),
        in_specs=specs + [ANYWHERE] * len(after),
        out_specs=[whole(shape) for shape, _ in outs],
        out_shape=[jax.ShapeDtypeStruct(shape, dtype) for shape, dtype in outs],
        scratch_shapes=list(scratch),
        compiler_params=room(20),
        cost_estimate=lasting(lasts),
        name=name,
    )(*arrays, *after)


def first_rows(filters, shifted_by):
    lane, tap = iota((TAPS, 2 * TAPS), 1), iota((TAPS, 2 * TAPS), 0)
    place = lane == (TAPS - tap if shifted_by else tap)
    return jnp.dot(filters, place.astype(F32).astype(BF16), preferred_element_type=F32)


def banded(rows, stack):
    for g in range(PER_TILE):
        first = jnp.broadcast_to(rows[g : g + 1], (TAPS, 2 * TAPS))
        skewed = pltpu.roll(first, 0, 1, stride=1, stride_axis=0)
        stack[g * TAPS : (g + 1) * TAPS, :] = skewed.astype(BF16)


def lane_group(shape):
    return iota(shape, len(shape) - 1) % LANES // GROUP


def own_lanes(stacked):
    group = lane_group((TAPS, 2 * LANES))
    chosen = jnp.zeros((TAPS, 2 * LANES), F32)
    for g in range(PER_TILE):
        chosen = jnp.where(group == g, stacked[g * TAPS : (g + 1) * TAPS], chosen)
    return chosen


def two_windows(first, second, third):
    upper = jnp.concatenate([first, second], 1)
    lower = jnp.concatenate([second, third], 1)
    return jnp.concatenate([upper, lower], 0)


def forward_kernel(filters, previous, signal, gating, response, kept, *refs):
    given, gated, stack = refs[:2], refs[2], refs[3]
    _, _, _, _, core = spot()
    rows = first_rows(filters[...], True)
    for i in range(signal.shape[1] // LANES):
        columns = slice(i * LANES, (i + 1) * LANES)
        band = stack.at[i % 2]
        banded(rows[i * PER_TILE : (i + 1) * PER_TILE], band)
        window = two_windows(previous[:, columns], signal[:TAPS, columns], signal[TAPS:, columns])
        made = own_lanes(jnp.dot(band[...], window, preferred_element_type=F32))
        for block in range(2):
            tokens = slice(block * TAPS, (block + 1) * TAPS)
            part = made[:, block * LANES : (block + 1) * LANES]
            response[tokens, columns] = part
            gated[tokens, columns] = (part * gating[tokens, columns].astype(F32)).astype(BF16)
    kept[...] = gated[:, aligned(core, kept.shape[1])]
    for i, out in enumerate(given):
        out[...] = gated[i * TAPS : (i + 1) * TAPS, aligned(1 - core, kept.shape[1])]


def forward(filters, previous, signal, gating):
    length, channels = signal.shape
    quarter = ((TAPS, channels // 2), BF16)
    return once(
        forward_kernel,
        "conv_forward",
        [filters, previous, signal, gating],
        [((length, channels), F32), ((length, channels // 2), BF16), quarter, quarter],
        [
            pltpu.VMEM((length, channels), BF16),
            pltpu.VMEM((2, PER_TILE * TAPS, 2 * TAPS), BF16),
        ],
    )


def join_kernel(kept, upper, lower, gated):
    _, _, _, _, core = spot()
    width = kept.shape[1]
    gated[: 2 * TAPS, aligned(core, width)] = kept[...]
    gated[:TAPS, aligned(1 - core, width)] = upper[...]
    gated[TAPS : 2 * TAPS, aligned(1 - core, width)] = lower[...]
    gated[2 * TAPS :] = gated[: gated.shape[0] - 2 * TAPS]


def join(kept, received, after):
    length, width = kept.shape
    shape = (length + 16, 2 * width)
    return once(join_kernel, "join", [kept, *received], [(shape, BF16)], (), after)[0]


def input_grad_kernel(filters, conv_grad, following, grad_input, stack):
    rows = first_rows(filters[...], False)
    for i in range(conv_grad.shape[1] // LANES):
        columns = slice(i * LANES, (i + 1) * LANES)
        band = stack.at[i % 2]
        banded(rows[i * PER_TILE : (i + 1) * PER_TILE], band)
        window = two_windows(
            conv_grad[:TAPS, columns], conv_grad[TAPS:, columns], following[:, columns]
        )
        made = own_lanes(jnp.dot(band[...], window, preferred_element_type=F32))
        for block in range(2):
            grad_input[block * TAPS : (block + 1) * TAPS, columns] = made[
                :, block * LANES : (block + 1) * LANES
            ].astype(BF16)


def input_grad(filters, conv_grad, following, after):
    return once(
        input_grad_kernel,
        "input_grad",
        [filters, conv_grad, following],
        [(conv_grad.shape, BF16)],
        [pltpu.VMEM((2, PER_TILE * TAPS, 2 * TAPS), BF16)],
        after,
    )[0]


def filter_grad_kernel(previous, signal, conv_grad, grad_filter, stack):
    square = (2 * TAPS, 2 * TAPS)
    turn = iota(square, 0) == (2 * TAPS - iota(square, 1)) % (2 * TAPS)
    turn = turn.astype(F32).astype(BF16)
    group = lane_group((TAPS, 2 * LANES))
    for i in range(signal.shape[1] // LANES):
        columns = slice(i * LANES, (i + 1) * LANES)
        masked = stack.at[i % 2]
        inputs = two_windows(previous[:, columns], signal[:TAPS, columns], signal[TAPS:, columns])
        turned = jnp.dot(turn, inputs, preferred_element_type=F32).astype(BF16)
        both = jnp.concatenate([conv_grad[:TAPS, columns], conv_grad[TAPS:, columns]], 1)
        both = both.astype(F32)
        for g in range(PER_TILE):
            masked[g * TAPS : (g + 1) * TAPS, :] = jnp.where(group == g, both, 0.0).astype(BF16)
        products = lax.dot_general(
            masked[...], turned, (((1,), (1,)), ((), ())), preferred_element_type=F32
        )
        for g in range(PER_TILE):
            skewed = pltpu.roll(products[g * TAPS : (g + 1) * TAPS], 0, 1, stride=1, stride_axis=0)
            row = i * PER_TILE + g
            grad_filter[row : row + 1, :] = jnp.sum(skewed[:, TAPS:], axis=0, keepdims=True)


def filter_grad(previous, signal, conv_grad, after):
    return once(
        filter_grad_kernel,
        "filter_grad",
        [previous, signal, conv_grad],
        [((signal.shape[1] // GROUP, TAPS), F32)],
        [pltpu.VMEM((2, PER_TILE * TAPS, 2 * TAPS), BF16)],
        after,
        4,
    )[0]


def pack_into(mine, other, outs):
    x, y, _, _, core = spot()
    part = mine.shape[0]
    depth = mine.shape[1] // SIDE

    @pl.when(core == 0)
    def _():
        for ref, rows in ((mine, slice(0, part)), (other, slice(part, 2 * part))):
            for s, out in enumerate(outs):
                for d in range(SIDE):
                    start = pl.multiple_of(d * depth + (x + s) % SIDE * WIDE, WIDE)
                    out[rows, d * WIDE : (d + 1) * WIDE] = ref[:, pl.ds(start, WIDE)]

    @pl.when(core == 1)
    def _():
        lower = iota((part, LANES), 1) < HALF
        for ref, rows in ((other, slice(0, part)), (mine, slice(part, 2 * part))):
            for s, out in enumerate(outs):
                to = (y + s) % SIDE
                upper_half = jnp.broadcast_to(to % 2, (part, LANES)) == 1
                for pair in range(2 * SIDE):
                    runs = []
                    for i in range(2):
                        start = pl.multiple_of((2 * pair + i) * WIDE + to // 2 * LANES, LANES)
                        runs.append(ref[:, pl.ds(start, LANES)].astype(F32))
                    first = jnp.where(upper_half, pltpu.roll(runs[0], HALF, 1), runs[0])
                    second = jnp.where(upper_half, runs[1], pltpu.roll(runs[1], HALF, 1))
                    both = jnp.where(lower, first, second).astype(BF16)
                    out[rows, pair * LANES : (pair + 1) * LANES] = both


def pack_kernel(mine, other, *outs):
    pack_into(mine, other, outs)


def pack(mine, other):
    rows, width = mine.shape
    return once(
        pack_kernel, "pack", [mine, other], [((2 * rows, width // SIDE), BF16)] * SIDE
    )


def relay_kernel(mine, other, before, after, opposite, *outs):
    pack_into(mine, other, outs)
    part = opposite.shape[0]
    outs[1][part:] = before[...]
    outs[2][part:] = opposite[...]
    outs[3][part:] = after[...]


def relay(mine, other, got_next, got_last, opposite):
    rows, width = opposite.shape
    return once(
        relay_kernel,
        "relay",
        [
            mine,
            other,
            (got_next, whole((TAPS, width))),
            (got_last, whole((TAPS, width), (1, 0))),
            opposite,
        ],
        [((rows, width), BF16)] + [((rows + TAPS, width), BF16)] * (SIDE - 1),
    )


def project_kernel(mine, other, weight, gating, response, *refs):
    _, _, _, half, core = spot()
    part = mine.shape[0]
    rows = refs[-1]
    conv_grad, grad_gate = refs[-3:-1]

    @pl.when(pl.program_id(0) == 0)
    def _():
        rows[aligned(core, part), :] = mine[...]
        rows[aligned(1 - core, part), :] = other[...]

    late = len(refs) > 3
    tokens = aligned(1 - half if late else half, TAPS)
    made = jnp.dot(rows[...], weight[...], preferred_element_type=F32)
    made_conv = (made * gating[tokens, :].astype(F32)).astype(BF16)
    made_gate = (made * response[tokens, :]).astype(BF16)
    if late:
        conv_grad[tokens, :] = made_conv
        grad_gate[tokens, :] = made_gate
        conv_grad[aligned(half, TAPS), :] = refs[0][...]
        grad_gate[aligned(half, TAPS), :] = refs[1][...]
    else:
        conv_grad[...] = made_conv
        grad_gate[...] = made_gate


def project(mine, other, weight, gating, response, done=(), after=()):
    length, channels = gating.shape
    depth = weight.shape[0]
    made = length if done else 2 * mine.shape[0]

    def body(*refs):
        kept = 5 + len(done)
        project_kernel(*refs[:kept], *refs[kept + len(after) :])

    return pl.pallas_call(
        body,
        grid=(channels // WIDE,),
        in_specs=[full(mine.shape)] * 2
        + [tile(depth, WIDE), tile(length, WIDE), tile(length, WIDE)]
        + [tile(TAPS, WIDE)] * len(done)
        + [ANYWHERE] * len(after),
        out_specs=[tile(made, WIDE)] * 2,
        out_shape=[jax.ShapeDtypeStruct((made, channels), BF16)] * 2,
        scratch_shapes=[pltpu.VMEM((2 * mine.shape[0], depth), BF16)],
        compiler_params=room(16),
        cost_estimate=lasting(5 if done else 0),
        name="project_late" if done else "project_early",
    )(mine, other, weight, gating, response, *done, *after)


def high_and_low(x):
    high = x.astype(BF16).astype(F32)
    return high, (x - high).astype(BF16).astype(F32)


def folded(x, rows):
    return jnp.concatenate([x[i : i + rows] for i in range(0, x.shape[0], rows)], 1)


def unfolded(x):
    return jnp.concatenate([x[:, i : i + LANES] for i in range(0, x.shape[1], LANES)], 0)


def riding(ref, start, rows):
    pair = ref[start : start + 2 * rows].astype(F32)
    return unfolded(pair[:rows] + pair[rows:])


def four_sum(parts):
    return (parts[0] + parts[2]) + (parts[1] + parts[3])


def weight_kernel(*refs):
    early, late = refs[:SIDE], refs[SIDE : 2 * SIDE]
    gated, got_next, before, after, got_last = refs[2 * SIDE : 2 * SIDE + 5]
    outs, turned, tokens = refs[-2 - SIDE : -2], refs[-2], refs[-1]
    x, y, _, half, core = spot()
    me = jnp.where(core == 0, y, x)
    upper = jnp.broadcast_to(half, before.shape) == 0
    opposite = (before[...].astype(F32), after[...].astype(F32))
    for i, (parts, h) in enumerate(((early, half), (late, 1 - half))):
        rows = aligned(h, TAPS)
        halves = opposite if i == 0 else opposite[::-1]
        blocks = (
            gated[rows, :],
            got_next[rows, :],
            jnp.where(upper, *halves).astype(BF16),
            got_last[rows, :],
        )
        for s in range(SIDE):
            at = slice((i * SIDE + s) * TAPS, (i * SIDE + s + 1) * TAPS)
            tokens[at] = blocks[s]
            transposed = parts[s][...].T
            for d in range(SIDE):
                for q in range(SIDE):
                    to = (q - me + SIDE) % SIDE * WIDE + d * HALF
                    start = d * WIDE + q * HALF
                    turned[pl.ds(pl.multiple_of(to, HALF), HALF), at] = transposed[
                        start : start + HALF
                    ]
    for s, out in enumerate(outs):
        features = turned[s * WIDE : (s + 1) * WIDE]
        out[...] = jnp.dot(features, tokens[...], preferred_element_type=F32).astype(out.dtype)


def weight_parts(early, own_late, gated, got, late, after):
    width = gated.shape[1]
    rows = own_late.shape[0]
    length = 2 * rows

    def block(array, start, count=rows):
        return array, whole((count, width), (start // count, 0))

    shape = (width // SIDE, width)
    return once(
        weight_kernel,
        "weight_parts",
        [
            early[0],
            early[1],
            block(late[1], rows),
            early[2],
            own_late,
            *[block(part, 0) for part in late],
            block(gated, 0, length),
            block(got[0], 0, length),
            block(late[0], rows),
            block(late[2], rows),
            block(got[1], 0, length),
        ],
        [(shape, F32)] + [(shape, BF16)] * (SIDE - 1),
        [pltpu.VMEM((width, 2 * SIDE * rows), BF16), pltpu.VMEM((2 * SIDE * rows, width), BF16)],
        after,
        4,
    )


def high_and_low(x):
    high = x.astype(BF16).astype(F32)
    return high, (x - high).astype(BF16).astype(F32)


def folded(x, rows):
    return jnp.concatenate([x[i : i + rows] for i in range(0, x.shape[0], rows)], 1)


def unfolded(x):
    return jnp.concatenate([x[:, i : i + LANES] for i in range(0, x.shape[1], LANES)], 0)


def riding(ref, start, rows):
    pair = ref[start : start + 2 * rows].astype(F32)
    return unfolded(pair[:rows] + pair[rows:])


def four_sum(parts):
    return (parts[0] + parts[2]) + (parts[1] + parts[3])


def first_sum_kernel(*refs):
    _, _, z, _, _ = spot()
    extra, outs, own_extra, kept = refs[SIDE], refs[SIDE + 1 : -2], refs[-2], refs[-1]
    run = kept.shape[0] // SIDE
    total = refs[0][...]
    for ref in refs[1:SIDE]:
        total = total + ref[...].astype(F32)
    for d in range(SIDE):
        kept[aligned((d - z + SIDE) % SIDE, run), :] = total[d * run : (d + 1) * run]
    high, low = (folded(part, own_extra.shape[0]) for part in high_and_low(extra[...]))
    own_extra[...] = high + low
    for s, out in enumerate(outs):
        out[:run] = kept[s * run : (s + 1) * run, :].astype(out.dtype)
        if s:
            out[run:] = jnp.concatenate([high, low], 0).astype(BF16)


def first_sum(parts, extra, after):
    rows, width = parts[0].shape
    below = LANES * extra.shape[0] // width
    run = rows // SIDE
    *sums, own_extra = once(
        first_sum_kernel,
        "first_sum",
        [*parts, extra],
        [((run, width), F32)]
        + [((run + 2 * below, width), BF16)] * (SIDE - 1)
        + [((below, width), F32)],
        [pltpu.VMEM((rows, width), F32)],
        after,
        1,
    )
    return sums, own_extra


def last_sum(parts, own_extra, filters, scale, filter_scale, after):
    rows, width = parts[0].shape
    below = own_extra.shape[0]

    def kernel(*refs):
        own, others, extra = refs[0], refs[1:SIDE], refs[SIDE]
        kept, given, filter_out, summed = refs[SIDE + 1 :]
        _, _, _, _, core = spot()
        total = own[...]
        for ref in others:
            total = total + ref[:rows].astype(F32)
        summed[...] = total * scale
        kept[...] = summed[:, aligned(core, width // 2)]
        given[...] = summed[:, aligned(1 - core, width // 2)]
        values = [unfolded(extra[...])] + [riding(ref, rows, below) for ref in others]
        filter_out[...] = four_sum(values) * filter_scale

    half = ((rows, width // 2), F32)
    return once(
        kernel,
        "last_sum",
        [*parts, own_extra],
        [half, half, (filters.shape, F32)],
        [pltpu.VMEM((rows, width), F32)],
        after,
    )


def beside(kept, received):
    def kernel(first, second, out):
        _, _, _, _, core = spot()
        out[:, aligned(core, first.shape[1])] = first[...]
        out[:, aligned(1 - core, first.shape[1])] = second[...]

    rows, width = kept.shape
    return once(kernel, "beside", [kept, received], [((rows, 2 * width), F32)])[0]


def tied(x, *after):
    return lax.optimization_barrier((x, *after))[0]


def paired(x, gather, by, before=()):
    return x + in_plane(tied(x, *before), gather, lambda place: place ^ by)


def local(conv_input, gate_value, out_grad, out_weight, filters):
    signal, gating, grads = conv_input[0], gate_value[0], out_grad[0]
    length, channels = signal.shape
    halo_sent = signal[length - TAPS :]
    signal, gating, filters, weight = (
        resident(x) for x in (signal, gating, filters, out_weight)
    )
    tokens_all = lax.axis_size("dp") * lax.axis_size("ctx") * length
    shifts = range(1, SIDE)

    late = moved(grads, "half")
    previous = shifted(halo_sent, 1)
    early_other = moved(grads, "core")
    grads = resident(grads)
    early = pack(grads, early_other)
    early_got = [stepped(early[1], True, 1), stepped(early[3], True, 3)]
    response, kept, *given = forward(filters, previous, signal, gating)
    gated = join(kept, [moved(part, "core") for part in given], early_got)
    got = [stepped(gated, True, 1), stepped(gated, True, 3)]
    conv_early, gate_early = project(grads, early_other, weight, gating, response)

    late_other = moved(tied(late, conv_early), "core")
    own_late, *late_sent = relay(late, late_other, *got, early[2])
    conv_grad, grad_gate = project(
        late, late_other, weight, gating, response, (conv_early, gate_early), (own_late,)
    )
    late_got = [stepped(late_sent[s - 1], True, s) for s in shifts]
    following = shifted(conv_grad[:TAPS], -1)
    filter_sum = filter_grad(previous, signal, conv_grad, ())
    parts = weight_parts([early[0], *early_got], own_late, gated, got, late_got, (filter_sum,))

    filter_sum = paired(filter_sum, True, 1)
    filter_sum = paired(filter_sum, True, 2, (parts[0],))
    filter_sum = paired(paired(filter_sum, False, 1), False, 2)
    parts = [parts[0]] + [stepped(parts[s], False, s) for s in shifts]
    sums, own_filter = first_sum(parts, filter_sum, (following,))
    grad_input = input_grad(filters, conv_grad, following, (sums[0],))
    line = [[(i, (i + s) % SIDE) for i in range(SIDE)] for s in shifts]
    sums = [sums[0]] + [lax.ppermute(sums[s], "dp", line[s - 1]) for s in shifts]
    kept, given, grad_filter = last_sum(
        sums,
        own_filter,
        filters,
        1.0 / math.sqrt(tokens_all),
        1.0 / math.sqrt(tokens_all * GROUP),
        (resident(grad_input),),
    )
    grad_weight = beside(kept, moved(given, "core"))
    return (grad_input[None], grad_gate[None], grad_weight, grad_filter)


def solution(mesh):
    placed = (
        P("dp", "ctx", "tp"),
        P("dp", "ctx", "tp"),
        P("dp", ("ctx", "tp"), None),
        P(None, "tp"),
        P("tp", None),
    )
    return jax.shard_map(
        local,
        mesh=mesh,
        in_specs=placed,
        out_specs=(
            P("dp", "ctx", "tp"),
            P("dp", "ctx", "tp"),
            P(("dp", "ctx"), "tp"),
            P("tp", None),
        ),
        check_vma=False,
    )
```

```python
import math

import jax
import jax.numpy as jnp
from jax import lax
from jax.experimental import pallas as pl
from jax.experimental.pallas import tpu as pltpu
from jax.sharding import PartitionSpec as P

F32 = jnp.float32
BF16 = jnp.bfloat16
SIDE = 4
TAPS = 128
GROUP = 16
LANES = 128
PER_TILE = LANES // GROUP
WIDE = 256


def room(mebibytes):
    return pltpu.CompilerParams(vmem_limit_bytes=mebibytes * 1024 * 1024)


def spot():
    ctx = lax.axis_index("ctx")
    tp = lax.axis_index("tp")
    return ctx // SIDE, ctx % SIDE, lax.axis_index("dp"), tp // 2, tp % 2


def moved(x, axis):
    step = 2 if axis == "half" else 1
    return lax.ppermute(x, "tp", [(i, i ^ step) for i in range(4)])


def in_plane(x, gather, target):
    pairs = []
    for i in range(SIDE * SIDE):
        for j in range(4):
            place_x, place_y = divmod(i, SIDE)
            if (j % 2 == 0) == gather:
                place_x = target(place_x)
            else:
                place_y = target(place_y)
            pairs.append((i * 4 + j, (place_x * SIDE + place_y) * 4 + j))
    return lax.ppermute(x, ("ctx", "tp"), pairs)


def stepped(x, gather, by):
    return in_plane(x, gather, lambda place: (place + by) % SIDE)


def shifted(x, by):
    devices = lax.axis_size("ctx")
    return lax.ppermute(x, "ctx", [(i, i + by) for i in range(devices) if 0 <= i + by < devices])


ANYWHERE = pl.BlockSpec(memory_space=pl.ANY)
HALF = LANES // 2


def resident(x):
    return pltpu.with_memory_space_constraint(x, pltpu.HBM)


def whole(shape, place=None):
    place = place or (0,) * len(shape)
    return pl.BlockSpec(tuple(shape), lambda i: place, pipeline_mode=pl.Buffered(1))


def full(shape):
    return pl.BlockSpec(tuple(shape), lambda i: (0,) * len(shape))


def tile(rows, width):
    return pl.BlockSpec((rows, width), lambda i: (0, i))


def iota(shape, dim):
    return lax.broadcasted_iota(jnp.int32, shape, dim)


def aligned(index, size):
    return pl.ds(pl.multiple_of(index * size, size), size)


def lasting(microseconds):
    return pl.CostEstimate(flops=int(microseconds * 1e9), bytes_accessed=0, transcendentals=0)


def once(kernel, name, ins, outs, scratch=(), after=(), lasts=0):
    def body(*refs):
        kernel(*refs[: len(ins)], *refs[len(ins) + len(after) :])

    specs = [i[1] if isinstance(i, tuple) else whole(i.shape) for i in ins]
    arrays = [i[0] if isinstance(i, tuple) else i for i in ins]
    return pl.pallas_call(
        body,
        grid=(1,),
        in_specs=specs + [ANYWHERE] * len(after),
        out_specs=[whole(shape) for shape, _ in outs],
        out_shape=[jax.ShapeDtypeStruct(shape, dtype) for shape, dtype in outs],
        scratch_shapes=list(scratch),
        compiler_params=room(20),
        cost_estimate=lasting(lasts),
        name=name,
    )(*arrays, *after)


def first_rows(filters, shifted_by):
    lane, tap = iota((TAPS, 2 * TAPS), 1), iota((TAPS, 2 * TAPS), 0)
    place = lane == (TAPS - tap if shifted_by else tap)
    return jnp.dot(filters, place.astype(F32).astype(BF16), preferred_element_type=F32)


def banded(rows, stack):
    for g in range(PER_TILE):
        first = jnp.broadcast_to(rows[g : g + 1], (TAPS, 2 * TAPS))
        skewed = pltpu.roll(first, 0, 1, stride=1, stride_axis=0)
        stack[g * TAPS : (g + 1) * TAPS, :] = skewed.astype(BF16)


def lane_group(shape):
    return iota(shape, len(shape) - 1) % LANES // GROUP


def own_lanes(stacked):
    group = lane_group((TAPS, 2 * LANES))
    chosen = jnp.zeros((TAPS, 2 * LANES), F32)
    for g in range(PER_TILE):
        chosen = jnp.where(group == g, stacked[g * TAPS : (g + 1) * TAPS], chosen)
    return chosen


def two_windows(first, second, third):
    upper = jnp.concatenate([first, second], 1)
    lower = jnp.concatenate([second, third], 1)
    return jnp.concatenate([upper, lower], 0)


def forward_kernel(filters, previous, signal, gating, response, kept, *refs):
    given, gated, stack = refs[:2], refs[2], refs[3]
    _, _, _, _, core = spot()
    rows = first_rows(filters[...], True)
    for i in range(signal.shape[1] // LANES):
        columns = slice(i * LANES, (i + 1) * LANES)
        band = stack.at[i % 2]
        banded(rows[i * PER_TILE : (i + 1) * PER_TILE], band)
        window = two_windows(previous[:, columns], signal[:TAPS, columns], signal[TAPS:, columns])
        made = own_lanes(jnp.dot(band[...], window, preferred_element_type=F32))
        for block in range(2):
            tokens = slice(block * TAPS, (block + 1) * TAPS)
            part = made[:, block * LANES : (block + 1) * LANES]
            response[tokens, columns] = part
            gated[tokens, columns] = (part * gating[tokens, columns].astype(F32)).astype(BF16)
    kept[...] = gated[:, aligned(core, kept.shape[1])]
    for i, out in enumerate(given):
        out[...] = gated[i * TAPS : (i + 1) * TAPS, aligned(1 - core, kept.shape[1])]


def forward(filters, previous, signal, gating, after):
    length, channels = signal.shape
    quarter = ((TAPS, channels // 2), BF16)
    return once(
        forward_kernel,
        "conv_forward",
        [filters, previous, signal, gating],
        [((length, channels), F32), ((length, channels // 2), BF16), quarter, quarter],
        [
            pltpu.VMEM((length, channels), BF16),
            pltpu.VMEM((2, PER_TILE * TAPS, 2 * TAPS), BF16),
        ],
        after,
    )


def join_kernel(kept, upper, lower, gated):
    _, _, _, _, core = spot()
    width = kept.shape[1]
    gated[: 2 * TAPS, aligned(core, width)] = kept[...]
    gated[:TAPS, aligned(1 - core, width)] = upper[...]
    gated[TAPS : 2 * TAPS, aligned(1 - core, width)] = lower[...]
    gated[2 * TAPS :] = gated[: gated.shape[0] - 2 * TAPS]


def join(kept, received, after):
    length, width = kept.shape
    shape = (length + 16, 2 * width)
    return once(join_kernel, "join", [kept, *received], [(shape, BF16)], (), after)[0]


def input_grad_kernel(filters, conv_grad, following, grad_input, stack):
    rows = first_rows(filters[...], False)
    for i in range(conv_grad.shape[1] // LANES):
        columns = slice(i * LANES, (i + 1) * LANES)
        band = stack.at[i % 2]
        banded(rows[i * PER_TILE : (i + 1) * PER_TILE], band)
        window = two_windows(
            conv_grad[:TAPS, columns], conv_grad[TAPS:, columns], following[:, columns]
        )
        made = own_lanes(jnp.dot(band[...], window, preferred_element_type=F32))
        for block in range(2):
            grad_input[block * TAPS : (block + 1) * TAPS, columns] = made[
                :, block * LANES : (block + 1) * LANES
            ].astype(BF16)


def input_grad(filters, conv_grad, following, after):
    return once(
        input_grad_kernel,
        "input_grad",
        [filters, conv_grad, following],
        [(conv_grad.shape, BF16)],
        [pltpu.VMEM((2, PER_TILE * TAPS, 2 * TAPS), BF16)],
        after,
    )[0]


def filter_grad_kernel(previous, signal, conv_grad, grad_filter, stack):
    square = (2 * TAPS, 2 * TAPS)
    turn = iota(square, 0) == (2 * TAPS - iota(square, 1)) % (2 * TAPS)
    turn = turn.astype(F32).astype(BF16)
    group = lane_group((TAPS, 2 * LANES))
    for i in range(signal.shape[1] // LANES):
        columns = slice(i * LANES, (i + 1) * LANES)
        masked = stack.at[i % 2]
        inputs = two_windows(previous[:, columns], signal[:TAPS, columns], signal[TAPS:, columns])
        turned = jnp.dot(turn, inputs, preferred_element_type=F32).astype(BF16)
        both = jnp.concatenate([conv_grad[:TAPS, columns], conv_grad[TAPS:, columns]], 1)
        both = both.astype(F32)
        for g in range(PER_TILE):
            masked[g * TAPS : (g + 1) * TAPS, :] = jnp.where(group == g, both, 0.0).astype(BF16)
        products = lax.dot_general(
            masked[...], turned, (((1,), (1,)), ((), ())), preferred_element_type=F32
        )
        for g in range(PER_TILE):
            skewed = pltpu.roll(products[g * TAPS : (g + 1) * TAPS], 0, 1, stride=1, stride_axis=0)
            row = i * PER_TILE + g
            grad_filter[row : row + 1, :] = jnp.sum(skewed[:, TAPS:], axis=0, keepdims=True)


def filter_grad(previous, signal, conv_grad, after):
    return once(
        filter_grad_kernel,
        "filter_grad",
        [previous, signal, conv_grad],
        [((signal.shape[1] // GROUP, TAPS), F32)],
        [pltpu.VMEM((2, PER_TILE * TAPS, 2 * TAPS), BF16)],
        after,
        4,
    )[0]


def pack_into(mine, other, outs):
    x, y, _, _, core = spot()
    part = mine.shape[0]
    depth = mine.shape[1] // SIDE

    @pl.when(core == 0)
    def _():
        for ref, rows in ((mine, slice(0, part)), (other, slice(part, 2 * part))):
            for s, out in enumerate(outs):
                for d in range(SIDE):
                    start = pl.multiple_of(d * depth + (x + s) % SIDE * WIDE, WIDE)
                    out[rows, d * WIDE : (d + 1) * WIDE] = ref[:, pl.ds(start, WIDE)]

    @pl.when(core == 1)
    def _():
        lower = iota((part, LANES), 1) < HALF
        for ref, rows in ((other, slice(0, part)), (mine, slice(part, 2 * part))):
            for s, out in enumerate(outs):
                to = (y + s) % SIDE
                upper_half = jnp.broadcast_to(to % 2, (part, LANES)) == 1
                for pair in range(2 * SIDE):
                    runs = []
                    for i in range(2):
                        start = pl.multiple_of((2 * pair + i) * WIDE + to // 2 * LANES, LANES)
                        runs.append(ref[:, pl.ds(start, LANES)].astype(F32))
                    first = jnp.where(upper_half, pltpu.roll(runs[0], HALF, 1), runs[0])
                    second = jnp.where(upper_half, runs[1], pltpu.roll(runs[1], HALF, 1))
                    both = jnp.where(lower, first, second).astype(BF16)
                    out[rows, pair * LANES : (pair + 1) * LANES] = both


def pack_kernel(mine, other, *outs):
    pack_into(mine, other, outs)


def pack(mine, other):
    rows, width = mine.shape
    return once(
        pack_kernel, "pack", [mine, other], [((2 * rows, width // SIDE), BF16)] * SIDE
    )


def relay_kernel(mine, other, before, after, *outs):
    pack_into(mine, other, outs)
    part = outs[0].shape[0]
    outs[1][part:] = before[...]
    outs[3][part:] = after[...]


def relay(mine, other, got_next, got_last):
    rows, width = 2 * mine.shape[0], got_next.shape[1]
    return once(
        relay_kernel,
        "relay",
        [
            mine,
            other,
            (got_next, whole((TAPS, width))),
            (got_last, whole((TAPS, width), (1, 0))),
        ],
        [((rows + s % 2 * TAPS, width), BF16) for s in range(SIDE)],
    )


def project_kernel(mine, other, weight, gating, response, *refs):
    _, _, _, half, core = spot()
    part = mine.shape[0]
    rows = refs[-1]
    conv_grad, grad_gate = refs[-3:-1]

    @pl.when(pl.program_id(0) == 0)
    def _():
        rows[aligned(core, part), :] = mine[...]
        rows[aligned(1 - core, part), :] = other[...]

    late = len(refs) > 3
    tokens = aligned(1 - half if late else half, TAPS)
    made = jnp.dot(rows[...], weight[...], preferred_element_type=F32)
    made_conv = (made * gating[tokens, :].astype(F32)).astype(BF16)
    made_gate = (made * response[tokens, :]).astype(BF16)
    if late:
        conv_grad[tokens, :] = made_conv
        grad_gate[tokens, :] = made_gate
        conv_grad[aligned(half, TAPS), :] = refs[0][...]
        grad_gate[aligned(half, TAPS), :] = refs[1][...]
    else:
        conv_grad[...] = made_conv
        grad_gate[...] = made_gate


def project(mine, other, weight, gating, response, done=(), after=()):
    length, channels = gating.shape
    depth = weight.shape[0]
    made = length if done else 2 * mine.shape[0]

    def body(*refs):
        kept = 5 + len(done)
        project_kernel(*refs[:kept], *refs[kept + len(after) :])

    return pl.pallas_call(
        body,
        grid=(channels // WIDE,),
        in_specs=[full(mine.shape)] * 2
        + [tile(depth, WIDE), tile(length, WIDE), tile(length, WIDE)]
        + [tile(TAPS, WIDE)] * len(done)
        + [ANYWHERE] * len(after),
        out_specs=[tile(made, WIDE)] * 2,
        out_shape=[jax.ShapeDtypeStruct((made, channels), BF16)] * 2,
        scratch_shapes=[pltpu.VMEM((2 * mine.shape[0], depth), BF16)],
        compiler_params=room(16),
        cost_estimate=lasting(5 if done else 0),
        name="project_late" if done else "project_early",
    )(mine, other, weight, gating, response, *done, *after)


def weight_kernel(*refs):
    early, late = refs[:SIDE], refs[SIDE : 2 * SIDE]
    gated, got_next, before, after, got_last = refs[2 * SIDE : 2 * SIDE + 5]
    outs, turned, tokens = refs[-2 - SIDE : -2], refs[-2], refs[-1]
    x, y, _, half, core = spot()
    me = jnp.where(core == 0, y, x)
    upper = jnp.broadcast_to(half, before.shape) == 0
    opposite = (before[...].astype(F32), after[...].astype(F32))
    for i, (parts, h) in enumerate(((early, half), (late, 1 - half))):
        rows = aligned(h, TAPS)
        halves = opposite if i == 0 else opposite[::-1]
        blocks = (
            gated[rows, :],
            got_next[rows, :],
            jnp.where(upper, *halves).astype(BF16),
            got_last[rows, :],
        )
        for s in range(SIDE):
            at = slice((i * SIDE + s) * TAPS, (i * SIDE + s + 1) * TAPS)
            tokens[at] = blocks[s]
            transposed = parts[s][...].T
            for d in range(SIDE):
                for q in range(SIDE):
                    to = (q - me + SIDE) % SIDE * WIDE + d * HALF
                    start = d * WIDE + q * HALF
                    turned[pl.ds(pl.multiple_of(to, HALF), HALF), at] = transposed[
                        start : start + HALF
                    ]
    for s, out in enumerate(outs):
        features = turned[s * WIDE : (s + 1) * WIDE]
        out[...] = jnp.dot(features, tokens[...], preferred_element_type=F32).astype(out.dtype)


def weight_parts(early, own_late, gated, got, late, after):
    width = gated.shape[1]
    rows = own_late.shape[0]
    length = 2 * rows

    def block(array, start, count=rows):
        return array, whole((count, width), (start // count, 0))

    shape = (width // SIDE, width)
    return once(
        weight_kernel,
        "weight_parts",
        [
            *early,
            own_late,
            *[block(part, 0) for part in late],
            block(gated, 0, length),
            block(got[0], 0, length),
            block(late[0], rows),
            block(late[2], rows),
            block(got[1], 0, length),
        ],
        [(shape, F32)] + [(shape, BF16)] * (SIDE - 1),
        [pltpu.VMEM((width, 2 * SIDE * rows), BF16), pltpu.VMEM((2 * SIDE * rows, width), BF16)],
        after,
        4,
    )


def four_sum(parts):
    return (parts[0] + parts[2]) + (parts[1] + parts[3])


def first_sum_kernel(*refs):
    _, _, z, _, _ = spot()
    outs, kept = refs[SIDE:-1], refs[-1]
    run = kept.shape[0] // SIDE
    total = refs[0][...]
    for ref in refs[1:SIDE]:
        total = total + ref[...].astype(F32)
    for d in range(SIDE):
        kept[aligned((d - z + SIDE) % SIDE, run), :] = total[d * run : (d + 1) * run]
    for s, out in enumerate(outs):
        out[...] = kept[s * run : (s + 1) * run, :].astype(out.dtype)


def first_sum(parts, after):
    rows, width = parts[0].shape
    run = rows // SIDE
    return once(
        first_sum_kernel,
        "first_sum",
        parts,
        [((run, width), F32)] + [((run, width), BF16)] * (SIDE - 1),
        [pltpu.VMEM((rows, width), F32)],
        after,
        1,
    )


def last_sum(parts, scale, after):
    rows, width = parts[0].shape

    def kernel(*refs):
        kept, given, summed = refs[SIDE:]
        _, _, _, _, core = spot()
        total = refs[0][...]
        for ref in refs[1:SIDE]:
            total = total + ref[...].astype(F32)
        summed[...] = total * scale
        kept[...] = summed[:, aligned(core, width // 2)]
        given[...] = summed[:, aligned(1 - core, width // 2)]

    half = ((rows, width // 2), F32)
    return once(
        kernel, "last_sum", parts, [half, half], [pltpu.VMEM((rows, width), F32)], after
    )


def beside(kept, received):
    def kernel(first, second, out):
        _, _, _, _, core = spot()
        out[:, aligned(core, first.shape[1])] = first[...]
        out[:, aligned(1 - core, first.shape[1])] = second[...]

    rows, width = kept.shape
    return once(kernel, "beside", [kept, received], [((rows, 2 * width), F32)])[0]


def tied(x, *after):
    return lax.optimization_barrier((x, *after))[0]


def paired(x, gather, by, before=()):
    return x + in_plane(tied(x, *before), gather, lambda place: place ^ by)


def local(conv_input, gate_value, out_grad, out_weight, filters):
    signal, gating, grads = conv_input[0], gate_value[0], out_grad[0]
    length, channels = signal.shape
    halo_sent = signal[length - TAPS :]
    signal, gating, filters, weight = (
        resident(x) for x in (signal, gating, filters, out_weight)
    )
    tokens_all = lax.axis_size("dp") * lax.axis_size("ctx") * length
    shifts = range(1, SIDE)

    late = moved(grads, "half")
    previous = shifted(halo_sent, 1)
    early_other = moved(grads, "core")
    grads = resident(grads)
    early = pack(grads, early_other)
    early_got = [stepped(early[s], True, s) for s in shifts]
    response, kept, *given = forward(filters, previous, signal, gating, early_got)
    gated = join(kept, [moved(part, "core") for part in given], ())
    got = [stepped(gated, True, 1), stepped(gated, True, 3)]
    conv_early, gate_early = project(grads, early_other, weight, gating, response)

    late_other = moved(tied(late, conv_early), "core")
    own_late, *late_sent = relay(late, late_other, *got)
    conv_grad, grad_gate = project(
        late, late_other, weight, gating, response, (conv_early, gate_early), (own_late,)
    )
    late_got = [stepped(late_sent[s - 1], True, s) for s in shifts]
    following = shifted(conv_grad[:TAPS], -1)
    parts = weight_parts([early[0], *early_got], own_late, gated, got, late_got, (conv_grad,))
    filter_sum = filter_grad(previous, signal, conv_grad, (parts[0],))
    filter_sum = four_sum([filter_sum] + [stepped(filter_sum, True, s) for s in shifts])
    parts = [parts[0]] + [stepped(parts[s], False, s) for s in shifts]
    sums = first_sum(parts, (following,))
    grad_input = input_grad(filters, conv_grad, following, (sums[0],))
    line = [[(i, (i + s) % SIDE) for i in range(SIDE)] for s in shifts]
    filter_sum = paired(paired(filter_sum, False, 1, (sums[0],)), False, 2)
    filter_sum = four_sum([filter_sum] + [lax.ppermute(filter_sum, "dp", pairs) for pairs in line])
    grad_filter = filter_sum * (1.0 / math.sqrt(tokens_all * GROUP))
    sums = [sums[0]] + [lax.ppermute(sums[s], "dp", line[s - 1]) for s in shifts]
    kept, given = last_sum(sums, 1.0 / math.sqrt(tokens_all), (resident(grad_input),))
    grad_weight = beside(kept, moved(given, "core"))
    return (grad_input[None], grad_gate[None], grad_weight, grad_filter)


def solution(mesh):
    placed = (
        P("dp", "ctx", "tp"),
        P("dp", "ctx", "tp"),
        P("dp", ("ctx", "tp"), None),
        P(None, "tp"),
        P("tp", None),
    )
    return jax.shard_map(
        local,
        mesh=mesh,
        in_specs=placed,
        out_specs=(
            P("dp", "ctx", "tp"),
            P("dp", "ctx", "tp"),
            P(("dp", "ctx"), "tp"),
            P("tp", None),
        ),
        check_vma=False,
    )
```

```python
import math

import jax
import jax.numpy as jnp
from jax import lax
from jax.experimental import pallas as pl
from jax.experimental.pallas import tpu as pltpu
from jax.sharding import PartitionSpec as P

F32 = jnp.float32
BF16 = jnp.bfloat16
SIDE = 4
TAPS = 128
GROUP = 16
LANES = 128
PER_TILE = LANES // GROUP
WIDE = 256


def room(mebibytes):
    return pltpu.CompilerParams(vmem_limit_bytes=mebibytes * 1024 * 1024)


def spot():
    ctx = lax.axis_index("ctx")
    tp = lax.axis_index("tp")
    return ctx // SIDE, ctx % SIDE, lax.axis_index("dp"), tp // 2, tp % 2


def moved(x, axis):
    step = 2 if axis == "half" else 1
    return lax.ppermute(x, "tp", [(i, i ^ step) for i in range(4)])


def in_plane(x, gather, target):
    pairs = []
    for i in range(SIDE * SIDE):
        for j in range(4):
            place_x, place_y = divmod(i, SIDE)
            if (j % 2 == 0) == gather:
                place_x = target(place_x)
            else:
                place_y = target(place_y)
            pairs.append((i * 4 + j, (place_x * SIDE + place_y) * 4 + j))
    return lax.ppermute(x, ("ctx", "tp"), pairs)


def stepped(x, gather, by):
    return in_plane(x, gather, lambda place: (place + by) % SIDE)


def shifted(x, by):
    devices = lax.axis_size("ctx")
    return lax.ppermute(x, "ctx", [(i, i + by) for i in range(devices) if 0 <= i + by < devices])


ANYWHERE = pl.BlockSpec(memory_space=pl.ANY)
HALF = LANES // 2


def resident(x):
    return pltpu.with_memory_space_constraint(x, pltpu.HBM)


def whole(shape, place=None):
    place = place or (0,) * len(shape)
    return pl.BlockSpec(tuple(shape), lambda i: place, pipeline_mode=pl.Buffered(1))


def full(shape):
    return pl.BlockSpec(tuple(shape), lambda i: (0,) * len(shape))


def tile(rows, width):
    return pl.BlockSpec((rows, width), lambda i: (0, i))


def iota(shape, dim):
    return lax.broadcasted_iota(jnp.int32, shape, dim)


def aligned(index, size):
    return pl.ds(pl.multiple_of(index * size, size), size)


def lasting(microseconds):
    return pl.CostEstimate(flops=int(microseconds * 1e9), bytes_accessed=0, transcendentals=0)


def once(kernel, name, ins, outs, scratch=(), after=(), lasts=0):
    def body(*refs):
        kernel(*refs[: len(ins)], *refs[len(ins) + len(after) :])

    specs = [i[1] if isinstance(i, tuple) else whole(i.shape) for i in ins]
    arrays = [i[0] if isinstance(i, tuple) else i for i in ins]
    return pl.pallas_call(
        body,
        grid=(1,),
        in_specs=specs + [ANYWHERE] * len(after),
        out_specs=[whole(shape) for shape, _ in outs],
        out_shape=[jax.ShapeDtypeStruct(shape, dtype) for shape, dtype in outs],
        scratch_shapes=list(scratch),
        compiler_params=room(20),
        cost_estimate=lasting(lasts),
        name=name,
    )(*arrays, *after)


def first_rows(filters, shifted_by):
    lane, tap = iota((TAPS, 2 * TAPS), 1), iota((TAPS, 2 * TAPS), 0)
    place = lane == (TAPS - tap if shifted_by else tap)
    return jnp.dot(filters, place.astype(F32).astype(BF16), preferred_element_type=F32)


def banded(rows, stack):
    for g in range(PER_TILE):
        first = jnp.broadcast_to(rows[g : g + 1], (TAPS, 2 * TAPS))
        skewed = pltpu.roll(first, 0, 1, stride=1, stride_axis=0)
        stack[g * TAPS : (g + 1) * TAPS, :] = skewed.astype(BF16)


def lane_group(shape):
    return iota(shape, len(shape) - 1) % LANES // GROUP


def own_lanes(stacked):
    group = lane_group((TAPS, 2 * LANES))
    chosen = jnp.zeros((TAPS, 2 * LANES), F32)
    for g in range(PER_TILE):
        chosen = jnp.where(group == g, stacked[g * TAPS : (g + 1) * TAPS], chosen)
    return chosen


def two_windows(first, second, third):
    upper = jnp.concatenate([first, second], 1)
    lower = jnp.concatenate([second, third], 1)
    return jnp.concatenate([upper, lower], 0)


def forward_kernel(filters, previous, signal, gating, response, kept, *refs):
    given, gated, stack = refs[:2], refs[2], refs[3]
    _, _, _, _, core = spot()
    rows = first_rows(filters[...], True)
    for i in range(signal.shape[1] // LANES):
        columns = slice(i * LANES, (i + 1) * LANES)
        band = stack.at[i % 2]
        banded(rows[i * PER_TILE : (i + 1) * PER_TILE], band)
        window = two_windows(previous[:, columns], signal[:TAPS, columns], signal[TAPS:, columns])
        made = own_lanes(jnp.dot(band[...], window, preferred_element_type=F32))
        for block in range(2):
            tokens = slice(block * TAPS, (block + 1) * TAPS)
            part = made[:, block * LANES : (block + 1) * LANES]
            response[tokens, columns] = part
            gated[tokens, columns] = (part * gating[tokens, columns].astype(F32)).astype(BF16)
    kept[...] = gated[:, aligned(core, kept.shape[1])]
    for i, out in enumerate(given):
        out[...] = gated[i * TAPS : (i + 1) * TAPS, aligned(1 - core, kept.shape[1])]


def forward(filters, previous, signal, gating):
    length, channels = signal.shape
    quarter = ((TAPS, channels // 2), BF16)
    return once(
        forward_kernel,
        "conv_forward",
        [filters, previous, signal, gating],
        [((length, channels), F32), ((length, channels // 2), BF16), quarter, quarter],
        [
            pltpu.VMEM((length, channels), BF16),
            pltpu.VMEM((2, PER_TILE * TAPS, 2 * TAPS), BF16),
        ],
    )


def join_kernel(kept, upper, lower, gated):
    _, _, _, _, core = spot()
    width = kept.shape[1]
    gated[: 2 * TAPS, aligned(core, width)] = kept[...]
    gated[:TAPS, aligned(1 - core, width)] = upper[...]
    gated[TAPS : 2 * TAPS, aligned(1 - core, width)] = lower[...]
    gated[2 * TAPS :] = gated[: gated.shape[0] - 2 * TAPS]


def join(kept, received, after):
    length, width = kept.shape
    shape = (length + 16, 2 * width)
    return once(join_kernel, "join", [kept, *received], [(shape, BF16)], (), after)[0]


def input_grad_kernel(filters, conv_grad, following, grad_input, stack):
    rows = first_rows(filters[...], False)
    for i in range(conv_grad.shape[1] // LANES):
        columns = slice(i * LANES, (i + 1) * LANES)
        band = stack.at[i % 2]
        banded(rows[i * PER_TILE : (i + 1) * PER_TILE], band)
        window = two_windows(
            conv_grad[:TAPS, columns], conv_grad[TAPS:, columns], following[:, columns]
        )
        made = own_lanes(jnp.dot(band[...], window, preferred_element_type=F32))
        for block in range(2):
            grad_input[block * TAPS : (block + 1) * TAPS, columns] = made[
                :, block * LANES : (block + 1) * LANES
            ].astype(BF16)


def input_grad(filters, conv_grad, following, after):
    return once(
        input_grad_kernel,
        "input_grad",
        [filters, conv_grad, following],
        [(conv_grad.shape, BF16)],
        [pltpu.VMEM((2, PER_TILE * TAPS, 2 * TAPS), BF16)],
        after,
    )[0]


def filter_grad_kernel(previous, signal, conv_grad, grad_filter, stack):
    square = (2 * TAPS, 2 * TAPS)
    turn = iota(square, 0) == (2 * TAPS - iota(square, 1)) % (2 * TAPS)
    turn = turn.astype(F32).astype(BF16)
    group = lane_group((TAPS, 2 * LANES))
    for i in range(signal.shape[1] // LANES):
        columns = slice(i * LANES, (i + 1) * LANES)
        masked = stack.at[i % 2]
        inputs = two_windows(previous[:, columns], signal[:TAPS, columns], signal[TAPS:, columns])
        turned = jnp.dot(turn, inputs, preferred_element_type=F32).astype(BF16)
        both = jnp.concatenate([conv_grad[:TAPS, columns], conv_grad[TAPS:, columns]], 1)
        both = both.astype(F32)
        for g in range(PER_TILE):
            masked[g * TAPS : (g + 1) * TAPS, :] = jnp.where(group == g, both, 0.0).astype(BF16)
        products = lax.dot_general(
            masked[...], turned, (((1,), (1,)), ((), ())), preferred_element_type=F32
        )
        for g in range(PER_TILE):
            skewed = pltpu.roll(products[g * TAPS : (g + 1) * TAPS], 0, 1, stride=1, stride_axis=0)
            row = i * PER_TILE + g
            grad_filter[row : row + 1, :] = jnp.sum(skewed[:, TAPS:], axis=0, keepdims=True)


def filter_grad(previous, signal, conv_grad, after):
    return once(
        filter_grad_kernel,
        "filter_grad",
        [previous, signal, conv_grad],
        [((signal.shape[1] // GROUP, TAPS), F32)],
        [pltpu.VMEM((2, PER_TILE * TAPS, 2 * TAPS), BF16)],
        after,
        4,
    )[0]


def pack_into(mine, other, outs):
    x, y, _, _, core = spot()
    part = mine.shape[0]
    depth = mine.shape[1] // SIDE

    @pl.when(core == 0)
    def _():
        for ref, rows in ((mine, slice(0, part)), (other, slice(part, 2 * part))):
            for s, out in enumerate(outs):
                for d in range(SIDE):
                    start = pl.multiple_of(d * depth + (x + s) % SIDE * WIDE, WIDE)
                    out[rows, d * WIDE : (d + 1) * WIDE] = ref[:, pl.ds(start, WIDE)]

    @pl.when(core == 1)
    def _():
        lower = iota((part, LANES), 1) < HALF
        for ref, rows in ((other, slice(0, part)), (mine, slice(part, 2 * part))):
            for s, out in enumerate(outs):
                to = (y + s) % SIDE
                upper_half = jnp.broadcast_to(to % 2, (part, LANES)) == 1
                for pair in range(2 * SIDE):
                    runs = []
                    for i in range(2):
                        start = pl.multiple_of((2 * pair + i) * WIDE + to // 2 * LANES, LANES)
                        runs.append(ref[:, pl.ds(start, LANES)].astype(F32))
                    first = jnp.where(upper_half, pltpu.roll(runs[0], HALF, 1), runs[0])
                    second = jnp.where(upper_half, runs[1], pltpu.roll(runs[1], HALF, 1))
                    both = jnp.where(lower, first, second).astype(BF16)
                    out[rows, pair * LANES : (pair + 1) * LANES] = both


def pack_kernel(mine, other, *outs):
    pack_into(mine, other, outs)


def pack(mine, other):
    rows, width = mine.shape
    return once(
        pack_kernel, "pack", [mine, other], [((2 * rows, width // SIDE), BF16)] * SIDE
    )


def relay_kernel(mine, other, before, after, opposite, *outs):
    pack_into(mine, other, outs)
    part = opposite.shape[0]
    outs[1][part:] = before[...]
    outs[2][part:] = opposite[...]
    outs[3][part:] = after[...]


def relay(mine, other, got_next, got_last, opposite):
    rows, width = opposite.shape
    return once(
        relay_kernel,
        "relay",
        [
            mine,
            other,
            (got_next, whole((TAPS, width))),
            (got_last, whole((TAPS, width), (1, 0))),
            opposite,
        ],
        [((rows, width), BF16)] + [((rows + TAPS, width), BF16)] * (SIDE - 1),
    )


def project_kernel(mine, other, weight, gating, response, *refs):
    _, _, _, half, core = spot()
    part = mine.shape[0]
    rows = refs[-1]
    conv_grad, grad_gate = refs[-3:-1]

    @pl.when(pl.program_id(0) == 0)
    def _():
        rows[aligned(core, part), :] = mine[...]
        rows[aligned(1 - core, part), :] = other[...]

    late = len(refs) > 3
    tokens = aligned(1 - half if late else half, TAPS)
    made = jnp.dot(rows[...], weight[...], preferred_element_type=F32)
    made_conv = (made * gating[tokens, :].astype(F32)).astype(BF16)
    made_gate = (made * response[tokens, :]).astype(BF16)
    if late:
        conv_grad[tokens, :] = made_conv
        grad_gate[tokens, :] = made_gate
        conv_grad[aligned(half, TAPS), :] = refs[0][...]
        grad_gate[aligned(half, TAPS), :] = refs[1][...]
    else:
        conv_grad[...] = made_conv
        grad_gate[...] = made_gate


def project(mine, other, weight, gating, response, done=(), after=()):
    length, channels = gating.shape
    depth = weight.shape[0]
    made = length if done else 2 * mine.shape[0]

    def body(*refs):
        kept = 5 + len(done)
        project_kernel(*refs[:kept], *refs[kept + len(after) :])

    return pl.pallas_call(
        body,
        grid=(channels // WIDE,),
        in_specs=[full(mine.shape)] * 2
        + [tile(depth, WIDE), tile(length, WIDE), tile(length, WIDE)]
        + [tile(TAPS, WIDE)] * len(done)
        + [ANYWHERE] * len(after),
        out_specs=[tile(made, WIDE)] * 2,
        out_shape=[jax.ShapeDtypeStruct((made, channels), BF16)] * 2,
        scratch_shapes=[pltpu.VMEM((2 * mine.shape[0], depth), BF16)],
        compiler_params=room(16),
        cost_estimate=lasting(5 if done else 0),
        name="project_late" if done else "project_early",
    )(mine, other, weight, gating, response, *done, *after)


def weight_kernel(*refs):
    early, late = refs[:SIDE], refs[SIDE : 2 * SIDE]
    gated, got_next, before, after, got_last = refs[2 * SIDE : 2 * SIDE + 5]
    outs, turned, tokens = refs[-2 - SIDE : -2], refs[-2], refs[-1]
    x, y, _, half, core = spot()
    me = jnp.where(core == 0, y, x)
    upper = jnp.broadcast_to(half, before.shape) == 0
    opposite = (before[...].astype(F32), after[...].astype(F32))
    for i, (parts, h) in enumerate(((early, half), (late, 1 - half))):
        rows = aligned(h, TAPS)
        halves = opposite if i == 0 else opposite[::-1]
        blocks = (
            gated[rows, :],
            got_next[rows, :],
            jnp.where(upper, *halves).astype(BF16),
            got_last[rows, :],
        )
        for s in range(SIDE):
            at = slice((i * SIDE + s) * TAPS, (i * SIDE + s + 1) * TAPS)
            tokens[at] = blocks[s]
            transposed = parts[s][...].T
            for d in range(SIDE):
                for q in range(SIDE):
                    to = (q - me + SIDE) % SIDE * WIDE + d * HALF
                    start = d * WIDE + q * HALF
                    turned[pl.ds(pl.multiple_of(to, HALF), HALF), at] = transposed[
                        start : start + HALF
                    ]
    for s, out in enumerate(outs):
        features = turned[s * WIDE : (s + 1) * WIDE]
        out[...] = jnp.dot(features, tokens[...], preferred_element_type=F32).astype(out.dtype)


def weight_parts(early, own_late, gated, got, late, after):
    width = gated.shape[1]
    rows = own_late.shape[0]
    length = 2 * rows

    def block(array, start, count=rows):
        return array, whole((count, width), (start // count, 0))

    shape = (width // SIDE, width)
    return once(
        weight_kernel,
        "weight_parts",
        [
            early[0],
            early[1],
            block(late[1], rows),
            early[2],
            own_late,
            *[block(part, 0) for part in late],
            block(gated, 0, length),
            block(got[0], 0, length),
            block(late[0], rows),
            block(late[2], rows),
            block(got[1], 0, length),
        ],
        [(shape, F32)] + [(shape, BF16)] * (SIDE - 1),
        [pltpu.VMEM((width, 2 * SIDE * rows), BF16), pltpu.VMEM((2 * SIDE * rows, width), BF16)],
        after,
        4,
    )


def high_and_low(x):
    high = x.astype(BF16).astype(F32)
    return high, (x - high).astype(BF16).astype(F32)


def folded(x, rows):
    return jnp.concatenate([x[i : i + rows] for i in range(0, x.shape[0], rows)], 1)


def unfolded(x):
    return jnp.concatenate([x[:, i : i + LANES] for i in range(0, x.shape[1], LANES)], 0)


def riding(ref, start, rows):
    pair = ref[start : start + 2 * rows].astype(F32)
    return unfolded(pair[:rows] + pair[rows:])


def four_sum(parts):
    return (parts[0] + parts[2]) + (parts[1] + parts[3])


def first_sum_kernel(*refs):
    _, _, z, _, _ = spot()
    extra, outs, own_extra, kept = refs[SIDE], refs[SIDE + 1 : -2], refs[-2], refs[-1]
    run = kept.shape[0] // SIDE
    total = refs[0][...]
    for ref in refs[1:SIDE]:
        total = total + ref[...].astype(F32)
    for d in range(SIDE):
        kept[aligned((d - z + SIDE) % SIDE, run), :] = total[d * run : (d + 1) * run]
    high, low = (folded(part, own_extra.shape[0]) for part in high_and_low(extra[...]))
    own_extra[...] = high + low
    for s, out in enumerate(outs):
        out[:run] = kept[s * run : (s + 1) * run, :].astype(out.dtype)
        if s:
            out[run:] = jnp.concatenate([high, low], 0).astype(BF16)


def first_sum(parts, extra, after):
    rows, width = parts[0].shape
    below = LANES * extra.shape[0] // width
    run = rows // SIDE
    *sums, own_extra = once(
        first_sum_kernel,
        "first_sum",
        [*parts, extra],
        [((run, width), F32)]
        + [((run + 2 * below, width), BF16)] * (SIDE - 1)
        + [((below, width), F32)],
        [pltpu.VMEM((rows, width), F32)],
        after,
        1,
    )
    return sums, own_extra


def last_sum(parts, own_extra, filters, scale, filter_scale, after):
    rows, width = parts[0].shape
    below = own_extra.shape[0]

    def kernel(*refs):
        own, others, extra = refs[0], refs[1:SIDE], refs[SIDE]
        kept, given, filter_out, summed = refs[SIDE + 1 :]
        _, _, _, _, core = spot()
        total = own[...]
        for ref in others:
            total = total + ref[:rows].astype(F32)
        summed[...] = total * scale
        kept[...] = summed[:, aligned(core, width // 2)]
        given[...] = summed[:, aligned(1 - core, width // 2)]
        values = [unfolded(extra[...])] + [riding(ref, rows, below) for ref in others]
        filter_out[...] = four_sum(values) * filter_scale

    half = ((rows, width // 2), F32)
    return once(
        kernel,
        "last_sum",
        [*parts, own_extra],
        [half, half, (filters.shape, F32)],
        [pltpu.VMEM((rows, width), F32)],
        after,
    )


def beside(kept, received):
    def kernel(first, second, out):
        _, _, _, _, core = spot()
        out[:, aligned(core, first.shape[1])] = first[...]
        out[:, aligned(1 - core, first.shape[1])] = second[...]

    rows, width = kept.shape
    return once(kernel, "beside", [kept, received], [((rows, 2 * width), F32)])[0]


def tied(x, *after):
    return lax.optimization_barrier((x, *after))[0]


def paired(x, gather, by, before=()):
    return x + in_plane(tied(x, *before), gather, lambda place: place ^ by)


def local(conv_input, gate_value, out_grad, out_weight, filters):
    signal, gating, grads = conv_input[0], gate_value[0], out_grad[0]
    length, channels = signal.shape
    halo_sent = signal[length - TAPS :]
    signal, gating, filters, weight = (
        resident(x) for x in (signal, gating, filters, out_weight)
    )
    tokens_all = lax.axis_size("dp") * lax.axis_size("ctx") * length
    shifts = range(1, SIDE)

    late = moved(grads, "half")
    previous = shifted(halo_sent, 1)
    early_other = moved(grads, "core")
    grads = resident(grads)
    early = pack(grads, early_other)
    early_got = [stepped(early[1], True, 1), stepped(early[3], True, 3)]
    response, kept, *given = forward(filters, previous, signal, gating)
    gated = join(kept, [moved(part, "core") for part in given], early_got)
    got = [stepped(gated, True, 1), stepped(gated, True, 3)]
    conv_early, gate_early = project(grads, early_other, weight, gating, response)

    late_other = moved(tied(late, conv_early), "core")
    own_late, *late_sent = relay(late, late_other, *got, early[2])
    conv_grad, grad_gate = project(
        late, late_other, weight, gating, response, (conv_early, gate_early), (own_late,)
    )
    late_got = [stepped(late_sent[s - 1], True, s) for s in shifts]
    filter_sum = filter_grad(previous, signal, conv_grad, ())
    parts = weight_parts([early[0], *early_got], own_late, gated, got, late_got, (filter_sum,))

    filter_sum = four_sum([filter_sum] + [stepped(filter_sum, True, s) for s in shifts])
    filter_sum = tied(filter_sum, parts[0])
    filter_sum = four_sum([filter_sum] + [stepped(filter_sum, False, s) for s in shifts])
    parts = [parts[0]] + [stepped(parts[s], False, s) for s in shifts]
    sums, own_filter = first_sum(parts, filter_sum, ())
    following = shifted(tied(conv_grad[:TAPS], filter_sum), -1)
    grad_input = input_grad(filters, conv_grad, following, (sums[0],))
    line = [[(i, (i + s) % SIDE) for i in range(SIDE)] for s in shifts]
    sums = [sums[0]] + [lax.ppermute(sums[s], "dp", line[s - 1]) for s in shifts]
    kept, given, grad_filter = last_sum(
        sums,
        own_filter,
        filters,
        1.0 / math.sqrt(tokens_all),
        1.0 / math.sqrt(tokens_all * GROUP),
        (resident(grad_input),),
    )
    grad_weight = beside(kept, moved(given, "core"))
    return (grad_input[None], grad_gate[None], grad_weight, grad_filter)


def solution(mesh):
    placed = (
        P("dp", "ctx", "tp"),
        P("dp", "ctx", "tp"),
        P("dp", ("ctx", "tp"), None),
        P(None, "tp"),
        P("tp", None),
    )
    return jax.shard_map(
        local,
        mesh=mesh,
        in_specs=placed,
        out_specs=(
            P("dp", "ctx", "tp"),
            P("dp", "ctx", "tp"),
            P(("dp", "ctx"), "tp"),
            P("tp", None),
        ),
        check_vma=False,
    )
```

```python
import math

import jax
import jax.numpy as jnp
from jax import lax
from jax.experimental import pallas as pl
from jax.experimental.pallas import tpu as pltpu
from jax.sharding import PartitionSpec as P

F32 = jnp.float32
BF16 = jnp.bfloat16
SIDE = 4
TAPS = 128
GROUP = 16
LANES = 128
PER_TILE = LANES // GROUP
WIDE = 256


def room(mebibytes):
    return pltpu.CompilerParams(vmem_limit_bytes=mebibytes * 1024 * 1024)


def spot():
    ctx = lax.axis_index("ctx")
    tp = lax.axis_index("tp")
    return ctx // SIDE, ctx % SIDE, lax.axis_index("dp"), tp // 2, tp % 2


def moved(x, axis):
    step = 2 if axis == "half" else 1
    return lax.ppermute(x, "tp", [(i, i ^ step) for i in range(4)])


def in_plane(x, gather, target):
    pairs = []
    for i in range(SIDE * SIDE):
        for j in range(4):
            place_x, place_y = divmod(i, SIDE)
            if (j % 2 == 0) == gather:
                place_x = target(place_x)
            else:
                place_y = target(place_y)
            pairs.append((i * 4 + j, (place_x * SIDE + place_y) * 4 + j))
    return lax.ppermute(x, ("ctx", "tp"), pairs)


def stepped(x, gather, by):
    return in_plane(x, gather, lambda place: (place + by) % SIDE)


def shifted(x, by):
    devices = lax.axis_size("ctx")
    return lax.ppermute(x, "ctx", [(i, i + by) for i in range(devices) if 0 <= i + by < devices])


ANYWHERE = pl.BlockSpec(memory_space=pl.ANY)
HALF = LANES // 2


def resident(x):
    return pltpu.with_memory_space_constraint(x, pltpu.HBM)


def whole(shape, place=None):
    place = place or (0,) * len(shape)
    return pl.BlockSpec(tuple(shape), lambda i: place, pipeline_mode=pl.Buffered(1))


def full(shape):
    return pl.BlockSpec(tuple(shape), lambda i: (0,) * len(shape))


def tile(rows, width):
    return pl.BlockSpec((rows, width), lambda i: (0, i))


def iota(shape, dim):
    return lax.broadcasted_iota(jnp.int32, shape, dim)


def aligned(index, size):
    return pl.ds(pl.multiple_of(index * size, size), size)


def lasting(microseconds):
    return pl.CostEstimate(flops=int(microseconds * 1e9), bytes_accessed=0, transcendentals=0)


def once(kernel, name, ins, outs, scratch=(), after=(), lasts=0):
    def body(*refs):
        kernel(*refs[: len(ins)], *refs[len(ins) + len(after) :])

    specs = [i[1] if isinstance(i, tuple) else whole(i.shape) for i in ins]
    arrays = [i[0] if isinstance(i, tuple) else i for i in ins]
    return pl.pallas_call(
        body,
        grid=(1,),
        in_specs=specs + [ANYWHERE] * len(after),
        out_specs=[whole(shape) for shape, _ in outs],
        out_shape=[jax.ShapeDtypeStruct(shape, dtype) for shape, dtype in outs],
        scratch_shapes=list(scratch),
        compiler_params=room(20),
        cost_estimate=lasting(lasts),
        name=name,
    )(*arrays, *after)


def first_rows(filters, shifted_by):
    lane, tap = iota((TAPS, 2 * TAPS), 1), iota((TAPS, 2 * TAPS), 0)
    place = lane == (TAPS - tap if shifted_by else tap)
    return jnp.dot(filters, place.astype(F32).astype(BF16), preferred_element_type=F32)


def banded(rows, stack):
    for g in range(PER_TILE):
        first = jnp.broadcast_to(rows[g : g + 1], (TAPS, 2 * TAPS))
        skewed = pltpu.roll(first, 0, 1, stride=1, stride_axis=0)
        stack[g * TAPS : (g + 1) * TAPS, :] = skewed.astype(BF16)


def lane_group(shape):
    return iota(shape, len(shape) - 1) % LANES // GROUP


def own_lanes(stacked):
    group = lane_group((TAPS, 2 * LANES))
    chosen = jnp.zeros((TAPS, 2 * LANES), F32)
    for g in range(PER_TILE):
        chosen = jnp.where(group == g, stacked[g * TAPS : (g + 1) * TAPS], chosen)
    return chosen


def two_windows(first, second, third):
    upper = jnp.concatenate([first, second], 1)
    lower = jnp.concatenate([second, third], 1)
    return jnp.concatenate([upper, lower], 0)


def forward_kernel(filters, previous, signal, gating, response, kept, *refs):
    given, gated, stack = refs[:2], refs[2], refs[3]
    _, _, _, _, core = spot()
    rows = first_rows(filters[...], True)
    for i in range(signal.shape[1] // LANES):
        columns = slice(i * LANES, (i + 1) * LANES)
        band = stack.at[i % 2]
        banded(rows[i * PER_TILE : (i + 1) * PER_TILE], band)
        window = two_windows(previous[:, columns], signal[:TAPS, columns], signal[TAPS:, columns])
        made = own_lanes(jnp.dot(band[...], window, preferred_element_type=F32))
        for block in range(2):
            tokens = slice(block * TAPS, (block + 1) * TAPS)
            part = made[:, block * LANES : (block + 1) * LANES]
            response[tokens, columns] = part
            gated[tokens, columns] = (part * gating[tokens, columns].astype(F32)).astype(BF16)
    kept[...] = gated[:, aligned(core, kept.shape[1])]
    for i, out in enumerate(given):
        out[...] = gated[i * TAPS : (i + 1) * TAPS, aligned(1 - core, kept.shape[1])]


def forward(filters, previous, signal, gating):
    length, channels = signal.shape
    quarter = ((TAPS, channels // 2), BF16)
    return once(
        forward_kernel,
        "conv_forward",
        [filters, previous, signal, gating],
        [((length, channels), F32), ((length, channels // 2), BF16), quarter, quarter],
        [
            pltpu.VMEM((length, channels), BF16),
            pltpu.VMEM((2, PER_TILE * TAPS, 2 * TAPS), BF16),
        ],
    )


def join_kernel(kept, upper, lower, gated):
    _, _, _, _, core = spot()
    width = kept.shape[1]
    gated[: 2 * TAPS, aligned(core, width)] = kept[...]
    gated[:TAPS, aligned(1 - core, width)] = upper[...]
    gated[TAPS : 2 * TAPS, aligned(1 - core, width)] = lower[...]
    gated[2 * TAPS :] = gated[: gated.shape[0] - 2 * TAPS]


def join(kept, received, after):
    length, width = kept.shape
    shape = (length + 16, 2 * width)
    return once(join_kernel, "join", [kept, *received], [(shape, BF16)], (), after)[0]


def input_grad_kernel(filters, conv_grad, following, grad_input, stack):
    rows = first_rows(filters[...], False)
    for i in range(conv_grad.shape[1] // LANES):
        columns = slice(i * LANES, (i + 1) * LANES)
        band = stack.at[i % 2]
        banded(rows[i * PER_TILE : (i + 1) * PER_TILE], band)
        window = two_windows(
            conv_grad[:TAPS, columns], conv_grad[TAPS:, columns], following[:, columns]
        )
        made = own_lanes(jnp.dot(band[...], window, preferred_element_type=F32))
        for block in range(2):
            grad_input[block * TAPS : (block + 1) * TAPS, columns] = made[
                :, block * LANES : (block + 1) * LANES
            ].astype(BF16)


def input_grad(filters, conv_grad, following, after):
    return once(
        input_grad_kernel,
        "input_grad",
        [filters, conv_grad, following],
        [(conv_grad.shape, BF16)],
        [pltpu.VMEM((2, PER_TILE * TAPS, 2 * TAPS), BF16)],
        after,
    )[0]


def filter_grad_kernel(previous, signal, conv_grad, grad_filter, stack):
    square = (2 * TAPS, 2 * TAPS)
    turn = iota(square, 0) == (2 * TAPS - iota(square, 1)) % (2 * TAPS)
    turn = turn.astype(F32).astype(BF16)
    group = lane_group((TAPS, 2 * LANES))
    for i in range(signal.shape[1] // LANES):
        columns = slice(i * LANES, (i + 1) * LANES)
        masked = stack.at[i % 2]
        inputs = two_windows(previous[:, columns], signal[:TAPS, columns], signal[TAPS:, columns])
        turned = jnp.dot(turn, inputs, preferred_element_type=F32).astype(BF16)
        both = jnp.concatenate([conv_grad[:TAPS, columns], conv_grad[TAPS:, columns]], 1)
        both = both.astype(F32)
        for g in range(PER_TILE):
            masked[g * TAPS : (g + 1) * TAPS, :] = jnp.where(group == g, both, 0.0).astype(BF16)
        products = lax.dot_general(
            masked[...], turned, (((1,), (1,)), ((), ())), preferred_element_type=F32
        )
        for g in range(PER_TILE):
            skewed = pltpu.roll(products[g * TAPS : (g + 1) * TAPS], 0, 1, stride=1, stride_axis=0)
            row = i * PER_TILE + g
            grad_filter[row : row + 1, :] = jnp.sum(skewed[:, TAPS:], axis=0, keepdims=True)


def filter_grad(previous, signal, conv_grad, after):
    return once(
        filter_grad_kernel,
        "filter_grad",
        [previous, signal, conv_grad],
        [((signal.shape[1] // GROUP, TAPS), F32)],
        [pltpu.VMEM((2, PER_TILE * TAPS, 2 * TAPS), BF16)],
        after,
        4,
    )[0]


def pack_into(mine, other, outs):
    x, y, _, _, core = spot()
    part = mine.shape[0]
    depth = mine.shape[1] // SIDE

    @pl.when(core == 0)
    def _():
        for ref, rows in ((mine, slice(0, part)), (other, slice(part, 2 * part))):
            for s, out in enumerate(outs):
                for d in range(SIDE):
                    start = pl.multiple_of(d * depth + (x + s) % SIDE * WIDE, WIDE)
                    out[rows, d * WIDE : (d + 1) * WIDE] = ref[:, pl.ds(start, WIDE)]

    @pl.when(core == 1)
    def _():
        lower = iota((part, LANES), 1) < HALF
        for ref, rows in ((other, slice(0, part)), (mine, slice(part, 2 * part))):
            for s, out in enumerate(outs):
                to = (y + s) % SIDE
                upper_half = jnp.broadcast_to(to % 2, (part, LANES)) == 1
                for pair in range(2 * SIDE):
                    runs = []
                    for i in range(2):
                        start = pl.multiple_of((2 * pair + i) * WIDE + to // 2 * LANES, LANES)
                        runs.append(ref[:, pl.ds(start, LANES)].astype(F32))
                    first = jnp.where(upper_half, pltpu.roll(runs[0], HALF, 1), runs[0])
                    second = jnp.where(upper_half, runs[1], pltpu.roll(runs[1], HALF, 1))
                    both = jnp.where(lower, first, second).astype(BF16)
                    out[rows, pair * LANES : (pair + 1) * LANES] = both


def pack_kernel(mine, other, *outs):
    pack_into(mine, other, outs)


def pack(mine, other):
    rows, width = mine.shape
    return once(
        pack_kernel, "pack", [mine, other], [((2 * rows, width // SIDE), BF16)] * SIDE
    )


def relay_kernel(mine, other, before, after, opposite, *outs):
    pack_into(mine, other, outs)
    part = opposite.shape[0]
    outs[1][part:] = before[...]
    outs[2][part:] = opposite[...]
    outs[3][part:] = after[...]


def relay(mine, other, got_next, got_last, opposite):
    rows, width = opposite.shape
    return once(
        relay_kernel,
        "relay",
        [
            mine,
            other,
            (got_next, whole((TAPS, width))),
            (got_last, whole((TAPS, width), (1, 0))),
            opposite,
        ],
        [((rows, width), BF16)] + [((rows + TAPS, width), BF16)] * (SIDE - 1),
    )


def project_kernel(early, early_other, late, late_other, weight, gating, response, conv_grad, grad_gate, rows):
    _, _, _, half, core = spot()
    part = early.shape[0]

    @pl.when(pl.program_id(0) == 0)
    def _():
        for ref, h, c in (
            (early, half, core),
            (early_other, half, 1 - core),
            (late, 1 - half, core),
            (late_other, 1 - half, 1 - core),
        ):
            rows[aligned(2 * h + c, part), :] = ref[...]

    made = jnp.dot(rows[...], weight[...], preferred_element_type=F32)
    conv_grad[...] = (made * gating[...].astype(F32)).astype(BF16)
    grad_gate[...] = (made * response[...]).astype(BF16)


def project(early, early_other, late, late_other, weight, gating, response, after):
    length, channels = gating.shape
    depth = weight.shape[0]

    def body(*refs):
        project_kernel(*refs[:7], *refs[7 + len(after) :])

    return pl.pallas_call(
        body,
        grid=(channels // WIDE,),
        in_specs=[full(early.shape)] * 4
        + [tile(depth, WIDE), tile(length, WIDE), tile(length, WIDE)]
        + [ANYWHERE] * len(after),
        out_specs=[tile(length, WIDE)] * 2,
        out_shape=[jax.ShapeDtypeStruct((length, channels), BF16)] * 2,
        scratch_shapes=[pltpu.VMEM((length, depth), BF16)],
        compiler_params=room(20),
        cost_estimate=lasting(6),
        name="project",
    )(early, early_other, late, late_other, weight, gating, response, *after)


def weight_kernel(*refs):
    early, late = refs[:SIDE], refs[SIDE : 2 * SIDE]
    gated, got_next, before, after, got_last = refs[2 * SIDE : 2 * SIDE + 5]
    outs, turned, tokens = refs[-2 - SIDE : -2], refs[-2], refs[-1]
    x, y, _, half, core = spot()
    me = jnp.where(core == 0, y, x)
    upper = jnp.broadcast_to(half, before.shape) == 0
    opposite = (before[...].astype(F32), after[...].astype(F32))
    for i, (parts, h) in enumerate(((early, half), (late, 1 - half))):
        rows = aligned(h, TAPS)
        halves = opposite if i == 0 else opposite[::-1]
        blocks = (
            gated[rows, :],
            got_next[rows, :],
            jnp.where(upper, *halves).astype(BF16),
            got_last[rows, :],
        )
        for s in range(SIDE):
            at = slice((i * SIDE + s) * TAPS, (i * SIDE + s + 1) * TAPS)
            tokens[at] = blocks[s]
            transposed = parts[s][...].T
            for d in range(SIDE):
                for q in range(SIDE):
                    to = (q - me + SIDE) % SIDE * WIDE + d * HALF
                    start = d * WIDE + q * HALF
                    turned[pl.ds(pl.multiple_of(to, HALF), HALF), at] = transposed[
                        start : start + HALF
                    ]
    for s, out in enumerate(outs):
        features = turned[s * WIDE : (s + 1) * WIDE]
        out[...] = jnp.dot(features, tokens[...], preferred_element_type=F32).astype(out.dtype)


def weight_parts(early, own_late, gated, got, late, after):
    width = gated.shape[1]
    rows = own_late.shape[0]
    length = 2 * rows

    def block(array, start, count=rows):
        return array, whole((count, width), (start // count, 0))

    shape = (width // SIDE, width)
    return once(
        weight_kernel,
        "weight_parts",
        [
            early[0],
            early[1],
            block(late[1], rows),
            early[2],
            own_late,
            *[block(part, 0) for part in late],
            block(gated, 0, length),
            block(got[0], 0, length),
            block(late[0], rows),
            block(late[2], rows),
            block(got[1], 0, length),
        ],
        [(shape, F32)] + [(shape, BF16)] * (SIDE - 1),
        [pltpu.VMEM((width, 2 * SIDE * rows), BF16), pltpu.VMEM((2 * SIDE * rows, width), BF16)],
        after,
        4,
    )


def first_sum_kernel(*refs):
    _, _, z, _, _ = spot()
    outs, kept = refs[SIDE:-1], refs[-1]
    run = kept.shape[0] // SIDE
    total = refs[0][...]
    for ref in refs[1:SIDE]:
        total = total + ref[...].astype(F32)
    for d in range(SIDE):
        kept[aligned((d - z + SIDE) % SIDE, run), :] = total[d * run : (d + 1) * run]
    for s, out in enumerate(outs):
        out[...] = kept[s * run : (s + 1) * run, :].astype(out.dtype)


def first_sum(parts, after):
    rows, width = parts[0].shape
    run = rows // SIDE
    return once(
        first_sum_kernel,
        "first_sum",
        parts,
        [((run, width), F32)] + [((run, width), BF16)] * (SIDE - 1),
        [pltpu.VMEM((rows, width), F32)],
        after,
        1,
    )


def last_sum(parts, scale, after):
    rows, width = parts[0].shape

    def kernel(*refs):
        kept, given, summed = refs[SIDE:]
        _, _, _, _, core = spot()
        total = refs[0][...]
        for ref in refs[1:SIDE]:
            total = total + ref[...].astype(F32)
        summed[...] = total * scale
        kept[...] = summed[:, aligned(core, width // 2)]
        given[...] = summed[:, aligned(1 - core, width // 2)]

    half = ((rows, width // 2), F32)
    return once(
        kernel, "last_sum", parts, [half, half], [pltpu.VMEM((rows, width), F32)], after
    )


def beside(kept, received):
    def kernel(first, second, out):
        _, _, _, _, core = spot()
        out[:, aligned(core, first.shape[1])] = first[...]
        out[:, aligned(1 - core, first.shape[1])] = second[...]

    rows, width = kept.shape
    return once(kernel, "beside", [kept, received], [((rows, 2 * width), F32)])[0]


def tied(x, *after):
    return lax.optimization_barrier((x, *after))[0]


def paired(x, gather, by, before=()):
    return x + in_plane(tied(x, *before), gather, lambda place: place ^ by)


def paired_z(x, by):
    return x + lax.ppermute(x, "dp", [(i, i ^ by) for i in range(SIDE)])


def local(conv_input, gate_value, out_grad, out_weight, filters):
    signal, gating, grads = conv_input[0], gate_value[0], out_grad[0]
    length, channels = signal.shape
    halo_sent = signal[length - TAPS :]
    signal, gating, filters, weight = (
        resident(x) for x in (signal, gating, filters, out_weight)
    )
    tokens_all = lax.axis_size("dp") * lax.axis_size("ctx") * length
    shifts = range(1, SIDE)

    late = moved(grads, "half")
    previous = shifted(halo_sent, 1)
    early_other = moved(grads, "core")
    grads = resident(grads)
    early = pack(grads, early_other)
    early_got = [stepped(early[1], True, 1), stepped(early[3], True, 3)]
    response, kept, *given = forward(filters, previous, signal, gating)
    gated = join(kept, [moved(part, "core") for part in given], early_got)
    got = [stepped(gated, True, 1), stepped(gated, True, 3)]
    late_other = moved(tied(late, gated), "core")
    own_late, *late_sent = relay(late, late_other, *got, early[2])
    conv_grad, grad_gate = project(
        grads, early_other, late, late_other, weight, gating, response, (own_late,)
    )
    late_got = [stepped(late_sent[s - 1], True, s) for s in shifts]
    filter_sum = filter_grad(previous, signal, conv_grad, ())
    parts = weight_parts([early[0], *early_got], own_late, gated, got, late_got, (filter_sum,))

    filter_sum = paired_z(paired_z(tied(filter_sum, parts[0]), 1), 2)
    following = shifted(tied(conv_grad[:TAPS], filter_sum), -1)
    filter_sum = paired(paired(filter_sum, True, 1), True, 2)
    parts = [parts[0]] + [stepped(parts[s], False, s) for s in shifts]
    sums = first_sum(parts, (filter_sum,))
    filter_sum = paired(paired(filter_sum, False, 1, (sums[0],)), False, 2)
    grad_filter = filter_sum * (1.0 / math.sqrt(tokens_all * GROUP))
    grad_input = input_grad(filters, conv_grad, following, (sums[0],))
    line = [[(i, (i + s) % SIDE) for i in range(SIDE)] for s in shifts]
    sums = [sums[0]] + [lax.ppermute(sums[s], "dp", line[s - 1]) for s in shifts]
    kept, given = last_sum(sums, 1.0 / math.sqrt(tokens_all), (resident(grad_input),))
    grad_weight = beside(kept, moved(given, "core"))
    return (grad_input[None], grad_gate[None], grad_weight, grad_filter)


def solution(mesh):
    placed = (
        P("dp", "ctx", "tp"),
        P("dp", "ctx", "tp"),
        P("dp", ("ctx", "tp"), None),
        P(None, "tp"),
        P("tp", None),
    )
    return jax.shard_map(
        local,
        mesh=mesh,
        in_specs=placed,
        out_specs=(
            P("dp", "ctx", "tp"),
            P("dp", "ctx", "tp"),
            P(("dp", "ctx"), "tp"),
            P("tp", None),
        ),
        check_vma=False,
    )
```

```python
import math

import jax
import jax.numpy as jnp
from jax import lax
from jax.experimental import pallas as pl
from jax.experimental.pallas import tpu as pltpu
from jax.sharding import PartitionSpec as P

F32 = jnp.float32
BF16 = jnp.bfloat16
SIDE = 4
TAPS = 128
GROUP = 16
LANES = 128
PER_TILE = LANES // GROUP
WIDE = 256


def room(mebibytes):
    return pltpu.CompilerParams(vmem_limit_bytes=mebibytes * 1024 * 1024)


def spot():
    ctx = lax.axis_index("ctx")
    tp = lax.axis_index("tp")
    return ctx // SIDE, ctx % SIDE, lax.axis_index("dp"), tp // 2, tp % 2


def moved(x, axis):
    step = 2 if axis == "half" else 1
    return lax.ppermute(x, "tp", [(i, i ^ step) for i in range(4)])


def in_plane(x, gather, target):
    pairs = []
    for i in range(SIDE * SIDE):
        for j in range(4):
            place_x, place_y = divmod(i, SIDE)
            if (j % 2 == 0) == gather:
                place_x = target(place_x)
            else:
                place_y = target(place_y)
            pairs.append((i * 4 + j, (place_x * SIDE + place_y) * 4 + j))
    return lax.ppermute(x, ("ctx", "tp"), pairs)


def stepped(x, gather, by):
    return in_plane(x, gather, lambda place: (place + by) % SIDE)


def shifted(x, by):
    devices = lax.axis_size("ctx")
    return lax.ppermute(x, "ctx", [(i, i + by) for i in range(devices) if 0 <= i + by < devices])


ANYWHERE = pl.BlockSpec(memory_space=pl.ANY)
HALF = LANES // 2


def resident(x):
    return pltpu.with_memory_space_constraint(x, pltpu.HBM)


def whole(shape, place=None):
    place = place or (0,) * len(shape)
    return pl.BlockSpec(tuple(shape), lambda i: place, pipeline_mode=pl.Buffered(1))


def full(shape):
    return pl.BlockSpec(tuple(shape), lambda i: (0,) * len(shape))


def tile(rows, width):
    return pl.BlockSpec((rows, width), lambda i: (0, i))


def iota(shape, dim):
    return lax.broadcasted_iota(jnp.int32, shape, dim)


def aligned(index, size):
    return pl.ds(pl.multiple_of(index * size, size), size)


def lasting(microseconds):
    return pl.CostEstimate(flops=int(microseconds * 1e9), bytes_accessed=0, transcendentals=0)


def once(kernel, name, ins, outs, scratch=(), after=(), lasts=0):
    def body(*refs):
        kernel(*refs[: len(ins)], *refs[len(ins) + len(after) :])

    specs = [i[1] if isinstance(i, tuple) else whole(i.shape) for i in ins]
    arrays = [i[0] if isinstance(i, tuple) else i for i in ins]
    return pl.pallas_call(
        body,
        grid=(1,),
        in_specs=specs + [ANYWHERE] * len(after),
        out_specs=[whole(shape) for shape, _ in outs],
        out_shape=[jax.ShapeDtypeStruct(shape, dtype) for shape, dtype in outs],
        scratch_shapes=list(scratch),
        compiler_params=room(20),
        cost_estimate=lasting(lasts),
        name=name,
    )(*arrays, *after)


def first_rows(filters, shifted_by):
    lane, tap = iota((TAPS, 2 * TAPS), 1), iota((TAPS, 2 * TAPS), 0)
    place = lane == (TAPS - tap if shifted_by else tap)
    return jnp.dot(filters, place.astype(F32).astype(BF16), preferred_element_type=F32)


def banded(rows, stack):
    for g in range(PER_TILE):
        first = jnp.broadcast_to(rows[g : g + 1], (TAPS, 2 * TAPS))
        skewed = pltpu.roll(first, 0, 1, stride=1, stride_axis=0)
        stack[g * TAPS : (g + 1) * TAPS, :] = skewed.astype(BF16)


def lane_group(shape):
    return iota(shape, len(shape) - 1) % LANES // GROUP


def own_lanes(stacked):
    group = lane_group((TAPS, 2 * LANES))
    chosen = jnp.zeros((TAPS, 2 * LANES), F32)
    for g in range(PER_TILE):
        chosen = jnp.where(group == g, stacked[g * TAPS : (g + 1) * TAPS], chosen)
    return chosen


def two_windows(first, second, third):
    upper = jnp.concatenate([first, second], 1)
    lower = jnp.concatenate([second, third], 1)
    return jnp.concatenate([upper, lower], 0)


def forward_kernel(filters, previous, signal, gating, response, kept, *refs):
    given, gated, stack = refs[:2], refs[2], refs[3]
    _, _, _, _, core = spot()
    rows = first_rows(filters[...], True)
    for i in range(signal.shape[1] // LANES):
        columns = slice(i * LANES, (i + 1) * LANES)
        band = stack.at[i % 2]
        banded(rows[i * PER_TILE : (i + 1) * PER_TILE], band)
        window = two_windows(previous[:, columns], signal[:TAPS, columns], signal[TAPS:, columns])
        made = own_lanes(jnp.dot(band[...], window, preferred_element_type=F32))
        for block in range(2):
            tokens = slice(block * TAPS, (block + 1) * TAPS)
            part = made[:, block * LANES : (block + 1) * LANES]
            response[tokens, columns] = part
            gated[tokens, columns] = (part * gating[tokens, columns].astype(F32)).astype(BF16)
    kept[...] = gated[:, aligned(core, kept.shape[1])]
    for i, out in enumerate(given):
        out[...] = gated[i * TAPS : (i + 1) * TAPS, aligned(1 - core, kept.shape[1])]


def forward(filters, previous, signal, gating):
    length, channels = signal.shape
    quarter = ((TAPS, channels // 2), BF16)
    return once(
        forward_kernel,
        "conv_forward",
        [filters, previous, signal, gating],
        [((length, channels), F32), ((length, channels // 2), BF16), quarter, quarter],
        [
            pltpu.VMEM((length, channels), BF16),
            pltpu.VMEM((2, PER_TILE * TAPS, 2 * TAPS), BF16),
        ],
    )


def join_kernel(kept, upper, lower, gated):
    _, _, _, _, core = spot()
    width = kept.shape[1]
    gated[: 2 * TAPS, aligned(core, width)] = kept[...]
    gated[:TAPS, aligned(1 - core, width)] = upper[...]
    gated[TAPS : 2 * TAPS, aligned(1 - core, width)] = lower[...]
    gated[2 * TAPS :] = gated[: gated.shape[0] - 2 * TAPS]


def join(kept, received, after):
    length, width = kept.shape
    shape = (length + 16, 2 * width)
    return once(join_kernel, "join", [kept, *received], [(shape, BF16)], (), after)[0]


def input_grad_kernel(filters, conv_grad, following, grad_input, stack):
    rows = first_rows(filters[...], False)
    for i in range(conv_grad.shape[1] // LANES):
        columns = slice(i * LANES, (i + 1) * LANES)
        band = stack.at[i % 2]
        banded(rows[i * PER_TILE : (i + 1) * PER_TILE], band)
        window = two_windows(
            conv_grad[:TAPS, columns], conv_grad[TAPS:, columns], following[:, columns]
        )
        made = own_lanes(jnp.dot(band[...], window, preferred_element_type=F32))
        for block in range(2):
            grad_input[block * TAPS : (block + 1) * TAPS, columns] = made[
                :, block * LANES : (block + 1) * LANES
            ].astype(BF16)


def input_grad(filters, conv_grad, following, after):
    return once(
        input_grad_kernel,
        "input_grad",
        [filters, conv_grad, following],
        [(conv_grad.shape, BF16)],
        [pltpu.VMEM((2, PER_TILE * TAPS, 2 * TAPS), BF16)],
        after,
    )[0]


def filter_grad_kernel(previous, signal, conv_grad, grad_filter, stack):
    square = (2 * TAPS, 2 * TAPS)
    turn = iota(square, 0) == (2 * TAPS - iota(square, 1)) % (2 * TAPS)
    turn = turn.astype(F32).astype(BF16)
    group = lane_group((TAPS, 2 * LANES))
    for i in range(signal.shape[1] // LANES):
        columns = slice(i * LANES, (i + 1) * LANES)
        masked = stack.at[i % 2]
        inputs = two_windows(previous[:, columns], signal[:TAPS, columns], signal[TAPS:, columns])
        turned = jnp.dot(turn, inputs, preferred_element_type=F32).astype(BF16)
        both = jnp.concatenate([conv_grad[:TAPS, columns], conv_grad[TAPS:, columns]], 1)
        both = both.astype(F32)
        for g in range(PER_TILE):
            masked[g * TAPS : (g + 1) * TAPS, :] = jnp.where(group == g, both, 0.0).astype(BF16)
        products = lax.dot_general(
            masked[...], turned, (((1,), (1,)), ((), ())), preferred_element_type=F32
        )
        for g in range(PER_TILE):
            skewed = pltpu.roll(products[g * TAPS : (g + 1) * TAPS], 0, 1, stride=1, stride_axis=0)
            row = i * PER_TILE + g
            grad_filter[row : row + 1, :] = jnp.sum(skewed[:, TAPS:], axis=0, keepdims=True)


def filter_grad(previous, signal, conv_grad, after):
    return once(
        filter_grad_kernel,
        "filter_grad",
        [previous, signal, conv_grad],
        [((signal.shape[1] // GROUP, TAPS), F32)],
        [pltpu.VMEM((2, PER_TILE * TAPS, 2 * TAPS), BF16)],
        after,
        4,
    )[0]


def pack_into(mine, other, outs):
    x, y, _, _, core = spot()
    part = mine.shape[0]
    depth = mine.shape[1] // SIDE

    @pl.when(core == 0)
    def _():
        for ref, rows in ((mine, slice(0, part)), (other, slice(part, 2 * part))):
            for s, out in enumerate(outs):
                for d in range(SIDE):
                    start = pl.multiple_of(d * depth + (x + s) % SIDE * WIDE, WIDE)
                    out[rows, d * WIDE : (d + 1) * WIDE] = ref[:, pl.ds(start, WIDE)]

    @pl.when(core == 1)
    def _():
        lower = iota((part, LANES), 1) < HALF
        for ref, rows in ((other, slice(0, part)), (mine, slice(part, 2 * part))):
            for s, out in enumerate(outs):
                to = (y + s) % SIDE
                upper_half = jnp.broadcast_to(to % 2, (part, LANES)) == 1
                for pair in range(2 * SIDE):
                    runs = []
                    for i in range(2):
                        start = pl.multiple_of((2 * pair + i) * WIDE + to // 2 * LANES, LANES)
                        runs.append(ref[:, pl.ds(start, LANES)].astype(F32))
                    first = jnp.where(upper_half, pltpu.roll(runs[0], HALF, 1), runs[0])
                    second = jnp.where(upper_half, runs[1], pltpu.roll(runs[1], HALF, 1))
                    both = jnp.where(lower, first, second).astype(BF16)
                    out[rows, pair * LANES : (pair + 1) * LANES] = both


def pack_kernel(mine, other, *outs):
    pack_into(mine, other, outs)


def pack(mine, other):
    rows, width = mine.shape
    return once(
        pack_kernel, "pack", [mine, other], [((2 * rows, width // SIDE), BF16)] * SIDE
    )


def relay_kernel(mine, other, before, after, opposite, *outs):
    pack_into(mine, other, outs)
    part = opposite.shape[0]
    outs[1][part:] = before[...]
    outs[2][part:] = opposite[...]
    outs[3][part:] = after[...]


def relay(mine, other, got_next, got_last, opposite):
    rows, width = opposite.shape
    return once(
        relay_kernel,
        "relay",
        [
            mine,
            other,
            (got_next, whole((TAPS, width))),
            (got_last, whole((TAPS, width), (1, 0))),
            opposite,
        ],
        [((rows, width), BF16)] + [((rows + TAPS, width), BF16)] * (SIDE - 1),
    )


def project_kernel(early, early_other, late, late_other, weight, gating, response, conv_grad, grad_gate, rows):
    _, _, _, half, core = spot()
    part = early.shape[0]

    @pl.when(pl.program_id(0) == 0)
    def _():
        for ref, h, c in (
            (early, half, core),
            (early_other, half, 1 - core),
            (late, 1 - half, core),
            (late_other, 1 - half, 1 - core),
        ):
            rows[aligned(2 * h + c, part), :] = ref[...]

    made = jnp.dot(rows[...], weight[...], preferred_element_type=F32)
    conv_grad[...] = (made * gating[...].astype(F32)).astype(BF16)
    grad_gate[...] = (made * response[...]).astype(BF16)


def project(early, early_other, late, late_other, weight, gating, response, after):
    length, channels = gating.shape
    depth = weight.shape[0]

    def body(*refs):
        project_kernel(*refs[:7], *refs[7 + len(after) :])

    return pl.pallas_call(
        body,
        grid=(channels // WIDE,),
        in_specs=[full(early.shape)] * 4
        + [tile(depth, WIDE), tile(length, WIDE), tile(length, WIDE)]
        + [ANYWHERE] * len(after),
        out_specs=[tile(length, WIDE)] * 2,
        out_shape=[jax.ShapeDtypeStruct((length, channels), BF16)] * 2,
        scratch_shapes=[pltpu.VMEM((length, depth), BF16)],
        compiler_params=room(20),
        cost_estimate=lasting(6),
        name="project",
    )(early, early_other, late, late_other, weight, gating, response, *after)


def weight_kernel(*refs):
    early, late = refs[:SIDE], refs[SIDE : 2 * SIDE]
    gated, got_next, before, after, got_last = refs[2 * SIDE : 2 * SIDE + 5]
    outs, turned, tokens = refs[-2 - SIDE : -2], refs[-2], refs[-1]
    x, y, _, half, core = spot()
    me = jnp.where(core == 0, y, x)
    upper = jnp.broadcast_to(half, before.shape) == 0
    opposite = (before[...].astype(F32), after[...].astype(F32))
    for i, (parts, h) in enumerate(((early, half), (late, 1 - half))):
        rows = aligned(h, TAPS)
        halves = opposite if i == 0 else opposite[::-1]
        blocks = (
            gated[rows, :],
            got_next[rows, :],
            jnp.where(upper, *halves).astype(BF16),
            got_last[rows, :],
        )
        for s in range(SIDE):
            at = slice((i * SIDE + s) * TAPS, (i * SIDE + s + 1) * TAPS)
            tokens[at] = blocks[s]
            transposed = parts[s][...].T
            for d in range(SIDE):
                for q in range(SIDE):
                    to = (q - me + SIDE) % SIDE * WIDE + d * HALF
                    start = d * WIDE + q * HALF
                    turned[pl.ds(pl.multiple_of(to, HALF), HALF), at] = transposed[
                        start : start + HALF
                    ]
    for s, out in enumerate(outs):
        features = turned[s * WIDE : (s + 1) * WIDE]
        out[...] = jnp.dot(features, tokens[...], preferred_element_type=F32).astype(out.dtype)


def weight_parts(early, own_late, gated, got, late, after):
    width = gated.shape[1]
    rows = own_late.shape[0]
    length = 2 * rows

    def block(array, start, count=rows):
        return array, whole((count, width), (start // count, 0))

    shape = (width // SIDE, width)
    return once(
        weight_kernel,
        "weight_parts",
        [
            early[0],
            early[1],
            block(late[1], rows),
            early[2],
            own_late,
            *[block(part, 0) for part in late],
            block(gated, 0, length),
            block(got[0], 0, length),
            block(late[0], rows),
            block(late[2], rows),
            block(got[1], 0, length),
        ],
        [(shape, F32)] + [(shape, BF16)] * (SIDE - 1),
        [pltpu.VMEM((width, 2 * SIDE * rows), BF16), pltpu.VMEM((2 * SIDE * rows, width), BF16)],
        after,
        4,
    )


def first_sum_kernel(*refs):
    _, _, z, _, _ = spot()
    outs, kept = refs[SIDE:-1], refs[-1]
    run = kept.shape[0] // SIDE
    total = refs[0][...]
    for ref in refs[1:SIDE]:
        total = total + ref[...].astype(F32)
    for d in range(SIDE):
        kept[aligned((d - z + SIDE) % SIDE, run), :] = total[d * run : (d + 1) * run]
    for s, out in enumerate(outs):
        out[...] = kept[s * run : (s + 1) * run, :].astype(out.dtype)


def first_sum(parts, after):
    rows, width = parts[0].shape
    run = rows // SIDE
    return once(
        first_sum_kernel,
        "first_sum",
        parts,
        [((run, width), F32)] + [((run, width), BF16)] * (SIDE - 1),
        [pltpu.VMEM((rows, width), F32)],
        after,
        1,
    )


def last_sum(parts, scale, after):
    rows, width = parts[0].shape

    def kernel(*refs):
        kept, given, summed = refs[SIDE:]
        _, _, _, _, core = spot()
        total = refs[0][...]
        for ref in refs[1:SIDE]:
            total = total + ref[...].astype(F32)
        summed[...] = total * scale
        kept[...] = summed[:, aligned(core, width // 2)]
        given[...] = summed[:, aligned(1 - core, width // 2)]

    half = ((rows, width // 2), F32)
    return once(
        kernel, "last_sum", parts, [half, half], [pltpu.VMEM((rows, width), F32)], after
    )


def beside(kept, received):
    def kernel(first, second, out):
        _, _, _, _, core = spot()
        out[:, aligned(core, first.shape[1])] = first[...]
        out[:, aligned(1 - core, first.shape[1])] = second[...]

    rows, width = kept.shape
    return once(kernel, "beside", [kept, received], [((rows, 2 * width), F32)])[0]


def tied(x, *after):
    return lax.optimization_barrier((x, *after))[0]


def paired(x, gather, by, before=()):
    return x + in_plane(tied(x, *before), gather, lambda place: place ^ by)


def paired_z(x, by):
    return x + lax.ppermute(x, "dp", [(i, i ^ by) for i in range(SIDE)])


def local(conv_input, gate_value, out_grad, out_weight, filters):
    signal, gating, grads = conv_input[0], gate_value[0], out_grad[0]
    length, channels = signal.shape
    halo_sent = signal[length - TAPS :]
    signal, gating, filters, weight = (
        resident(x) for x in (signal, gating, filters, out_weight)
    )
    tokens_all = lax.axis_size("dp") * lax.axis_size("ctx") * length
    shifts = range(1, SIDE)

    late = moved(grads, "half")
    previous = shifted(halo_sent, 1)
    early_other = moved(grads, "core")
    grads = resident(grads)
    early = pack(grads, early_other)
    early_got = [stepped(early[1], True, 1), stepped(early[3], True, 3)]
    response, kept, *given = forward(filters, previous, signal, gating)
    gated = join(kept, [moved(part, "core") for part in given], early_got)
    got = [stepped(gated, True, 1), stepped(gated, True, 3)]
    late_other = moved(tied(late, gated), "core")
    own_late, *late_sent = relay(late, late_other, *got, early[2])
    conv_grad, grad_gate = project(
        grads, early_other, late, late_other, weight, gating, response, (own_late,)
    )
    late_got = [stepped(late_sent[s - 1], True, s) for s in shifts]
    filter_sum = paired(filter_grad(previous, signal, conv_grad, ()), True, 1)
    parts = weight_parts([early[0], *early_got], own_late, gated, got, late_got, (filter_sum,))

    filter_sum = paired_z(paired_z(tied(filter_sum, parts[0]), 1), 2)
    following = shifted(tied(conv_grad[:TAPS], filter_sum), -1)
    filter_sum = paired(filter_sum, True, 2)
    parts = [parts[0]] + [stepped(parts[s], False, s) for s in shifts]
    sums = first_sum(parts, (filter_sum,))
    filter_sum = paired(paired(filter_sum, False, 1, (sums[0],)), False, 2)
    grad_filter = filter_sum * (1.0 / math.sqrt(tokens_all * GROUP))
    grad_input = input_grad(filters, conv_grad, following, (sums[0],))
    line = [[(i, (i + s) % SIDE) for i in range(SIDE)] for s in shifts]
    sums = [sums[0]] + [lax.ppermute(sums[s], "dp", line[s - 1]) for s in shifts]
    kept, given = last_sum(sums, 1.0 / math.sqrt(tokens_all), (resident(grad_input),))
    grad_weight = beside(kept, moved(given, "core"))
    return (grad_input[None], grad_gate[None], grad_weight, grad_filter)


def solution(mesh):
    placed = (
        P("dp", "ctx", "tp"),
        P("dp", "ctx", "tp"),
        P("dp", ("ctx", "tp"), None),
        P(None, "tp"),
        P("tp", None),
    )
    return jax.shard_map(
        local,
        mesh=mesh,
        in_specs=placed,
        out_specs=(
            P("dp", "ctx", "tp"),
            P("dp", "ctx", "tp"),
            P(("dp", "ctx"), "tp"),
            P("tp", None),
        ),
        check_vma=False,
    )
```

```python
import math

import jax
import jax.numpy as jnp
from jax import lax
from jax.experimental import pallas as pl
from jax.experimental.pallas import tpu as pltpu
from jax.sharding import PartitionSpec as P

F32 = jnp.float32
BF16 = jnp.bfloat16
SIDE = 4
TAPS = 128
GROUP = 16
LANES = 128
PER_TILE = LANES // GROUP
WIDE = 256


def room(mebibytes):
    return pltpu.CompilerParams(vmem_limit_bytes=mebibytes * 1024 * 1024)


def spot():
    ctx = lax.axis_index("ctx")
    tp = lax.axis_index("tp")
    return ctx // SIDE, ctx % SIDE, lax.axis_index("dp"), tp // 2, tp % 2


def moved(x, axis):
    step = 2 if axis == "half" else 1
    return lax.ppermute(x, "tp", [(i, i ^ step) for i in range(4)])


def in_plane(x, gather, target):
    pairs = []
    for i in range(SIDE * SIDE):
        for j in range(4):
            place_x, place_y = divmod(i, SIDE)
            if (j % 2 == 0) == gather:
                place_x = target(place_x)
            else:
                place_y = target(place_y)
            pairs.append((i * 4 + j, (place_x * SIDE + place_y) * 4 + j))
    return lax.ppermute(x, ("ctx", "tp"), pairs)


def stepped(x, gather, by):
    return in_plane(x, gather, lambda place: (place + by) % SIDE)


def shifted(x, by):
    devices = lax.axis_size("ctx")
    return lax.ppermute(x, "ctx", [(i, i + by) for i in range(devices) if 0 <= i + by < devices])


ANYWHERE = pl.BlockSpec(memory_space=pl.ANY)
HALF = LANES // 2


def resident(x):
    return pltpu.with_memory_space_constraint(x, pltpu.HBM)


def whole(shape, place=None):
    place = place or (0,) * len(shape)
    return pl.BlockSpec(tuple(shape), lambda i: place, pipeline_mode=pl.Buffered(1))


def full(shape):
    return pl.BlockSpec(tuple(shape), lambda i: (0,) * len(shape))


def tile(rows, width):
    return pl.BlockSpec((rows, width), lambda i: (0, i))


def iota(shape, dim):
    return lax.broadcasted_iota(jnp.int32, shape, dim)


def aligned(index, size):
    return pl.ds(pl.multiple_of(index * size, size), size)


def lasting(microseconds):
    return pl.CostEstimate(flops=int(microseconds * 1e9), bytes_accessed=0, transcendentals=0)


def once(kernel, name, ins, outs, scratch=(), after=(), lasts=0):
    def body(*refs):
        kernel(*refs[: len(ins)], *refs[len(ins) + len(after) :])

    specs = [i[1] if isinstance(i, tuple) else whole(i.shape) for i in ins]
    arrays = [i[0] if isinstance(i, tuple) else i for i in ins]
    return pl.pallas_call(
        body,
        grid=(1,),
        in_specs=specs + [ANYWHERE] * len(after),
        out_specs=[whole(shape) for shape, _ in outs],
        out_shape=[jax.ShapeDtypeStruct(shape, dtype) for shape, dtype in outs],
        scratch_shapes=list(scratch),
        compiler_params=room(20),
        cost_estimate=lasting(lasts),
        name=name,
    )(*arrays, *after)


def first_rows(filters, shifted_by):
    lane, tap = iota((TAPS, 2 * TAPS), 1), iota((TAPS, 2 * TAPS), 0)
    place = lane == (TAPS - tap if shifted_by else tap)
    return jnp.dot(filters, place.astype(F32).astype(BF16), preferred_element_type=F32)


def banded(rows, stack):
    for g in range(PER_TILE):
        first = jnp.broadcast_to(rows[g : g + 1], (TAPS, 2 * TAPS))
        skewed = pltpu.roll(first, 0, 1, stride=1, stride_axis=0)
        stack[g * TAPS : (g + 1) * TAPS, :] = skewed.astype(BF16)


def lane_group(shape):
    return iota(shape, len(shape) - 1) % LANES // GROUP


def own_lanes(stacked):
    group = lane_group((TAPS, 2 * LANES))
    chosen = jnp.zeros((TAPS, 2 * LANES), F32)
    for g in range(PER_TILE):
        chosen = jnp.where(group == g, stacked[g * TAPS : (g + 1) * TAPS], chosen)
    return chosen


def two_windows(first, second, third):
    upper = jnp.concatenate([first, second], 1)
    lower = jnp.concatenate([second, third], 1)
    return jnp.concatenate([upper, lower], 0)


def forward_kernel(filters, previous, signal, gating, response, kept, *refs):
    given, gated, stack = refs[:2], refs[2], refs[3]
    _, _, _, _, core = spot()
    rows = first_rows(filters[...], True)
    for i in range(signal.shape[1] // LANES):
        columns = slice(i * LANES, (i + 1) * LANES)
        band = stack.at[i % 2]
        banded(rows[i * PER_TILE : (i + 1) * PER_TILE], band)
        window = two_windows(previous[:, columns], signal[:TAPS, columns], signal[TAPS:, columns])
        made = own_lanes(jnp.dot(band[...], window, preferred_element_type=F32))
        for block in range(2):
            tokens = slice(block * TAPS, (block + 1) * TAPS)
            part = made[:, block * LANES : (block + 1) * LANES]
            response[tokens, columns] = part
            gated[tokens, columns] = (part * gating[tokens, columns].astype(F32)).astype(BF16)
    kept[...] = gated[:, aligned(core, kept.shape[1])]
    for i, out in enumerate(given):
        out[...] = gated[i * TAPS : (i + 1) * TAPS, aligned(1 - core, kept.shape[1])]


def forward(filters, previous, signal, gating):
    length, channels = signal.shape
    quarter = ((TAPS, channels // 2), BF16)
    return once(
        forward_kernel,
        "conv_forward",
        [filters, previous, signal, gating],
        [((length, channels), F32), ((length, channels // 2), BF16), quarter, quarter],
        [
            pltpu.VMEM((length, channels), BF16),
            pltpu.VMEM((2, PER_TILE * TAPS, 2 * TAPS), BF16),
        ],
    )


def join_kernel(kept, upper, lower, gated):
    _, _, _, _, core = spot()
    width = kept.shape[1]
    gated[: 2 * TAPS, aligned(core, width)] = kept[...]
    gated[:TAPS, aligned(1 - core, width)] = upper[...]
    gated[TAPS : 2 * TAPS, aligned(1 - core, width)] = lower[...]
    gated[2 * TAPS :] = gated[: gated.shape[0] - 2 * TAPS]


def join(kept, received, after):
    length, width = kept.shape
    shape = (length + 16, 2 * width)
    return once(join_kernel, "join", [kept, *received], [(shape, BF16)], (), after)[0]


def input_grad_kernel(filters, conv_grad, following, grad_input, stack):
    rows = first_rows(filters[...], False)
    for i in range(conv_grad.shape[1] // LANES):
        columns = slice(i * LANES, (i + 1) * LANES)
        band = stack.at[i % 2]
        banded(rows[i * PER_TILE : (i + 1) * PER_TILE], band)
        window = two_windows(
            conv_grad[:TAPS, columns], conv_grad[TAPS:, columns], following[:, columns]
        )
        made = own_lanes(jnp.dot(band[...], window, preferred_element_type=F32))
        for block in range(2):
            grad_input[block * TAPS : (block + 1) * TAPS, columns] = made[
                :, block * LANES : (block + 1) * LANES
            ].astype(BF16)


def input_grad(filters, conv_grad, following, after):
    return once(
        input_grad_kernel,
        "input_grad",
        [filters, conv_grad, following],
        [(conv_grad.shape, BF16)],
        [pltpu.VMEM((2, PER_TILE * TAPS, 2 * TAPS), BF16)],
        after,
    )[0]


def filter_grad_kernel(previous, signal, conv_grad, grad_filter, stack):
    square = (2 * TAPS, 2 * TAPS)
    turn = iota(square, 0) == (2 * TAPS - iota(square, 1)) % (2 * TAPS)
    turn = turn.astype(F32).astype(BF16)
    group = lane_group((TAPS, 2 * LANES))
    for i in range(signal.shape[1] // LANES):
        columns = slice(i * LANES, (i + 1) * LANES)
        masked = stack.at[i % 2]
        inputs = two_windows(previous[:, columns], signal[:TAPS, columns], signal[TAPS:, columns])
        turned = jnp.dot(turn, inputs, preferred_element_type=F32).astype(BF16)
        both = jnp.concatenate([conv_grad[:TAPS, columns], conv_grad[TAPS:, columns]], 1)
        both = both.astype(F32)
        for g in range(PER_TILE):
            masked[g * TAPS : (g + 1) * TAPS, :] = jnp.where(group == g, both, 0.0).astype(BF16)
        products = lax.dot_general(
            masked[...], turned, (((1,), (1,)), ((), ())), preferred_element_type=F32
        )
        for g in range(PER_TILE):
            skewed = pltpu.roll(products[g * TAPS : (g + 1) * TAPS], 0, 1, stride=1, stride_axis=0)
            row = i * PER_TILE + g
            grad_filter[row : row + 1, :] = jnp.sum(skewed[:, TAPS:], axis=0, keepdims=True)


def filter_grad(previous, signal, conv_grad, after):
    return once(
        filter_grad_kernel,
        "filter_grad",
        [previous, signal, conv_grad],
        [((signal.shape[1] // GROUP, TAPS), F32)],
        [pltpu.VMEM((2, PER_TILE * TAPS, 2 * TAPS), BF16)],
        after,
        4,
    )[0]


def pack_into(mine, other, outs):
    x, y, _, _, core = spot()
    part = mine.shape[0]
    depth = mine.shape[1] // SIDE

    @pl.when(core == 0)
    def _():
        for ref, rows in ((mine, slice(0, part)), (other, slice(part, 2 * part))):
            for s, out in enumerate(outs):
                for d in range(SIDE):
                    start = pl.multiple_of(d * depth + (x + s) % SIDE * WIDE, WIDE)
                    out[rows, d * WIDE : (d + 1) * WIDE] = ref[:, pl.ds(start, WIDE)]

    @pl.when(core == 1)
    def _():
        lower = iota((part, LANES), 1) < HALF
        for ref, rows in ((other, slice(0, part)), (mine, slice(part, 2 * part))):
            for s, out in enumerate(outs):
                to = (y + s) % SIDE
                upper_half = jnp.broadcast_to(to % 2, (part, LANES)) == 1
                for pair in range(2 * SIDE):
                    runs = []
                    for i in range(2):
                        start = pl.multiple_of((2 * pair + i) * WIDE + to // 2 * LANES, LANES)
                        runs.append(ref[:, pl.ds(start, LANES)].astype(F32))
                    first = jnp.where(upper_half, pltpu.roll(runs[0], HALF, 1), runs[0])
                    second = jnp.where(upper_half, runs[1], pltpu.roll(runs[1], HALF, 1))
                    both = jnp.where(lower, first, second).astype(BF16)
                    out[rows, pair * LANES : (pair + 1) * LANES] = both


def pack_kernel(mine, other, *outs):
    pack_into(mine, other, outs)


def pack(mine, other):
    rows, width = mine.shape
    return once(
        pack_kernel, "pack", [mine, other], [((2 * rows, width // SIDE), BF16)] * SIDE
    )


def relay_kernel(mine, other, before, after, opposite, *outs):
    pack_into(mine, other, outs)
    part = opposite.shape[0]
    outs[1][part:] = before[...]
    outs[2][part:] = opposite[...]
    outs[3][part:] = after[...]


def relay(mine, other, got_next, got_last, opposite):
    rows, width = opposite.shape
    return once(
        relay_kernel,
        "relay",
        [
            mine,
            other,
            (got_next, whole((TAPS, width))),
            (got_last, whole((TAPS, width), (1, 0))),
            opposite,
        ],
        [((rows, width), BF16)] + [((rows + TAPS, width), BF16)] * (SIDE - 1),
    )


def project_kernel(early, early_other, late, late_other, weight, gating, response, conv_grad, grad_gate, rows):
    _, _, _, half, core = spot()
    part = early.shape[0]

    @pl.when(pl.program_id(0) == 0)
    def _():
        for ref, h, c in (
            (early, half, core),
            (early_other, half, 1 - core),
            (late, 1 - half, core),
            (late_other, 1 - half, 1 - core),
        ):
            rows[aligned(2 * h + c, part), :] = ref[...]

    made = jnp.dot(rows[...], weight[...], preferred_element_type=F32)
    conv_grad[...] = (made * gating[...].astype(F32)).astype(BF16)
    grad_gate[...] = (made * response[...]).astype(BF16)


def project(early, early_other, late, late_other, weight, gating, response, after):
    length, channels = gating.shape
    depth = weight.shape[0]

    def body(*refs):
        project_kernel(*refs[:7], *refs[7 + len(after) :])

    return pl.pallas_call(
        body,
        grid=(channels // WIDE,),
        in_specs=[full(early.shape)] * 4
        + [tile(depth, WIDE), tile(length, WIDE), tile(length, WIDE)]
        + [ANYWHERE] * len(after),
        out_specs=[tile(length, WIDE)] * 2,
        out_shape=[jax.ShapeDtypeStruct((length, channels), BF16)] * 2,
        scratch_shapes=[pltpu.VMEM((length, depth), BF16)],
        compiler_params=room(20),
        cost_estimate=lasting(6),
        name="project",
    )(early, early_other, late, late_other, weight, gating, response, *after)


def weight_kernel(*refs):
    early, late = refs[:SIDE], refs[SIDE : 2 * SIDE]
    gated, got_next, before, after, got_last = refs[2 * SIDE : 2 * SIDE + 5]
    outs, turned, tokens = refs[-2 - SIDE : -2], refs[-2], refs[-1]
    x, y, _, half, core = spot()
    me = jnp.where(core == 0, y, x)
    upper = jnp.broadcast_to(half, before.shape) == 0
    opposite = (before[...].astype(F32), after[...].astype(F32))
    for i, (parts, h) in enumerate(((early, half), (late, 1 - half))):
        rows = aligned(h, TAPS)
        halves = opposite if i == 0 else opposite[::-1]
        blocks = (
            gated[rows, :],
            got_next[rows, :],
            jnp.where(upper, *halves).astype(BF16),
            got_last[rows, :],
        )
        for s in range(SIDE):
            at = slice((i * SIDE + s) * TAPS, (i * SIDE + s + 1) * TAPS)
            tokens[at] = blocks[s]
            transposed = parts[s][...].T
            for d in range(SIDE):
                for q in range(SIDE):
                    to = (q - me + SIDE) % SIDE * WIDE + d * HALF
                    start = d * WIDE + q * HALF
                    turned[pl.ds(pl.multiple_of(to, HALF), HALF), at] = transposed[
                        start : start + HALF
                    ]
    for s, out in enumerate(outs):
        features = turned[s * WIDE : (s + 1) * WIDE]
        out[...] = jnp.dot(features, tokens[...], preferred_element_type=F32).astype(out.dtype)


def weight_parts(early, own_late, gated, got, late, after):
    width = gated.shape[1]
    rows = own_late.shape[0]
    length = 2 * rows

    def block(array, start, count=rows):
        return array, whole((count, width), (start // count, 0))

    shape = (width // SIDE, width)
    return once(
        weight_kernel,
        "weight_parts",
        [
            early[0],
            early[1],
            block(late[1], rows),
            early[2],
            own_late,
            *[block(part, 0) for part in late],
            block(gated, 0, length),
            block(got[0], 0, length),
            block(late[0], rows),
            block(late[2], rows),
            block(got[1], 0, length),
        ],
        [(shape, F32)] + [(shape, BF16)] * (SIDE - 1),
        [pltpu.VMEM((width, 2 * SIDE * rows), BF16), pltpu.VMEM((2 * SIDE * rows, width), BF16)],
        after,
        4,
    )


def first_sum_kernel(*refs):
    _, _, z, _, _ = spot()
    outs, kept = refs[SIDE:-1], refs[-1]
    run = kept.shape[0] // SIDE
    total = refs[0][...]
    for ref in refs[1:SIDE]:
        total = total + ref[...].astype(F32)
    for d in range(SIDE):
        kept[aligned((d - z + SIDE) % SIDE, run), :] = total[d * run : (d + 1) * run]
    for s, out in enumerate(outs):
        out[...] = kept[s * run : (s + 1) * run, :].astype(out.dtype)


def first_sum(parts, after):
    rows, width = parts[0].shape
    run = rows // SIDE
    return once(
        first_sum_kernel,
        "first_sum",
        parts,
        [((run, width), F32)] + [((run, width), BF16)] * (SIDE - 1),
        [pltpu.VMEM((rows, width), F32)],
        after,
        1,
    )


def last_sum(parts, scale, after):
    rows, width = parts[0].shape

    def kernel(*refs):
        kept, given, summed = refs[SIDE:]
        _, _, _, _, core = spot()
        total = refs[0][...]
        for ref in refs[1:SIDE]:
            total = total + ref[...].astype(F32)
        summed[...] = total * scale
        kept[...] = summed[:, aligned(core, width // 2)]
        given[...] = summed[:, aligned(1 - core, width // 2)]

    half = ((rows, width // 2), F32)
    return once(
        kernel, "last_sum", parts, [half, half], [pltpu.VMEM((rows, width), F32)], after
    )


def beside(kept, received):
    def kernel(first, second, out):
        _, _, _, _, core = spot()
        out[:, aligned(core, first.shape[1])] = first[...]
        out[:, aligned(1 - core, first.shape[1])] = second[...]

    rows, width = kept.shape
    return once(kernel, "beside", [kept, received], [((rows, 2 * width), F32)])[0]


def tied(x, *after):
    return lax.optimization_barrier((x, *after))[0]


def paired(x, gather, by, before=()):
    return x + in_plane(tied(x, *before), gather, lambda place: place ^ by)


def paired_z(x, by):
    return x + lax.ppermute(x, "dp", [(i, i ^ by) for i in range(SIDE)])


def local(conv_input, gate_value, out_grad, out_weight, filters):
    signal, gating, grads = conv_input[0], gate_value[0], out_grad[0]
    length, channels = signal.shape
    halo_sent = signal[length - TAPS :]
    signal, gating, filters, weight = (
        resident(x) for x in (signal, gating, filters, out_weight)
    )
    tokens_all = lax.axis_size("dp") * lax.axis_size("ctx") * length
    shifts = range(1, SIDE)

    late = moved(grads, "half")
    previous = shifted(halo_sent, 1)
    early_other = moved(grads, "core")
    grads = resident(grads)
    early = pack(grads, early_other)
    early_got = [stepped(early[1], True, 1), stepped(early[3], True, 3)]
    response, kept, *given = forward(filters, previous, signal, gating)
    gated = join(kept, [moved(part, "core") for part in given], early_got)
    got = [stepped(gated, True, 1), stepped(gated, True, 3)]
    late_other = moved(tied(late, gated), "core")
    own_late, *late_sent = relay(late, late_other, *got, early[2])
    conv_grad, grad_gate = project(
        grads, early_other, late, late_other, weight, gating, response, (own_late,)
    )
    late_got = [stepped(late_sent[s - 1], True, s) for s in shifts]
    filter_sum = filter_grad(previous, signal, conv_grad, ())
    parts = weight_parts([early[0], *early_got], own_late, gated, got, late_got, (filter_sum,))

    filter_sum = paired_z(paired_z(tied(filter_sum, parts[0]), 1), 2)
    following = shifted(tied(conv_grad[:TAPS], filter_sum), -1)
    filter_sum = paired(filter_sum, True, 1)
    parts = [parts[0]] + [stepped(parts[s], False, s) for s in shifts]
    sums = first_sum(parts, (filter_sum,))
    grad_input = input_grad(filters, conv_grad, following, (sums[0],))
    filter_sum = paired(filter_sum, True, 2, (sums[0],))
    filter_sum = paired(paired(filter_sum, False, 1, (resident(grad_input),)), False, 2)
    grad_filter = filter_sum * (1.0 / math.sqrt(tokens_all * GROUP))
    line = [[(i, (i + s) % SIDE) for i in range(SIDE)] for s in shifts]
    sums = [sums[0]] + [lax.ppermute(sums[s], "dp", line[s - 1]) for s in shifts]
    kept, given = last_sum(sums, 1.0 / math.sqrt(tokens_all), (resident(grad_input),))
    grad_weight = beside(kept, moved(given, "core"))
    return (grad_input[None], grad_gate[None], grad_weight, grad_filter)


def solution(mesh):
    placed = (
        P("dp", "ctx", "tp"),
        P("dp", "ctx", "tp"),
        P("dp", ("ctx", "tp"), None),
        P(None, "tp"),
        P("tp", None),
    )
    return jax.shard_map(
        local,
        mesh=mesh,
        in_specs=placed,
        out_specs=(
            P("dp", "ctx", "tp"),
            P("dp", "ctx", "tp"),
            P(("dp", "ctx"), "tp"),
            P("tp", None),
        ),
        check_vma=False,
    )
```

```python
import math

import jax
import jax.numpy as jnp
from jax import lax
from jax.experimental import pallas as pl
from jax.experimental.pallas import tpu as pltpu
from jax.sharding import PartitionSpec as P

F32 = jnp.float32
BF16 = jnp.bfloat16
SIDE = 4
TAPS = 128
GROUP = 16
LANES = 128
PER_TILE = LANES // GROUP
WIDE = 256


def room(mebibytes):
    return pltpu.CompilerParams(vmem_limit_bytes=mebibytes * 1024 * 1024)


def spot():
    ctx = lax.axis_index("ctx")
    tp = lax.axis_index("tp")
    return ctx // SIDE, ctx % SIDE, lax.axis_index("dp"), tp // 2, tp % 2


def moved(x, axis):
    step = 2 if axis == "half" else 1
    return lax.ppermute(x, "tp", [(i, i ^ step) for i in range(4)])


def in_plane(x, gather, target):
    pairs = []
    for i in range(SIDE * SIDE):
        for j in range(4):
            place_x, place_y = divmod(i, SIDE)
            if (j % 2 == 0) == gather:
                place_x = target(place_x)
            else:
                place_y = target(place_y)
            pairs.append((i * 4 + j, (place_x * SIDE + place_y) * 4 + j))
    return lax.ppermute(x, ("ctx", "tp"), pairs)


def stepped(x, gather, by):
    return in_plane(x, gather, lambda place: (place + by) % SIDE)


def shifted(x, by):
    devices = lax.axis_size("ctx")
    return lax.ppermute(x, "ctx", [(i, i + by) for i in range(devices) if 0 <= i + by < devices])


ANYWHERE = pl.BlockSpec(memory_space=pl.ANY)
HALF = LANES // 2


def resident(x):
    return pltpu.with_memory_space_constraint(x, pltpu.HBM)


def whole(shape, place=None):
    place = place or (0,) * len(shape)
    return pl.BlockSpec(tuple(shape), lambda i: place, pipeline_mode=pl.Buffered(1))


def full(shape):
    return pl.BlockSpec(tuple(shape), lambda i: (0,) * len(shape))


def tile(rows, width):
    return pl.BlockSpec((rows, width), lambda i: (0, i))


def iota(shape, dim):
    return lax.broadcasted_iota(jnp.int32, shape, dim)


def aligned(index, size):
    return pl.ds(pl.multiple_of(index * size, size), size)


def lasting(microseconds):
    return pl.CostEstimate(flops=int(microseconds * 1e9), bytes_accessed=0, transcendentals=0)


def once(kernel, name, ins, outs, scratch=(), after=(), lasts=0):
    def body(*refs):
        kernel(*refs[: len(ins)], *refs[len(ins) + len(after) :])

    specs = [i[1] if isinstance(i, tuple) else whole(i.shape) for i in ins]
    arrays = [i[0] if isinstance(i, tuple) else i for i in ins]
    return pl.pallas_call(
        body,
        grid=(1,),
        in_specs=specs + [ANYWHERE] * len(after),
        out_specs=[whole(shape) for shape, _ in outs],
        out_shape=[jax.ShapeDtypeStruct(shape, dtype) for shape, dtype in outs],
        scratch_shapes=list(scratch),
        compiler_params=room(20),
        cost_estimate=lasting(lasts),
        name=name,
    )(*arrays, *after)


def first_rows(filters, shifted_by):
    lane, tap = iota((TAPS, 2 * TAPS), 1), iota((TAPS, 2 * TAPS), 0)
    place = lane == (TAPS - tap if shifted_by else tap)
    return jnp.dot(filters, place.astype(F32).astype(BF16), preferred_element_type=F32)


def banded(rows, stack):
    for g in range(PER_TILE):
        first = jnp.broadcast_to(rows[g : g + 1], (TAPS, 2 * TAPS))
        skewed = pltpu.roll(first, 0, 1, stride=1, stride_axis=0)
        stack[g * TAPS : (g + 1) * TAPS, :] = skewed.astype(BF16)


def lane_group(shape):
    return iota(shape, len(shape) - 1) % LANES // GROUP


def own_lanes(stacked):
    group = lane_group((TAPS, 2 * LANES))
    chosen = jnp.zeros((TAPS, 2 * LANES), F32)
    for g in range(PER_TILE):
        chosen = jnp.where(group == g, stacked[g * TAPS : (g + 1) * TAPS], chosen)
    return chosen


def two_windows(first, second, third):
    upper = jnp.concatenate([first, second], 1)
    lower = jnp.concatenate([second, third], 1)
    return jnp.concatenate([upper, lower], 0)


def forward_kernel(filters, previous, signal, gating, response, kept, *refs):
    given, gated, stack = refs[:2], refs[2], refs[3]
    _, _, _, _, core = spot()
    rows = first_rows(filters[...], True)
    for i in range(signal.shape[1] // LANES):
        columns = slice(i * LANES, (i + 1) * LANES)
        band = stack.at[i % 2]
        banded(rows[i * PER_TILE : (i + 1) * PER_TILE], band)
        window = two_windows(previous[:, columns], signal[:TAPS, columns], signal[TAPS:, columns])
        made = own_lanes(jnp.dot(band[...], window, preferred_element_type=F32))
        for block in range(2):
            tokens = slice(block * TAPS, (block + 1) * TAPS)
            part = made[:, block * LANES : (block + 1) * LANES]
            response[tokens, columns] = part
            gated[tokens, columns] = (part * gating[tokens, columns].astype(F32)).astype(BF16)
    kept[...] = gated[:, aligned(core, kept.shape[1])]
    for i, out in enumerate(given):
        out[...] = gated[i * TAPS : (i + 1) * TAPS, aligned(1 - core, kept.shape[1])]


def forward(filters, previous, signal, gating):
    length, channels = signal.shape
    quarter = ((TAPS, channels // 2), BF16)
    return once(
        forward_kernel,
        "conv_forward",
        [filters, previous, signal, gating],
        [((length, channels), F32), ((length, channels // 2), BF16), quarter, quarter],
        [
            pltpu.VMEM((length, channels), BF16),
            pltpu.VMEM((2, PER_TILE * TAPS, 2 * TAPS), BF16),
        ],
    )


def join_kernel(kept, upper, lower, gated):
    _, _, _, _, core = spot()
    width = kept.shape[1]
    gated[: 2 * TAPS, aligned(core, width)] = kept[...]
    gated[:TAPS, aligned(1 - core, width)] = upper[...]
    gated[TAPS : 2 * TAPS, aligned(1 - core, width)] = lower[...]
    gated[2 * TAPS :] = gated[: gated.shape[0] - 2 * TAPS]


def join(kept, received, after):
    length, width = kept.shape
    shape = (length + 16, 2 * width)
    return once(join_kernel, "join", [kept, *received], [(shape, BF16)], (), after)[0]


def input_grad_kernel(filters, conv_grad, following, grad_input, stack):
    rows = first_rows(filters[...], False)
    for i in range(conv_grad.shape[1] // LANES):
        columns = slice(i * LANES, (i + 1) * LANES)
        band = stack.at[i % 2]
        banded(rows[i * PER_TILE : (i + 1) * PER_TILE], band)
        window = two_windows(
            conv_grad[:TAPS, columns], conv_grad[TAPS:, columns], following[:, columns]
        )
        made = own_lanes(jnp.dot(band[...], window, preferred_element_type=F32))
        for block in range(2):
            grad_input[block * TAPS : (block + 1) * TAPS, columns] = made[
                :, block * LANES : (block + 1) * LANES
            ].astype(BF16)


def input_grad(filters, conv_grad, following, after):
    return once(
        input_grad_kernel,
        "input_grad",
        [filters, conv_grad, following],
        [(conv_grad.shape, BF16)],
        [pltpu.VMEM((2, PER_TILE * TAPS, 2 * TAPS), BF16)],
        after,
    )[0]


def filter_grad_kernel(previous, signal, conv_grad, grad_filter, stack):
    square = (2 * TAPS, 2 * TAPS)
    turn = iota(square, 0) == (2 * TAPS - iota(square, 1)) % (2 * TAPS)
    turn = turn.astype(F32).astype(BF16)
    group = lane_group((TAPS, 2 * LANES))
    for i in range(signal.shape[1] // LANES):
        columns = slice(i * LANES, (i + 1) * LANES)
        masked = stack.at[i % 2]
        inputs = two_windows(previous[:, columns], signal[:TAPS, columns], signal[TAPS:, columns])
        turned = jnp.dot(turn, inputs, preferred_element_type=F32).astype(BF16)
        both = jnp.concatenate([conv_grad[:TAPS, columns], conv_grad[TAPS:, columns]], 1)
        both = both.astype(F32)
        for g in range(PER_TILE):
            masked[g * TAPS : (g + 1) * TAPS, :] = jnp.where(group == g, both, 0.0).astype(BF16)
        products = lax.dot_general(
            masked[...], turned, (((1,), (1,)), ((), ())), preferred_element_type=F32
        )
        for g in range(PER_TILE):
            skewed = pltpu.roll(products[g * TAPS : (g + 1) * TAPS], 0, 1, stride=1, stride_axis=0)
            row = i * PER_TILE + g
            grad_filter[row : row + 1, :] = jnp.sum(skewed[:, TAPS:], axis=0, keepdims=True)


def filter_grad(previous, signal, conv_grad, after):
    return once(
        filter_grad_kernel,
        "filter_grad",
        [previous, signal, conv_grad],
        [((signal.shape[1] // GROUP, TAPS), F32)],
        [pltpu.VMEM((2, PER_TILE * TAPS, 2 * TAPS), BF16)],
        after,
        4,
    )[0]


def pack_into(mine, other, outs):
    x, y, _, _, core = spot()
    part = mine.shape[0]
    depth = mine.shape[1] // SIDE

    @pl.when(core == 0)
    def _():
        for ref, rows in ((mine, slice(0, part)), (other, slice(part, 2 * part))):
            for s, out in enumerate(outs):
                for d in range(SIDE):
                    start = pl.multiple_of(d * depth + (x + s) % SIDE * WIDE, WIDE)
                    out[rows, d * WIDE : (d + 1) * WIDE] = ref[:, pl.ds(start, WIDE)]

    @pl.when(core == 1)
    def _():
        lower = iota((part, LANES), 1) < HALF
        for ref, rows in ((other, slice(0, part)), (mine, slice(part, 2 * part))):
            for s, out in enumerate(outs):
                to = (y + s) % SIDE
                upper_half = jnp.broadcast_to(to % 2, (part, LANES)) == 1
                for pair in range(2 * SIDE):
                    runs = []
                    for i in range(2):
                        start = pl.multiple_of((2 * pair + i) * WIDE + to // 2 * LANES, LANES)
                        runs.append(ref[:, pl.ds(start, LANES)].astype(F32))
                    first = jnp.where(upper_half, pltpu.roll(runs[0], HALF, 1), runs[0])
                    second = jnp.where(upper_half, runs[1], pltpu.roll(runs[1], HALF, 1))
                    both = jnp.where(lower, first, second).astype(BF16)
                    out[rows, pair * LANES : (pair + 1) * LANES] = both


def pack_kernel(mine, other, *outs):
    pack_into(mine, other, outs)


def pack(mine, other):
    rows, width = mine.shape
    return once(
        pack_kernel, "pack", [mine, other], [((2 * rows, width // SIDE), BF16)] * SIDE
    )


def relay_kernel(mine, other, before, after, opposite, *outs):
    pack_into(mine, other, outs)
    part = opposite.shape[0]
    outs[1][part:] = before[...]
    outs[2][part:] = opposite[...]
    outs[3][part:] = after[...]


def relay(mine, other, got_next, got_last, opposite):
    rows, width = opposite.shape
    return once(
        relay_kernel,
        "relay",
        [
            mine,
            other,
            (got_next, whole((TAPS, width))),
            (got_last, whole((TAPS, width), (1, 0))),
            opposite,
        ],
        [((rows, width), BF16)] + [((rows + TAPS, width), BF16)] * (SIDE - 1),
    )


def project_kernel(early, early_other, late, late_other, weight, gating, response, conv_grad, grad_gate, rows):
    _, _, _, half, core = spot()
    part = early.shape[0]

    @pl.when(pl.program_id(0) == 0)
    def _():
        for ref, h, c in (
            (early, half, core),
            (early_other, half, 1 - core),
            (late, 1 - half, core),
            (late_other, 1 - half, 1 - core),
        ):
            rows[aligned(2 * h + c, part), :] = ref[...]

    made = jnp.dot(rows[...], weight[...], preferred_element_type=F32)
    conv_grad[...] = (made * gating[...].astype(F32)).astype(BF16)
    grad_gate[...] = (made * response[...]).astype(BF16)


def project(early, early_other, late, late_other, weight, gating, response, after):
    length, channels = gating.shape
    depth = weight.shape[0]

    def body(*refs):
        project_kernel(*refs[:7], *refs[7 + len(after) :])

    return pl.pallas_call(
        body,
        grid=(channels // WIDE,),
        in_specs=[full(early.shape)] * 4
        + [tile(depth, WIDE), tile(length, WIDE), tile(length, WIDE)]
        + [ANYWHERE] * len(after),
        out_specs=[tile(length, WIDE)] * 2,
        out_shape=[jax.ShapeDtypeStruct((length, channels), BF16)] * 2,
        scratch_shapes=[pltpu.VMEM((length, depth), BF16)],
        compiler_params=room(20),
        cost_estimate=lasting(6),
        name="project",
    )(early, early_other, late, late_other, weight, gating, response, *after)


def weight_kernel(*refs):
    early, late = refs[:SIDE], refs[SIDE : 2 * SIDE]
    gated, got_next, before, after, got_last = refs[2 * SIDE : 2 * SIDE + 5]
    outs, turned, tokens = refs[-2 - SIDE : -2], refs[-2], refs[-1]
    x, y, _, half, core = spot()
    me = jnp.where(core == 0, y, x)
    upper = jnp.broadcast_to(half, before.shape) == 0
    opposite = (before[...].astype(F32), after[...].astype(F32))
    for i, (parts, h) in enumerate(((early, half), (late, 1 - half))):
        rows = aligned(h, TAPS)
        halves = opposite if i == 0 else opposite[::-1]
        blocks = (
            gated[rows, :],
            got_next[rows, :],
            jnp.where(upper, *halves).astype(BF16),
            got_last[rows, :],
        )
        for s in range(SIDE):
            at = slice((i * SIDE + s) * TAPS, (i * SIDE + s + 1) * TAPS)
            tokens[at] = blocks[s]
            transposed = parts[s][...].T
            for d in range(SIDE):
                for q in range(SIDE):
                    to = (q - me + SIDE) % SIDE * WIDE + d * HALF
                    start = d * WIDE + q * HALF
                    turned[pl.ds(pl.multiple_of(to, HALF), HALF), at] = transposed[
                        start : start + HALF
                    ]
    for s, out in enumerate(outs):
        features = turned[s * WIDE : (s + 1) * WIDE]
        out[...] = jnp.dot(features, tokens[...], preferred_element_type=F32).astype(out.dtype)


def weight_parts(early, own_late, gated, got, late, after):
    width = gated.shape[1]
    rows = own_late.shape[0]
    length = 2 * rows

    def block(array, start, count=rows):
        return array, whole((count, width), (start // count, 0))

    shape = (width // SIDE, width)
    return once(
        weight_kernel,
        "weight_parts",
        [
            early[0],
            early[1],
            block(late[1], rows),
            early[2],
            own_late,
            *[block(part, 0) for part in late],
            block(gated, 0, length),
            block(got[0], 0, length),
            block(late[0], rows),
            block(late[2], rows),
            block(got[1], 0, length),
        ],
        [(shape, F32)] + [(shape, BF16)] * (SIDE - 1),
        [pltpu.VMEM((width, 2 * SIDE * rows), BF16), pltpu.VMEM((2 * SIDE * rows, width), BF16)],
        after,
        4,
    )


def first_sum_kernel(*refs):
    _, _, z, _, _ = spot()
    outs, kept = refs[SIDE:-1], refs[-1]
    run = kept.shape[0] // SIDE
    total = refs[0][...]
    for ref in refs[1:SIDE]:
        total = total + ref[...].astype(F32)
    for d in range(SIDE):
        kept[aligned((d - z + SIDE) % SIDE, run), :] = total[d * run : (d + 1) * run]
    for s, out in enumerate(outs):
        out[...] = kept[s * run : (s + 1) * run, :].astype(out.dtype)


def first_sum(parts, after):
    rows, width = parts[0].shape
    run = rows // SIDE
    return once(
        first_sum_kernel,
        "first_sum",
        parts,
        [((run, width), F32)] + [((run, width), BF16)] * (SIDE - 1),
        [pltpu.VMEM((rows, width), F32)],
        after,
        1,
    )


def last_sum(parts, scale, after):
    rows, width = parts[0].shape

    def kernel(*refs):
        kept, given, summed = refs[SIDE:]
        _, _, _, _, core = spot()
        total = refs[0][...]
        for ref in refs[1:SIDE]:
            total = total + ref[...].astype(F32)
        summed[...] = total * scale
        kept[...] = summed[:, aligned(core, width // 2)]
        given[...] = summed[:, aligned(1 - core, width // 2)]

    half = ((rows, width // 2), F32)
    return once(
        kernel, "last_sum", parts, [half, half], [pltpu.VMEM((rows, width), F32)], after
    )


def beside(kept, received):
    def kernel(first, second, out):
        _, _, _, _, core = spot()
        out[:, aligned(core, first.shape[1])] = first[...]
        out[:, aligned(1 - core, first.shape[1])] = second[...]

    rows, width = kept.shape
    return once(kernel, "beside", [kept, received], [((rows, 2 * width), F32)])[0]


def tied(x, *after):
    return lax.optimization_barrier((x, *after))[0]


def paired(x, gather, by, before=()):
    return x + in_plane(tied(x, *before), gather, lambda place: place ^ by)


def paired_z(x, by):
    return x + lax.ppermute(x, "dp", [(i, i ^ by) for i in range(SIDE)])


def local(conv_input, gate_value, out_grad, out_weight, filters):
    signal, gating, grads = conv_input[0], gate_value[0], out_grad[0]
    length, channels = signal.shape
    halo_sent = signal[length - TAPS :]
    signal, gating, filters, weight = (
        resident(x) for x in (signal, gating, filters, out_weight)
    )
    tokens_all = lax.axis_size("dp") * lax.axis_size("ctx") * length
    shifts = range(1, SIDE)

    late = moved(grads, "half")
    previous = shifted(halo_sent, 1)
    early_other = moved(grads, "core")
    grads = resident(grads)
    early = pack(grads, early_other)
    early_got = [stepped(early[1], True, 1), stepped(early[3], True, 3)]
    response, kept, *given = forward(filters, previous, signal, gating)
    gated = join(kept, [moved(part, "core") for part in given], early_got)
    got = [stepped(gated, True, 1), stepped(gated, True, 3)]
    late_other = moved(tied(late, gated), "core")
    own_late, *late_sent = relay(late, late_other, *got, early[2])
    conv_grad, grad_gate = project(
        grads, early_other, late, late_other, weight, gating, response, (own_late,)
    )
    late_got = [stepped(late_sent[s - 1], True, s) for s in shifts]
    filter_sum = filter_grad(previous, signal, conv_grad, ())
    parts = weight_parts([early[0], *early_got], own_late, gated, got, late_got, (filter_sum,))

    filter_sum = paired_z(paired_z(tied(filter_sum, parts[0]), 1), 2)
    following = shifted(tied(conv_grad[:TAPS], filter_sum), -1)
    filter_sum = paired(filter_sum, True, 1)
    padded = jnp.pad(filter_sum, ((0, 3 * filter_sum.shape[0]), (0, 0)))
    padded = in_plane(padded, True, lambda place: place ^ 2)
    filter_sum = filter_sum + padded[: filter_sum.shape[0]]
    parts = [parts[0]] + [stepped(parts[s], False, s) for s in shifts]
    sums = first_sum(parts, ())
    grad_input = input_grad(filters, conv_grad, following, (sums[0],))
    filter_sum = paired(filter_sum, False, 1, (sums[0],))
    filter_sum = paired(filter_sum, False, 2, (resident(grad_input),))
    grad_filter = filter_sum * (1.0 / math.sqrt(tokens_all * GROUP))
    line = [[(i, (i + s) % SIDE) for i in range(SIDE)] for s in shifts]
    sums = [sums[0]] + [lax.ppermute(sums[s], "dp", line[s - 1]) for s in shifts]
    kept, given = last_sum(sums, 1.0 / math.sqrt(tokens_all), (resident(grad_input),))
    grad_weight = beside(kept, moved(given, "core"))
    return (grad_input[None], grad_gate[None], grad_weight, grad_filter)


def solution(mesh):
    placed = (
        P("dp", "ctx", "tp"),
        P("dp", "ctx", "tp"),
        P("dp", ("ctx", "tp"), None),
        P(None, "tp"),
        P("tp", None),
    )
    return jax.shard_map(
        local,
        mesh=mesh,
        in_specs=placed,
        out_specs=(
            P("dp", "ctx", "tp"),
            P("dp", "ctx", "tp"),
            P(("dp", "ctx"), "tp"),
            P("tp", None),
        ),
        check_vma=False,
    )
```

```python
import math

import jax
import jax.numpy as jnp
from jax import lax
from jax.experimental import pallas as pl
from jax.experimental.pallas import tpu as pltpu
from jax.sharding import PartitionSpec as P

F32 = jnp.float32
BF16 = jnp.bfloat16
SIDE = 4
TAPS = 128
GROUP = 16
LANES = 128
PER_TILE = LANES // GROUP
WIDE = 256


def room(mebibytes):
    return pltpu.CompilerParams(vmem_limit_bytes=mebibytes * 1024 * 1024)


def spot():
    ctx = lax.axis_index("ctx")
    tp = lax.axis_index("tp")
    return ctx // SIDE, ctx % SIDE, lax.axis_index("dp"), tp // 2, tp % 2


def moved(x, axis):
    step = 2 if axis == "half" else 1
    return lax.ppermute(x, "tp", [(i, i ^ step) for i in range(4)])


def in_plane(x, gather, target):
    pairs = []
    for i in range(SIDE * SIDE):
        for j in range(4):
            place_x, place_y = divmod(i, SIDE)
            if (j % 2 == 0) == gather:
                place_x = target(place_x)
            else:
                place_y = target(place_y)
            pairs.append((i * 4 + j, (place_x * SIDE + place_y) * 4 + j))
    return lax.ppermute(x, ("ctx", "tp"), pairs)


def stepped(x, gather, by):
    return in_plane(x, gather, lambda place: (place + by) % SIDE)


def shifted(x, by):
    devices = lax.axis_size("ctx")
    return lax.ppermute(x, "ctx", [(i, i + by) for i in range(devices) if 0 <= i + by < devices])


ANYWHERE = pl.BlockSpec(memory_space=pl.ANY)
HALF = LANES // 2


def resident(x):
    return pltpu.with_memory_space_constraint(x, pltpu.HBM)


def whole(shape, place=None):
    place = place or (0,) * len(shape)
    return pl.BlockSpec(tuple(shape), lambda i: place, pipeline_mode=pl.Buffered(1))


def full(shape):
    return pl.BlockSpec(tuple(shape), lambda i: (0,) * len(shape))


def tile(rows, width):
    return pl.BlockSpec((rows, width), lambda i: (0, i))


def iota(shape, dim):
    return lax.broadcasted_iota(jnp.int32, shape, dim)


def aligned(index, size):
    return pl.ds(pl.multiple_of(index * size, size), size)


def lasting(microseconds):
    return pl.CostEstimate(flops=int(microseconds * 1e9), bytes_accessed=0, transcendentals=0)


def once(kernel, name, ins, outs, scratch=(), after=(), lasts=0):
    def body(*refs):
        kernel(*refs[: len(ins)], *refs[len(ins) + len(after) :])

    specs = [i[1] if isinstance(i, tuple) else whole(i.shape) for i in ins]
    arrays = [i[0] if isinstance(i, tuple) else i for i in ins]
    return pl.pallas_call(
        body,
        grid=(1,),
        in_specs=specs + [ANYWHERE] * len(after),
        out_specs=[whole(shape) for shape, _ in outs],
        out_shape=[jax.ShapeDtypeStruct(shape, dtype) for shape, dtype in outs],
        scratch_shapes=list(scratch),
        compiler_params=room(20),
        cost_estimate=lasting(lasts),
        name=name,
    )(*arrays, *after)


def first_rows(filters, shifted_by):
    lane, tap = iota((TAPS, 2 * TAPS), 1), iota((TAPS, 2 * TAPS), 0)
    place = lane == (TAPS - tap if shifted_by else tap)
    return jnp.dot(filters, place.astype(F32).astype(BF16), preferred_element_type=F32)


def banded(rows, stack):
    for g in range(PER_TILE):
        first = jnp.broadcast_to(rows[g : g + 1], (TAPS, 2 * TAPS))
        skewed = pltpu.roll(first, 0, 1, stride=1, stride_axis=0)
        stack[g * TAPS : (g + 1) * TAPS, :] = skewed.astype(BF16)


def lane_group(shape):
    return iota(shape, len(shape) - 1) % LANES // GROUP


def own_lanes(stacked):
    group = lane_group((TAPS, 2 * LANES))
    chosen = jnp.zeros((TAPS, 2 * LANES), F32)
    for g in range(PER_TILE):
        chosen = jnp.where(group == g, stacked[g * TAPS : (g + 1) * TAPS], chosen)
    return chosen


def two_windows(first, second, third):
    upper = jnp.concatenate([first, second], 1)
    lower = jnp.concatenate([second, third], 1)
    return jnp.concatenate([upper, lower], 0)


def forward_kernel(filters, previous, signal, gating, response, kept, *refs):
    given, gated, stack = refs[:2], refs[2], refs[3]
    _, _, _, _, core = spot()
    rows = first_rows(filters[...], True)
    for i in range(signal.shape[1] // LANES):
        columns = slice(i * LANES, (i + 1) * LANES)
        band = stack.at[i % 2]
        banded(rows[i * PER_TILE : (i + 1) * PER_TILE], band)
        window = two_windows(previous[:, columns], signal[:TAPS, columns], signal[TAPS:, columns])
        made = own_lanes(jnp.dot(band[...], window, preferred_element_type=F32))
        for block in range(2):
            tokens = slice(block * TAPS, (block + 1) * TAPS)
            part = made[:, block * LANES : (block + 1) * LANES]
            response[tokens, columns] = part
            gated[tokens, columns] = (part * gating[tokens, columns].astype(F32)).astype(BF16)
    kept[...] = gated[:, aligned(core, kept.shape[1])]
    for i, out in enumerate(given):
        out[...] = gated[i * TAPS : (i + 1) * TAPS, aligned(1 - core, kept.shape[1])]


def forward(filters, previous, signal, gating):
    length, channels = signal.shape
    quarter = ((TAPS, channels // 2), BF16)
    return once(
        forward_kernel,
        "conv_forward",
        [filters, previous, signal, gating],
        [((length, channels), F32), ((length, channels // 2), BF16), quarter, quarter],
        [
            pltpu.VMEM((length, channels), BF16),
            pltpu.VMEM((2, PER_TILE * TAPS, 2 * TAPS), BF16),
        ],
    )


def join_kernel(kept, upper, lower, gated):
    _, _, _, _, core = spot()
    width = kept.shape[1]
    gated[: 2 * TAPS, aligned(core, width)] = kept[...]
    gated[:TAPS, aligned(1 - core, width)] = upper[...]
    gated[TAPS : 2 * TAPS, aligned(1 - core, width)] = lower[...]
    gated[2 * TAPS :] = gated[: gated.shape[0] - 2 * TAPS]


def join(kept, received, after):
    length, width = kept.shape
    shape = (length + 16, 2 * width)
    return once(join_kernel, "join", [kept, *received], [(shape, BF16)], (), after)[0]


def input_grad_kernel(filters, conv_grad, following, grad_input, stack):
    rows = first_rows(filters[...], False)
    for i in range(conv_grad.shape[1] // LANES):
        columns = slice(i * LANES, (i + 1) * LANES)
        band = stack.at[i % 2]
        banded(rows[i * PER_TILE : (i + 1) * PER_TILE], band)
        window = two_windows(
            conv_grad[:TAPS, columns], conv_grad[TAPS:, columns], following[:, columns]
        )
        made = own_lanes(jnp.dot(band[...], window, preferred_element_type=F32))
        for block in range(2):
            grad_input[block * TAPS : (block + 1) * TAPS, columns] = made[
                :, block * LANES : (block + 1) * LANES
            ].astype(BF16)


def input_grad(filters, conv_grad, following, after):
    return once(
        input_grad_kernel,
        "input_grad",
        [filters, conv_grad, (following, whole((TAPS, conv_grad.shape[1])))],
        [(conv_grad.shape, BF16)],
        [pltpu.VMEM((2, PER_TILE * TAPS, 2 * TAPS), BF16)],
        after,
    )[0]


def filter_grad_kernel(previous, signal, conv_grad, grad_filter, stack):
    square = (2 * TAPS, 2 * TAPS)
    turn = iota(square, 0) == (2 * TAPS - iota(square, 1)) % (2 * TAPS)
    turn = turn.astype(F32).astype(BF16)
    group = lane_group((TAPS, 2 * LANES))
    for i in range(signal.shape[1] // LANES):
        columns = slice(i * LANES, (i + 1) * LANES)
        masked = stack.at[i % 2]
        inputs = two_windows(previous[:, columns], signal[:TAPS, columns], signal[TAPS:, columns])
        turned = jnp.dot(turn, inputs, preferred_element_type=F32).astype(BF16)
        both = jnp.concatenate([conv_grad[:TAPS, columns], conv_grad[TAPS:, columns]], 1)
        both = both.astype(F32)
        for g in range(PER_TILE):
            masked[g * TAPS : (g + 1) * TAPS, :] = jnp.where(group == g, both, 0.0).astype(BF16)
        products = lax.dot_general(
            masked[...], turned, (((1,), (1,)), ((), ())), preferred_element_type=F32
        )
        for g in range(PER_TILE):
            skewed = pltpu.roll(products[g * TAPS : (g + 1) * TAPS], 0, 1, stride=1, stride_axis=0)
            row = i * PER_TILE + g
            grad_filter[row : row + 1, :] = jnp.sum(skewed[:, TAPS:], axis=0, keepdims=True)


def filter_grad(previous, signal, conv_grad, after):
    return once(
        filter_grad_kernel,
        "filter_grad",
        [previous, signal, conv_grad],
        [((signal.shape[1] // GROUP, TAPS), F32)],
        [pltpu.VMEM((2, PER_TILE * TAPS, 2 * TAPS), BF16)],
        after,
        4,
    )[0]


def pack_into(mine, other, outs):
    x, y, _, _, core = spot()
    part = mine.shape[0]
    depth = mine.shape[1] // SIDE

    @pl.when(core == 0)
    def _():
        for ref, rows in ((mine, slice(0, part)), (other, slice(part, 2 * part))):
            for s, out in enumerate(outs):
                for d in range(SIDE):
                    start = pl.multiple_of(d * depth + (x + s) % SIDE * WIDE, WIDE)
                    out[rows, d * WIDE : (d + 1) * WIDE] = ref[:, pl.ds(start, WIDE)]

    @pl.when(core == 1)
    def _():
        lower = iota((part, LANES), 1) < HALF
        for ref, rows in ((other, slice(0, part)), (mine, slice(part, 2 * part))):
            for s, out in enumerate(outs):
                to = (y + s) % SIDE
                upper_half = jnp.broadcast_to(to % 2, (part, LANES)) == 1
                for pair in range(2 * SIDE):
                    runs = []
                    for i in range(2):
                        start = pl.multiple_of((2 * pair + i) * WIDE + to // 2 * LANES, LANES)
                        runs.append(ref[:, pl.ds(start, LANES)].astype(F32))
                    first = jnp.where(upper_half, pltpu.roll(runs[0], HALF, 1), runs[0])
                    second = jnp.where(upper_half, runs[1], pltpu.roll(runs[1], HALF, 1))
                    both = jnp.where(lower, first, second).astype(BF16)
                    out[rows, pair * LANES : (pair + 1) * LANES] = both


def pack_kernel(mine, other, *outs):
    pack_into(mine, other, outs)


def pack(mine, other):
    rows, width = mine.shape
    return once(
        pack_kernel, "pack", [mine, other], [((2 * rows, width // SIDE), BF16)] * SIDE
    )


def relay_kernel(mine, other, before, after, opposite, *outs):
    pack_into(mine, other, outs)
    part = opposite.shape[0]
    outs[1][part:] = before[...]
    outs[2][part:] = opposite[...]
    outs[3][part:] = after[...]


def relay(mine, other, got_next, got_last, opposite):
    rows, width = opposite.shape
    return once(
        relay_kernel,
        "relay",
        [
            mine,
            other,
            (got_next, whole((TAPS, width))),
            (got_last, whole((TAPS, width), (1, 0))),
            opposite,
        ],
        [((rows, width), BF16)] + [((rows + TAPS, width), BF16)] * (SIDE - 1),
    )


def project_kernel(early, early_other, late, late_other, weight, gating, response, conv_grad, grad_gate, rows):
    _, _, _, half, core = spot()
    part = early.shape[0]

    @pl.when(pl.program_id(0) == 0)
    def _():
        for ref, h, c in (
            (early, half, core),
            (early_other, half, 1 - core),
            (late, 1 - half, core),
            (late_other, 1 - half, 1 - core),
        ):
            rows[aligned(2 * h + c, part), :] = ref[...]

    made = jnp.dot(rows[...], weight[...], preferred_element_type=F32)
    conv_grad[...] = (made * gating[...].astype(F32)).astype(BF16)
    grad_gate[...] = (made * response[...]).astype(BF16)


def project(early, early_other, late, late_other, weight, gating, response, after):
    length, channels = gating.shape
    depth = weight.shape[0]

    def body(*refs):
        project_kernel(*refs[:7], *refs[7 + len(after) :])

    return pl.pallas_call(
        body,
        grid=(channels // WIDE,),
        in_specs=[full(early.shape)] * 4
        + [tile(depth, WIDE), tile(length, WIDE), tile(length, WIDE)]
        + [ANYWHERE] * len(after),
        out_specs=[tile(length, WIDE)] * 2,
        out_shape=[jax.ShapeDtypeStruct((length, channels), BF16)] * 2,
        scratch_shapes=[pltpu.VMEM((length, depth), BF16)],
        compiler_params=room(20),
        cost_estimate=lasting(6),
        name="project",
    )(early, early_other, late, late_other, weight, gating, response, *after)


def weight_kernel(*refs):
    early, late = refs[:SIDE], refs[SIDE : 2 * SIDE]
    gated, got_next, before, after, got_last = refs[2 * SIDE : 2 * SIDE + 5]
    outs, turned, tokens = refs[-2 - SIDE : -2], refs[-2], refs[-1]
    x, y, _, half, core = spot()
    me = jnp.where(core == 0, y, x)
    upper = jnp.broadcast_to(half, before.shape) == 0
    opposite = (before[...].astype(F32), after[...].astype(F32))
    for i, (parts, h) in enumerate(((early, half), (late, 1 - half))):
        rows = aligned(h, TAPS)
        halves = opposite if i == 0 else opposite[::-1]
        blocks = (
            gated[rows, :],
            got_next[rows, :],
            jnp.where(upper, *halves).astype(BF16),
            got_last[rows, :],
        )
        for s in range(SIDE):
            at = slice((i * SIDE + s) * TAPS, (i * SIDE + s + 1) * TAPS)
            tokens[at] = blocks[s]
            transposed = parts[s][...].T
            for d in range(SIDE):
                for q in range(SIDE):
                    to = (q - me + SIDE) % SIDE * WIDE + d * HALF
                    start = d * WIDE + q * HALF
                    turned[pl.ds(pl.multiple_of(to, HALF), HALF), at] = transposed[
                        start : start + HALF
                    ]
    for s, out in enumerate(outs):
        features = turned[s * WIDE : (s + 1) * WIDE]
        out[...] = jnp.dot(features, tokens[...], preferred_element_type=F32).astype(out.dtype)


def weight_parts(early, own_late, gated, got, late, after):
    width = gated.shape[1]
    rows = own_late.shape[0]
    length = 2 * rows

    def block(array, start, count=rows):
        return array, whole((count, width), (start // count, 0))

    shape = (width // SIDE, width)
    return once(
        weight_kernel,
        "weight_parts",
        [
            early[0],
            early[1],
            block(late[1], rows),
            early[2],
            own_late,
            *[block(part, 0) for part in late],
            block(gated, 0, length),
            block(got[0], 0, length),
            block(late[0], rows),
            block(late[2], rows),
            block(got[1], 0, length),
        ],
        [(shape, F32)] + [(shape, BF16)] * (SIDE - 1),
        [pltpu.VMEM((width, 2 * SIDE * rows), BF16), pltpu.VMEM((2 * SIDE * rows, width), BF16)],
        after,
        4,
    )


def first_sum_kernel(*refs):
    _, _, z, _, _ = spot()
    outs, kept = refs[SIDE:-1], refs[-1]
    run = kept.shape[0] // SIDE
    total = refs[0][...]
    for ref in refs[1:SIDE]:
        total = total + ref[...].astype(F32)
    for d in range(SIDE):
        kept[aligned((d - z + SIDE) % SIDE, run), :] = total[d * run : (d + 1) * run]
    for s, out in enumerate(outs):
        out[...] = kept[s * run : (s + 1) * run, :].astype(out.dtype)


def first_sum(parts, after):
    rows, width = parts[0].shape
    run = rows // SIDE
    return once(
        first_sum_kernel,
        "first_sum",
        parts,
        [((run, width), F32)] + [((run, width), BF16)] * (SIDE - 1),
        [pltpu.VMEM((rows, width), F32)],
        after,
        1,
    )


def last_sum(parts, scale, after):
    rows, width = parts[0].shape

    def kernel(*refs):
        kept, given, summed = refs[SIDE:]
        _, _, _, _, core = spot()
        total = refs[0][...]
        for ref in refs[1:SIDE]:
            total = total + ref[...].astype(F32)
        summed[...] = total * scale
        kept[...] = summed[:, aligned(core, width // 2)]
        given[...] = summed[:, aligned(1 - core, width // 2)]

    half = ((rows, width // 2), F32)
    return once(
        kernel, "last_sum", parts, [half, half], [pltpu.VMEM((rows, width), F32)], after
    )


def beside(kept, received):
    def kernel(first, second, out):
        _, _, _, _, core = spot()
        out[:, aligned(core, first.shape[1])] = first[...]
        out[:, aligned(1 - core, first.shape[1])] = second[...]

    rows, width = kept.shape
    return once(kernel, "beside", [kept, received], [((rows, 2 * width), F32)])[0]


def tied(x, *after):
    return lax.optimization_barrier((x, *after))[0]


def paired(x, gather, by, before=()):
    return x + in_plane(tied(x, *before), gather, lambda place: place ^ by)


def paired_z(x, by):
    return x + lax.ppermute(x, "dp", [(i, i ^ by) for i in range(SIDE)])


def local(conv_input, gate_value, out_grad, out_weight, filters):
    signal, gating, grads = conv_input[0], gate_value[0], out_grad[0]
    length, channels = signal.shape
    halo_sent = signal[length - TAPS :]
    signal, gating, filters, weight = (
        resident(x) for x in (signal, gating, filters, out_weight)
    )
    tokens_all = lax.axis_size("dp") * lax.axis_size("ctx") * length
    shifts = range(1, SIDE)

    late = moved(grads, "half")
    previous = shifted(halo_sent, 1)
    early_other = moved(grads, "core")
    grads = resident(grads)
    early = pack(grads, early_other)
    early_got = [stepped(early[1], True, 1), stepped(early[3], True, 3)]
    response, kept, *given = forward(filters, previous, signal, gating)
    gated = join(kept, [moved(part, "core") for part in given], early_got)
    got = [stepped(gated, True, 1), stepped(gated, True, 3)]
    late_other = moved(tied(late, gated), "core")
    own_late, *late_sent = relay(late, late_other, *got, early[2])
    conv_grad, grad_gate = project(
        grads, early_other, late, late_other, weight, gating, response, (own_late,)
    )
    late_got = [stepped(late_sent[s - 1], True, s) for s in shifts]
    filter_sum = filter_grad(previous, signal, conv_grad, ())
    parts = weight_parts([early[0], *early_got], own_late, gated, got, late_got, (filter_sum,))

    filter_sum = paired_z(paired_z(tied(filter_sum, parts[0]), 1), 2)
    following = shifted(tied(conv_grad[: TAPS + 64], filter_sum), -1)
    filter_sum = paired(filter_sum, True, 1)
    padded = jnp.pad(filter_sum, ((0, 3 * filter_sum.shape[0]), (0, 0)))
    padded = in_plane(padded, True, lambda place: place ^ 2)
    filter_sum = filter_sum + padded[: filter_sum.shape[0]]
    parts = [parts[0]] + [stepped(parts[s], False, s) for s in shifts]
    sums = first_sum(parts, ())
    grad_input = input_grad(filters, conv_grad, following, (sums[0],))
    filter_sum = paired(filter_sum, False, 1, (sums[0],))
    filter_sum = paired(filter_sum, False, 2, (resident(grad_input),))
    grad_filter = filter_sum * (1.0 / math.sqrt(tokens_all * GROUP))
    line = [[(i, (i + s) % SIDE) for i in range(SIDE)] for s in shifts]
    sums = [sums[0]] + [lax.ppermute(sums[s], "dp", line[s - 1]) for s in shifts]
    kept, given = last_sum(sums, 1.0 / math.sqrt(tokens_all), (resident(grad_input),))
    grad_weight = beside(kept, moved(given, "core"))
    return (grad_input[None], grad_gate[None], grad_weight, grad_filter)


def solution(mesh):
    placed = (
        P("dp", "ctx", "tp"),
        P("dp", "ctx", "tp"),
        P("dp", ("ctx", "tp"), None),
        P(None, "tp"),
        P("tp", None),
    )
    return jax.shard_map(
        local,
        mesh=mesh,
        in_specs=placed,
        out_specs=(
            P("dp", "ctx", "tp"),
            P("dp", "ctx", "tp"),
            P(("dp", "ctx"), "tp"),
            P("tp", None),
        ),
        check_vma=False,
    )
```

```python
import math

import jax
import jax.numpy as jnp
from jax import lax
from jax.experimental import pallas as pl
from jax.experimental.pallas import tpu as pltpu
from jax.sharding import PartitionSpec as P

F32 = jnp.float32
BF16 = jnp.bfloat16
SIDE = 4
TAPS = 128
GROUP = 16
LANES = 128
PER_TILE = LANES // GROUP
WIDE = 256


def room(mebibytes):
    return pltpu.CompilerParams(vmem_limit_bytes=mebibytes * 1024 * 1024)


def spot():
    ctx = lax.axis_index("ctx")
    tp = lax.axis_index("tp")
    return ctx // SIDE, ctx % SIDE, lax.axis_index("dp"), tp // 2, tp % 2


def moved(x, axis):
    step = 2 if axis == "half" else 1
    return lax.ppermute(x, "tp", [(i, i ^ step) for i in range(4)])


def in_plane(x, gather, target):
    pairs = []
    for i in range(SIDE * SIDE):
        for j in range(4):
            place_x, place_y = divmod(i, SIDE)
            if (j % 2 == 0) == gather:
                place_x = target(place_x)
            else:
                place_y = target(place_y)
            pairs.append((i * 4 + j, (place_x * SIDE + place_y) * 4 + j))
    return lax.ppermute(x, ("ctx", "tp"), pairs)


def stepped(x, gather, by):
    return in_plane(x, gather, lambda place: (place + by) % SIDE)


def shifted(x, by):
    devices = lax.axis_size("ctx")
    return lax.ppermute(x, "ctx", [(i, i + by) for i in range(devices) if 0 <= i + by < devices])


ANYWHERE = pl.BlockSpec(memory_space=pl.ANY)
HALF = LANES // 2


def resident(x):
    return pltpu.with_memory_space_constraint(x, pltpu.HBM)


def whole(shape, place=None):
    place = place or (0,) * len(shape)
    return pl.BlockSpec(tuple(shape), lambda i: place, pipeline_mode=pl.Buffered(1))


def full(shape):
    return pl.BlockSpec(tuple(shape), lambda i: (0,) * len(shape))


def tile(rows, width):
    return pl.BlockSpec((rows, width), lambda i: (0, i))


def iota(shape, dim):
    return lax.broadcasted_iota(jnp.int32, shape, dim)


def aligned(index, size):
    return pl.ds(pl.multiple_of(index * size, size), size)


def lasting(microseconds):
    return pl.CostEstimate(flops=int(microseconds * 1e9), bytes_accessed=0, transcendentals=0)


def once(kernel, name, ins, outs, scratch=(), after=(), lasts=0):
    def body(*refs):
        kernel(*refs[: len(ins)], *refs[len(ins) + len(after) :])

    specs = [i[1] if isinstance(i, tuple) else whole(i.shape) for i in ins]
    arrays = [i[0] if isinstance(i, tuple) else i for i in ins]
    return pl.pallas_call(
        body,
        grid=(1,),
        in_specs=specs + [ANYWHERE] * len(after),
        out_specs=[whole(shape) for shape, _ in outs],
        out_shape=[jax.ShapeDtypeStruct(shape, dtype) for shape, dtype in outs],
        scratch_shapes=list(scratch),
        compiler_params=room(20),
        cost_estimate=lasting(lasts),
        name=name,
    )(*arrays, *after)


def first_rows(filters, shifted_by):
    lane, tap = iota((TAPS, 2 * TAPS), 1), iota((TAPS, 2 * TAPS), 0)
    place = lane == (TAPS - tap if shifted_by else tap)
    return jnp.dot(filters, place.astype(F32).astype(BF16), preferred_element_type=F32)


def banded(rows, stack):
    for g in range(PER_TILE):
        first = jnp.broadcast_to(rows[g : g + 1], (TAPS, 2 * TAPS))
        skewed = pltpu.roll(first, 0, 1, stride=1, stride_axis=0)
        stack[g * TAPS : (g + 1) * TAPS, :] = skewed.astype(BF16)


def lane_group(shape):
    return iota(shape, len(shape) - 1) % LANES // GROUP


def own_lanes(stacked):
    group = lane_group((TAPS, 2 * LANES))
    chosen = jnp.zeros((TAPS, 2 * LANES), F32)
    for g in range(PER_TILE):
        chosen = jnp.where(group == g, stacked[g * TAPS : (g + 1) * TAPS], chosen)
    return chosen


def two_windows(first, second, third):
    upper = jnp.concatenate([first, second], 1)
    lower = jnp.concatenate([second, third], 1)
    return jnp.concatenate([upper, lower], 0)


def forward_kernel(filters, previous, signal, gating, response, kept, *refs):
    given, gated, stack = refs[:2], refs[2], refs[3]
    _, _, _, _, core = spot()
    rows = first_rows(filters[...], True)
    for i in range(signal.shape[1] // LANES):
        columns = slice(i * LANES, (i + 1) * LANES)
        band = stack.at[i % 2]
        banded(rows[i * PER_TILE : (i + 1) * PER_TILE], band)
        window = two_windows(previous[:, columns], signal[:TAPS, columns], signal[TAPS:, columns])
        made = own_lanes(jnp.dot(band[...], window, preferred_element_type=F32))
        for block in range(2):
            tokens = slice(block * TAPS, (block + 1) * TAPS)
            part = made[:, block * LANES : (block + 1) * LANES]
            response[tokens, columns] = part
            gated[tokens, columns] = (part * gating[tokens, columns].astype(F32)).astype(BF16)
    kept[...] = gated[:, aligned(core, kept.shape[1])]
    for i, out in enumerate(given):
        out[...] = gated[i * TAPS : (i + 1) * TAPS, aligned(1 - core, kept.shape[1])]


def forward(filters, previous, signal, gating):
    length, channels = signal.shape
    quarter = ((TAPS, channels // 2), BF16)
    return once(
        forward_kernel,
        "conv_forward",
        [filters, previous, signal, gating],
        [((length, channels), F32), ((length, channels // 2), BF16), quarter, quarter],
        [
            pltpu.VMEM((length, channels), BF16),
            pltpu.VMEM((2, PER_TILE * TAPS, 2 * TAPS), BF16),
        ],
    )


def join_kernel(kept, upper, lower, gated):
    _, _, _, _, core = spot()
    width = kept.shape[1]
    gated[: 2 * TAPS, aligned(core, width)] = kept[...]
    gated[:TAPS, aligned(1 - core, width)] = upper[...]
    gated[TAPS : 2 * TAPS, aligned(1 - core, width)] = lower[...]
    gated[2 * TAPS :] = gated[: gated.shape[0] - 2 * TAPS]


def join(kept, received, after):
    length, width = kept.shape
    shape = (length + 16, 2 * width)
    return once(join_kernel, "join", [kept, *received], [(shape, BF16)], (), after)[0]


def input_grad_kernel(filters, conv_grad, following, grad_input, stack):
    rows = first_rows(filters[...], False)
    for i in range(conv_grad.shape[1] // LANES):
        columns = slice(i * LANES, (i + 1) * LANES)
        band = stack.at[i % 2]
        banded(rows[i * PER_TILE : (i + 1) * PER_TILE], band)
        window = two_windows(
            conv_grad[:TAPS, columns], conv_grad[TAPS:, columns], following[:, columns]
        )
        made = own_lanes(jnp.dot(band[...], window, preferred_element_type=F32))
        for block in range(2):
            grad_input[block * TAPS : (block + 1) * TAPS, columns] = made[
                :, block * LANES : (block + 1) * LANES
            ].astype(BF16)


def input_grad(filters, conv_grad, following, after):
    return once(
        input_grad_kernel,
        "input_grad",
        [filters, conv_grad, following],
        [(conv_grad.shape, BF16)],
        [pltpu.VMEM((2, PER_TILE * TAPS, 2 * TAPS), BF16)],
        after,
    )[0]


def filter_grad_kernel(previous, signal, conv_grad, grad_filter, stack):
    square = (2 * TAPS, 2 * TAPS)
    turn = iota(square, 0) == (2 * TAPS - iota(square, 1)) % (2 * TAPS)
    turn = turn.astype(F32).astype(BF16)
    group = lane_group((TAPS, 2 * LANES))
    for i in range(signal.shape[1] // LANES):
        columns = slice(i * LANES, (i + 1) * LANES)
        masked = stack.at[i % 2]
        inputs = two_windows(previous[:, columns], signal[:TAPS, columns], signal[TAPS:, columns])
        turned = jnp.dot(turn, inputs, preferred_element_type=F32).astype(BF16)
        both = jnp.concatenate([conv_grad[:TAPS, columns], conv_grad[TAPS:, columns]], 1)
        both = both.astype(F32)
        for g in range(PER_TILE):
            masked[g * TAPS : (g + 1) * TAPS, :] = jnp.where(group == g, both, 0.0).astype(BF16)
        products = lax.dot_general(
            masked[...], turned, (((1,), (1,)), ((), ())), preferred_element_type=F32
        )
        for g in range(PER_TILE):
            skewed = pltpu.roll(products[g * TAPS : (g + 1) * TAPS], 0, 1, stride=1, stride_axis=0)
            row = i * PER_TILE + g
            grad_filter[row : row + 1, :] = jnp.sum(skewed[:, TAPS:], axis=0, keepdims=True)


def filter_grad(previous, signal, conv_grad, after):
    return once(
        filter_grad_kernel,
        "filter_grad",
        [previous, signal, conv_grad],
        [((signal.shape[1] // GROUP, TAPS), F32)],
        [pltpu.VMEM((2, PER_TILE * TAPS, 2 * TAPS), BF16)],
        after,
        4,
    )[0]


def pack_into(mine, other, outs):
    x, y, _, _, core = spot()
    part = mine.shape[0]
    depth = mine.shape[1] // SIDE

    @pl.when(core == 0)
    def _():
        for ref, rows in ((mine, slice(0, part)), (other, slice(part, 2 * part))):
            for s, out in enumerate(outs):
                for d in range(SIDE):
                    start = pl.multiple_of(d * depth + (x + s) % SIDE * WIDE, WIDE)
                    out[rows, d * WIDE : (d + 1) * WIDE] = ref[:, pl.ds(start, WIDE)]

    @pl.when(core == 1)
    def _():
        lower = iota((part, LANES), 1) < HALF
        for ref, rows in ((other, slice(0, part)), (mine, slice(part, 2 * part))):
            for s, out in enumerate(outs):
                to = (y + s) % SIDE
                upper_half = jnp.broadcast_to(to % 2, (part, LANES)) == 1
                for pair in range(2 * SIDE):
                    runs = []
                    for i in range(2):
                        start = pl.multiple_of((2 * pair + i) * WIDE + to // 2 * LANES, LANES)
                        runs.append(ref[:, pl.ds(start, LANES)].astype(F32))
                    first = jnp.where(upper_half, pltpu.roll(runs[0], HALF, 1), runs[0])
                    second = jnp.where(upper_half, runs[1], pltpu.roll(runs[1], HALF, 1))
                    both = jnp.where(lower, first, second).astype(BF16)
                    out[rows, pair * LANES : (pair + 1) * LANES] = both


def pack_kernel(mine, other, *outs):
    pack_into(mine, other, outs)


def pack(mine, other):
    rows, width = mine.shape
    return once(
        pack_kernel, "pack", [mine, other], [((2 * rows, width // SIDE), BF16)] * SIDE
    )


def relay_kernel(mine, other, before, after, opposite, *outs):
    pack_into(mine, other, outs)
    part = opposite.shape[0]
    outs[1][part:] = before[...]
    outs[2][part:] = opposite[...]
    outs[3][part:] = after[...]


def relay(mine, other, got_next, got_last, opposite):
    rows, width = opposite.shape
    return once(
        relay_kernel,
        "relay",
        [
            mine,
            other,
            (got_next, whole((TAPS, width))),
            (got_last, whole((TAPS, width), (1, 0))),
            opposite,
        ],
        [((rows, width), BF16)] + [((rows + TAPS, width), BF16)] * (SIDE - 1),
    )


def project_kernel(early, early_other, late, late_other, weight, gating, response, conv_grad, grad_gate, rows):
    _, _, _, half, core = spot()
    part = early.shape[0]

    @pl.when(pl.program_id(0) == 0)
    def _():
        for ref, h, c in (
            (early, half, core),
            (early_other, half, 1 - core),
            (late, 1 - half, core),
            (late_other, 1 - half, 1 - core),
        ):
            rows[aligned(2 * h + c, part), :] = ref[...]

    made = jnp.dot(rows[...], weight[...], preferred_element_type=F32)
    conv_grad[...] = (made * gating[...].astype(F32)).astype(BF16)
    grad_gate[...] = (made * response[...]).astype(BF16)


def project(early, early_other, late, late_other, weight, gating, response, after):
    length, channels = gating.shape
    depth = weight.shape[0]

    def body(*refs):
        project_kernel(*refs[:7], *refs[7 + len(after) :])

    return pl.pallas_call(
        body,
        grid=(channels // WIDE,),
        in_specs=[full(early.shape)] * 4
        + [tile(depth, WIDE), tile(length, WIDE), tile(length, WIDE)]
        + [ANYWHERE] * len(after),
        out_specs=[tile(length, WIDE)] * 2,
        out_shape=[jax.ShapeDtypeStruct((length, channels), BF16)] * 2,
        scratch_shapes=[pltpu.VMEM((length, depth), BF16)],
        compiler_params=room(20),
        cost_estimate=lasting(6),
        name="project",
    )(early, early_other, late, late_other, weight, gating, response, *after)


def weight_kernel(*refs):
    early, late = refs[:SIDE], refs[SIDE : 2 * SIDE]
    gated, got_next, before, after, got_last = refs[2 * SIDE : 2 * SIDE + 5]
    outs, turned, tokens = refs[-2 - SIDE : -2], refs[-2], refs[-1]
    x, y, _, half, core = spot()
    me = jnp.where(core == 0, y, x)
    upper = jnp.broadcast_to(half, before.shape) == 0
    opposite = (before[...].astype(F32), after[...].astype(F32))
    for i, (parts, h) in enumerate(((early, half), (late, 1 - half))):
        rows = aligned(h, TAPS)
        halves = opposite if i == 0 else opposite[::-1]
        blocks = (
            gated[rows, :],
            got_next[rows, :],
            jnp.where(upper, *halves).astype(BF16),
            got_last[rows, :],
        )
        for s in range(SIDE):
            at = slice((i * SIDE + s) * TAPS, (i * SIDE + s + 1) * TAPS)
            tokens[at] = blocks[s]
            transposed = parts[s][...].T
            for d in range(SIDE):
                for q in range(SIDE):
                    to = (q - me + SIDE) % SIDE * WIDE + d * HALF
                    start = d * WIDE + q * HALF
                    turned[pl.ds(pl.multiple_of(to, HALF), HALF), at] = transposed[
                        start : start + HALF
                    ]
    for s, out in enumerate(outs):
        features = turned[s * WIDE : (s + 1) * WIDE]
        out[...] = jnp.dot(features, tokens[...], preferred_element_type=F32).astype(out.dtype)


def weight_parts(early, own_late, gated, got, late, after):
    width = gated.shape[1]
    rows = own_late.shape[0]
    length = 2 * rows

    def block(array, start, count=rows):
        return array, whole((count, width), (start // count, 0))

    shape = (width // SIDE, width)
    return once(
        weight_kernel,
        "weight_parts",
        [
            early[0],
            early[1],
            block(late[1], rows),
            early[2],
            own_late,
            *[block(part, 0) for part in late],
            block(gated, 0, length),
            block(got[0], 0, length),
            block(late[0], rows),
            block(late[2], rows),
            block(got[1], 0, length),
        ],
        [(shape, F32)] + [(shape, BF16)] * (SIDE - 1),
        [pltpu.VMEM((width, 2 * SIDE * rows), BF16), pltpu.VMEM((2 * SIDE * rows, width), BF16)],
        after,
        4,
    )


def first_sum_kernel(*refs):
    _, _, z, _, _ = spot()
    outs, kept = refs[SIDE:-1], refs[-1]
    run = kept.shape[0] // SIDE
    total = refs[0][...]
    for ref in refs[1:SIDE]:
        total = total + ref[...].astype(F32)
    for d in range(SIDE):
        kept[aligned((d - z + SIDE) % SIDE, run), :] = total[d * run : (d + 1) * run]
    for s, out in enumerate(outs):
        out[...] = kept[s * run : (s + 1) * run, :].astype(out.dtype)


def first_sum(parts, after):
    rows, width = parts[0].shape
    run = rows // SIDE
    return once(
        first_sum_kernel,
        "first_sum",
        parts,
        [((run, width), F32)] + [((run, width), BF16)] * (SIDE - 1),
        [pltpu.VMEM((rows, width), F32)],
        after,
        1,
    )


def last_sum(parts, scale, after):
    rows, width = parts[0].shape

    def kernel(*refs):
        kept, given, summed = refs[SIDE:]
        _, _, _, _, core = spot()
        total = refs[0][...]
        for ref in refs[1:SIDE]:
            total = total + ref[...].astype(F32)
        summed[...] = total * scale
        kept[...] = summed[:, aligned(core, width // 2)]
        given[...] = summed[:, aligned(1 - core, width // 2)]

    half = ((rows, width // 2), F32)
    return once(
        kernel, "last_sum", parts, [half, half], [pltpu.VMEM((rows, width), F32)], after
    )


def beside(kept, received):
    def kernel(first, second, out):
        _, _, _, _, core = spot()
        out[:, aligned(core, first.shape[1])] = first[...]
        out[:, aligned(1 - core, first.shape[1])] = second[...]

    rows, width = kept.shape
    return once(kernel, "beside", [kept, received], [((rows, 2 * width), F32)])[0]


def tied(x, *after):
    return lax.optimization_barrier((x, *after))[0]


def paired(x, gather, by, before=()):
    return x + in_plane(tied(x, *before), gather, lambda place: place ^ by)


def paired_z(x, by):
    return x + lax.ppermute(x, "dp", [(i, i ^ by) for i in range(SIDE)])


def local(conv_input, gate_value, out_grad, out_weight, filters):
    signal, gating, grads = conv_input[0], gate_value[0], out_grad[0]
    length, channels = signal.shape
    halo_sent = signal[length - TAPS :]
    signal, gating, filters, weight = (
        resident(x) for x in (signal, gating, filters, out_weight)
    )
    tokens_all = lax.axis_size("dp") * lax.axis_size("ctx") * length
    shifts = range(1, SIDE)

    late = moved(grads, "half")
    previous = shifted(halo_sent, 1)
    early_other = moved(grads, "core")
    grads = resident(grads)
    early = pack(grads, early_other)
    early_got = [stepped(early[1], True, 1), stepped(early[3], True, 3)]
    response, kept, *given = forward(filters, previous, signal, gating)
    gated = join(kept, [moved(part, "core") for part in given], early_got)
    got = [stepped(gated, True, 1), stepped(gated, True, 3)]
    late_other = moved(tied(late, gated), "core")
    own_late, *late_sent = relay(late, late_other, *got, early[2])
    conv_grad, grad_gate = project(
        grads, early_other, late, late_other, weight, gating, response, (own_late,)
    )
    late_got = [stepped(late_sent[s - 1], True, s) for s in shifts]
    filter_sum = filter_grad(previous, signal, conv_grad, ())
    parts = weight_parts([early[0], *early_got], own_late, gated, got, late_got, (filter_sum,))

    filter_sum = paired_z(paired_z(tied(filter_sum, parts[0]), 1), 2)
    following = shifted(tied(conv_grad[:TAPS], filter_sum), -1)
    filter_sum = paired(filter_sum, True, 1)
    padded = jnp.pad(filter_sum, ((0, 2 * filter_sum.shape[0]), (0, 0)))
    padded = in_plane(padded, True, lambda place: place ^ 2)
    filter_sum = filter_sum + padded[: filter_sum.shape[0]]
    parts = [parts[0]] + [stepped(parts[s], False, s) for s in shifts]
    sums = first_sum(parts, ())
    grad_input = input_grad(filters, conv_grad, following, (sums[0],))
    filter_sum = paired(filter_sum, False, 1, (sums[0],))
    filter_sum = paired(filter_sum, False, 2, (resident(grad_input),))
    grad_filter = filter_sum * (1.0 / math.sqrt(tokens_all * GROUP))
    line = [[(i, (i + s) % SIDE) for i in range(SIDE)] for s in shifts]
    sums = [sums[0]] + [lax.ppermute(sums[s], "dp", line[s - 1]) for s in shifts]
    kept, given = last_sum(sums, 1.0 / math.sqrt(tokens_all), (resident(grad_input),))
    grad_weight = beside(kept, moved(given, "core"))
    return (grad_input[None], grad_gate[None], grad_weight, grad_filter)


def solution(mesh):
    placed = (
        P("dp", "ctx", "tp"),
        P("dp", "ctx", "tp"),
        P("dp", ("ctx", "tp"), None),
        P(None, "tp"),
        P("tp", None),
    )
    return jax.shard_map(
        local,
        mesh=mesh,
        in_specs=placed,
        out_specs=(
            P("dp", "ctx", "tp"),
            P("dp", "ctx", "tp"),
            P(("dp", "ctx"), "tp"),
            P("tp", None),
        ),
        check_vma=False,
    )
```
